256 devices in a mesh: tx: 16 (over y_lo, z), ty: 16 (over y_hi, x, core).
Axes of the slice: x: 4, y: 4 (y_hi: 2, y_lo: 2; y = y_hi * 2 + y_lo), z: 8, core: 2. Of those that a mesh axis runs over, the one named last changes fastest.
Arguments:
- concentration: float32 [128, 256, 256], P('tx', 'ty'), may hold values from -6 to 6
- source: float32 [128, 256, 256], P('tx', 'ty'), may hold values from -4 to 4
- material: int32 [128, 256, 256], P('tx', 'ty'), may hold values from 0 to 7
Outputs:
- updated: float32 [128, 256, 256], P('tx', 'ty')
The draws below stay inside these ranges and needn't reach their ends.
All inputs are finite; a program needn't handle non-finite values.
Results may differ from the reference program's by a relative error of at most 0.00017.
Values sent between devices are 32-bit elements; how exact they have to be, the bound alone decides.
A program may use at most 128 MiB of HBM per device.

```python
import jax
import jax.numpy as jnp

NX = 128
NY = 256
NZ = 256


def draw_source(key, part):
    return jnp.clip(jax.random.normal(key, (NX, NY, NZ), jnp.float32), -4.0, 4.0)


def with_ends(values, stream_key, smallest, top_value):
    place = [jax.random.randint(jax.random.fold_in(stream_key, axis), (), 0, length) for axis, length in enumerate(values.shape)]
    widest = values.shape.index(max(values.shape))
    next_to = place[:widest] + [(place[widest] + 1) % values.shape[widest]] + place[widest + 1:]
    return values.at[tuple(place)].set(smallest).at[tuple(next_to)].set(top_value)


def block_scale(key, shape, pieces, least, top_value):
    def one(position, parts):
        heights = jax.random.uniform(jax.random.fold_in(jax.random.fold_in(key, 6), position), (parts,), jnp.float32, least / len(pieces), top_value / len(pieces))
        return jnp.repeat(jnp.exp(heights), shape[position] // parts).reshape((-1,) + (1,) * (len(shape) - position - 1))

    factor_of = one(*pieces[0])
    for cut in pieces[1:]:
        factor_of = factor_of * one(*cut)
    return factor_of


def scatter_about(own_key, shape, width, reach, cuts=(), kind=jnp.bfloat16):
    values = jax.random.normal(own_key, shape, jnp.float32) * width
    if len(cuts) > 0:
        values = block_scale(own_key, shape, cuts, -0.22, 0.18) * values
    return jnp.clip(values, min=-reach, max=reach).astype(kind)


def setup_inputs(seed: int = 0) -> dict:
    seeds = jax.random.split(jax.random.key(seed), 4)
    return {
        "concentration": scatter_about(seeds[0], (NX, NY, NZ), 1.0, 6.0, ((0, 16), (1, 16)), jnp.float32),
        "source": draw_source(jax.random.fold_in(seeds[3], 71), 0),
        "material": with_ends(jax.random.randint(seeds[2], (NX, NY, NZ), 0, 8), jax.random.fold_in(seeds[2], 1), 0, 7).astype(jnp.int32),
    }


mass_rate = 0.001
relax_weight = 0.8
diffusivities = (0.15, 0.3, 0.5, 0.8, 1.2, 2.0, 3.2, 5.0)

def lookup(material):
    result = jnp.zeros(material.shape, jnp.float32)
    for slot_id, coeff_value in enumerate(diffusivities):
        result = jnp.where(material == slot_id, jnp.float32(coeff_value), result)
    return result

def couplings(kappa_pad, scales):
    scale_x, scale_y, scale_z = scales
    centre = kappa_pad[1:-1, 1:-1]
    return [0.5 * scale_x * (centre + kappa_pad[2:, 1:-1]), 0.5 * scale_x * (centre + kappa_pad[:-2, 1:-1]), 0.5 * scale_y * (centre + kappa_pad[1:-1, 2:]), 0.5 * scale_y * (centre + kappa_pad[1:-1, :-2]), 0.5 * scale_z * (centre + jnp.roll(centre, -1, axis=2)), 0.5 * scale_z * (centre + jnp.roll(centre, 1, axis=2))]

def diagonal_of(coupled):
    summed = mass_rate + coupled[0]
    for coupled_term in coupled[1:]:
        summed = summed + coupled_term
    return summed

def operate(field_pad, coupled, diagonal):
    centre = field_pad[1:-1, 1:-1]
    beside_all = (field_pad[2:, 1:-1], field_pad[:-2, 1:-1], field_pad[1:-1, 2:], field_pad[1:-1, :-2], jnp.roll(centre, -1, axis=2), jnp.roll(centre, 1, axis=2))
    off_sum = coupled[0] * beside_all[0]
    for number in range(1, 6):
        off_sum = off_sum + coupled[number] * beside_all[number]
    return diagonal * centre - off_sum

def sweep(field_pad, forcing, coupled, diagonal):
    centre = field_pad[1:-1, 1:-1]
    return centre + relax_weight * (forcing - operate(field_pad, coupled, diagonal)) / diagonal

def restrict(cells, ratios=(2, 2, 2)):
    size_x, size_y, size_z = cells.shape
    ratio_x, ratio_y, ratio_z = ratios
    grouped = cells.reshape(size_x // ratio_x, ratio_x, size_y // ratio_y, ratio_y, size_z // ratio_z, ratio_z)
    return jnp.sum(grouped, axis=(1, 3, 5)) * (1.0 / (ratio_x * ratio_y * ratio_z))

def prolong(coarse, ratios=(2, 2, 2)):
    return jnp.repeat(jnp.repeat(jnp.repeat(coarse, ratios[0], 0), ratios[1], 1), ratios[2], 2)

def wrap_pad(cells):
    return jnp.pad(cells, ((1, 1), (1, 1), (0, 0)), mode='wrap')

def scales_of(spacing):
    return tuple((1.0 / (step_size * step_size) for step_size in spacing))

def next_ratios(shape):
    return tuple((2 if extent % 2 == 0 else 1 for extent in shape))

def exact_solve(forcing, coupled, diagonal):
    shape = forcing.shape
    cells = forcing.size
    basis = jnp.eye(cells, dtype=forcing.dtype).reshape((cells,) + shape)
    matrix = jax.vmap(lambda unit: operate(wrap_pad(unit), coupled, diagonal).reshape(cells))(basis)
    return jnp.linalg.solve(matrix, forcing.reshape(cells)).reshape(shape)

def coarse_solve(forcing, kappa, spacing):
    coupled = couplings(wrap_pad(kappa), scales_of(spacing))
    diagonal = diagonal_of(coupled)
    ratios = next_ratios(forcing.shape)
    if forcing.size <= 64 or ratios == (1, 1, 1):
        return exact_solve(forcing, coupled, diagonal)
    current = relax_weight * forcing / diagonal
    current = sweep(wrap_pad(current), forcing, coupled, diagonal)
    residual = forcing - operate(wrap_pad(current), coupled, diagonal)
    wider = tuple((step_size * ratio for step_size, ratio in zip(spacing, ratios)))
    correction = coarse_solve(restrict(residual, ratios), restrict(kappa, ratios), wider)
    current = current + prolong(correction, ratios)
    for repeat in range(2):
        current = sweep(wrap_pad(current), forcing, coupled, diagonal)
    return current

def reference(concentration, source, material):
    kappas = [lookup(material)]
    for depth_level in range(3):
        kappas.append(restrict(kappas[-1]))
    operators = []
    for depth_level in range(3):
        coupled = couplings(wrap_pad(kappas[depth_level]), (0.25 ** depth_level,) * 3)
        operators.append((coupled, diagonal_of(coupled)))

    def vcycle(depth_level, initial, forcing):
        if depth_level == 3:
            return coarse_solve(forcing, kappas[3], (8.0, 8.0, 8.0))
        coupled, diagonal = operators[depth_level]
        if initial is None:
            current = relax_weight * forcing / diagonal
        else:
            current = sweep(wrap_pad(initial), forcing, coupled, diagonal)
        current = sweep(wrap_pad(current), forcing, coupled, diagonal)
        residual = forcing - operate(wrap_pad(current), coupled, diagonal)
        correction = vcycle(depth_level + 1, None, restrict(residual))
        current = current + prolong(correction)
        for repeat in range(2):
            current = sweep(wrap_pad(current), forcing, coupled, diagonal)
        return current
    forcing_top = mass_rate * concentration + source
    return vcycle(0, concentration, forcing_top)
```

```python
import jax
import jax.numpy as jnp
from jax import lax
from jax.experimental import pallas as pl
from jax.experimental.pallas import tpu as pltpu
from jax.sharding import PartitionSpec as P

MESH = pl.DeviceIdType.MESH
F32 = jnp.float32
BF16 = jnp.bfloat16
RATE = 0.001
RELAX = 0.8
TABLE = (0.15, 0.3, 0.5, 0.8, 1.2, 2.0, 3.2, 5.0)
N = 16


def iota(shape, axis):
    return lax.broadcasted_iota(jnp.int32, shape, axis)


def roll(v, shift, axis):
    return pltpu.roll(v, shift % v.shape[axis], axis)


def dot01(v, m):
    hi = v.astype(BF16)
    rest = v - hi.astype(F32)
    mid = rest.astype(BF16)
    low = (rest - mid.astype(F32)).astype(BF16)
    a, b, c = [jnp.dot(piece, m, preferred_element_type=F32) for piece in (hi, mid, low)]
    return a + (b + c)


def each(low, high, unroll, body):
    count = high - low
    whole = count // unroll
    if whole > 1:

        def step(i, carry):
            for k in range(unroll):
                body(low + i * unroll + k)
            return carry

        lax.fori_loop(0, whole, step, 0)
        rest = low + whole * unroll
    else:
        rest = low
    for x in range(rest, high):
        body(x)


def make_ops(kappa, ops, scale, layers, unroll):
    cx, cy, cz, w = ops
    half = 0.5 * scale

    def couple(x):
        k = kappa[x]
        cx[x] = half * (k + kappa[x + 1])
        cy[x] = half * (k + roll(k, -1, 0))
        cz[x] = half * (k + roll(k, -1, 1))

    def weigh(x):
        a, b = cy[x], cz[x]
        diag = (RATE + cx[x] + cx[x - 1]) + (a + roll(a, 1, 0)) + (b + roll(b, 1, 1))
        w[x] = RELAX / diag

    each(0, layers - 1, unroll, couple)
    each(1, layers - 1, unroll, weigh)


def residual(v, below, above, g, cx, cxm, cy, cz):
    fy = cy * (roll(v, -1, 0) - v)
    fz = cz * (roll(v, -1, 1) - v)
    r = (g - RATE * v) + (cx * (above - v) - cxm * (v - below))
    return r + (fy - roll(fy, 1, 0)) + (fz - roll(fz, 1, 1))


def res_at(v, g, ops, x):
    cx, cy, cz, _ = ops
    return residual(v[x], v[x - 1], v[x + 1], g[x], cx[x], cx[x - 1], cy[x], cz[x])


def sweep(v, out, g, ops, low, high, unroll):
    def body(x):
        out[x] = v[x] + ops[3][x] * res_at(v, g, ops, x)

    each(low, high, unroll, body)


def x_hi_next(v):
    lane = iota(v.shape, 1)
    return jnp.where(lane % 4 == 3, roll(v, 3, 1), roll(v, -1, 1))


def x_hi_prev(v):
    lane = iota(v.shape, 1)
    return jnp.where(lane % 4 == 0, roll(v, -3, 1), roll(v, 1, 1))


def low_couple(kappa, s, scale):
    half = 0.5 * scale
    nxt = kappa[1:] + [x_hi_next(kappa[0])]
    cx = [half * (k + n) for k, n in zip(kappa, nxt)]
    cy = [half * (k + roll(k, -s, 0)) for k in kappa]
    cz = [half * (k + roll(k, -4 * s, 1)) for k in kappa]
    cxm = [x_hi_prev(cx[-1])] + cx[:-1]
    w = []
    for a, am, b, c in zip(cx, cxm, cy, cz):
        diag = (RATE + a + am) + (b + roll(b, s, 0)) + (c + roll(c, 4 * s, 1))
        w.append(RELAX / diag)
    return cx, cy, cz, w


def low_res(v, g, ops, s):
    cx, cy, cz, _ = ops
    nxt = v[1:] + [x_hi_next(v[0])]
    fx = [c * (n - u) for c, n, u in zip(cx, nxt, v)]
    fxm = [x_hi_prev(fx[-1])] + fx[:-1]
    out = []
    for u, f, a, am, b, c in zip(v, g, fx, fxm, cy, cz):
        fy = b * (roll(u, -s, 0) - u)
        fz = c * (roll(u, -4 * s, 1) - u)
        r = (f - RATE * u) + (a - am)
        out.append(r + (fy - roll(fy, s, 0)) + (fz - roll(fz, 4 * s, 1)))
    return out


def low_sweep(v, g, ops, s):
    return [u + w * r for u, w, r in zip(v, ops[3], low_res(v, g, ops, s))]


def low_restrict(v, s):
    if len(v) > 1:
        v = [v[2 * k] + v[2 * k + 1] for k in range(len(v) // 2)]
    else:
        u = v[0]
        lane = iota(u.shape, 1)
        v = [u + jnp.where(lane % 2 == 0, roll(u, -1, 1), roll(u, 1, 1))]
    out = []
    for u in v:
        row, lane = iota(u.shape, 0), iota(u.shape, 1)
        u = u + jnp.where((row // s) % 2 == 0, roll(u, -s, 0), roll(u, s, 0))
        u = u + jnp.where((lane // (4 * s)) % 2 == 0, roll(u, -4 * s, 1), roll(u, 4 * s, 1))
        out.append(u * 0.125)
    return out


def pack_six(v):
    lane = iota((8, 128), 1)
    y = (lane % 32) // 4
    out = v[24:32]
    for k in (2, 1, 0):
        out = jnp.where(y == k, v[8 * k : 8 * k + 8], out)
    return out


def kernel(conc, source, material, out, *scratch):
    names = [name for name, _ in SCRATCH]
    s = dict(zip(names, scratch))
    ops0, ops1, ops2 = [[s[f"{name}{level}"] for name in ("cx", "cy", "cz", "w")] for level in (0, 1, 2)]
    me_x, me_y = lax.axis_index("tx"), lax.axis_index("ty")

    def device(dx, dy):
        return (lax.rem(me_x + (dx + N), N), lax.rem(me_y + (dy + N), N))

    counter = {}

    def copy(group, src, dst, dx, dy):
        k = counter.get(group, 0)
        counter[group] = k + 1
        c = pltpu.make_async_remote_copy(
            src, dst, s[group + "_s"].at[k], s[group + "_r"].at[k], device_id=device(dx, dy), device_id_type=MESH
        )
        c.start()
        return c

    sent = []

    def arrive(copies):
        for c in copies:
            c.wait_recv()
        sent.extend(copies)

    tile0 = (slice(3, 11), slice(0, 16))
    loads = [
        pltpu.make_async_copy(material, s["mat"], s["load"].at[0]),
        pltpu.make_async_copy(conc, s["va"].at[3:11, 0:16], s["load"].at[1]),
        pltpu.make_async_copy(source, s["src"].at[3:11, 0:16], s["load"].at[2]),
    ]
    for c in loads:
        c.start()
    barrier = pltpu.get_barrier_semaphore()
    peers = [(d, 0) for d in range(1, N)] + [(0, d) for d in range(1, N)]
    peers += [(a, b) for a in (-2, -1, 1, 2) for b in (-1, 1)]
    for p in peers:
        pl.semaphore_signal(barrier, inc=1, device_id=device(*p), device_id_type=MESH)

    def matrix(name, rule):
        shape = s[name].shape
        s[name][...] = jnp.where(rule(iota(shape, 0), iota(shape, 1)), 1.0, 0.0).astype(BF16)

    matrix("r01", lambda i, j: i // 2 == j)
    matrix("r12", lambda i, j: i // 2 == j % 64)
    matrix("r23", lambda i, j: i // 2 == j // 4)
    matrix("p32", lambda i, j: i // 4 == (j % 64) // 2)
    matrix("p21", lambda i, j: i == j // 2)
    matrix("p10", lambda i, j: i == j // 2)
    matrix("sel", lambda i, j: ((i % 32) // 4 < 4) & (i % 2 == 0) & (j == ((i % 32) // 4) * 8 + (i // 32) * 2 + (i % 4) // 2))
    matrix("spr", lambda i, j: i == (j // 128) * 8 + ((j % 128) // 32) * 2 + (j % 4) // 2)

    loads[0].wait()
    k0 = s["k0"]

    def lookup(x):
        m = s["mat"][x]
        result = jnp.zeros(m.shape, F32)
        for slot, value in enumerate(TABLE):
            result = jnp.where(m == slot, F32(value), result)
        k0[x + 3, 0:16] = result

    each(0, 8, 2, lookup)
    loads[1].wait()
    loads[2].wait()
    pl.semaphore_wait(barrier, len(peers))

    def halo0(group, ref, dest, w, c):
        edge, below = s[group + "_e"], s[group + "_b"]
        for x in range(8):
            edge[x] = roll(ref[x + 3, 8:16], w, 0)
        copies = []
        for dx, dy in ((1, 0), (-1, 0), (0, 1), (0, -1), (1, 1), (1, -1), (-1, 1), (-1, -1)):
            n = c if dy else w
            x0, x1 = {0: (3, 11), -1: (3, 3 + n), 1: (11 - n, 11)}[dx]
            y0, y1 = x0 - 8 * dx, x1 - 8 * dx
            if dy == 0:
                copies.append(copy(group, ref.at[x0:x1, 0:16], dest.at[y0:y1, 0:16], dx, dy))
            elif dy < 0:
                copies.append(copy(group, ref.at[x0:x1, 0:w], dest.at[y0:y1, 16 : 16 + w], dx, dy))
            else:
                copies.append(copy(group, edge.at[x0 - 3 : x1 - 3, 0:w], below.at[y0:y1, 0:w], dx, dy))
        return copies

    def merge0(group, dest, w):
        below = s[group + "_b"]
        row = iota((8, 256), 0)
        for x in range(14):
            dest[x, 16:24] = jnp.where(row < 4, dest[x, 16:24], roll(below[x], -w, 0))

    in_k0 = halo0("hk", k0, k0, 3, 2)
    in_va = halo0("hv", s["va"], s["va"], 3, 2)
    in_src = halo0("hs", s["src"], s["src"], 2, 1)

    t0, t1, t2 = s["t0"], s["t1"], s["t2"]

    def put0(c, pair):
        t0[c, 0] = pair[:16, :128]
        t0[c, 1] = pair[:16, 128:]

    def take0():
        rows = []
        for c in range(4):
            halves = [t0[c, h, pl.ds(0, 8, stride=2), :] + t0[c, h, pl.ds(1, 8, stride=2), :] for h in range(2)]
            rows.append(jnp.concatenate(halves, axis=1))
        return dot01(jnp.concatenate(rows, axis=0), s["r01"][...]) * 0.125

    def row_pairs(ref, k, start, count):
        return ref[k, pl.ds(start, count, stride=2), :] + ref[k, pl.ds(start + 1, count, stride=2), :]

    k1, k2, x2k, x2f = s["k1"], s["k2"], s["x2k"], s["x2f"]
    for c in range(4):
        put0(c, k0[3 + 2 * c, 0:16] + k0[4 + 2 * c, 0:16])
    tile = take0()
    for c in range(4):
        k1[7 + c, 0:8] = tile[8 * c : 8 * c + 8]

    def halo1(group, ref, w):
        copies = []
        for dx, dy in ((1, 0), (-1, 0), (0, 1), (0, -1), (2, 0), (-2, 0), (1, 1), (1, -1), (-1, 1), (-1, -1), (2, 1), (2, -1), (-2, 1), (-2, -1)):
            nx = {0: 4, 1: 4, 2: w - 4 if dy == 0 else w - 5}[abs(dx)]
            ny = 8 if dy == 0 else {0: w, 1: w - 1, 2: w - 5}[abs(dx)]
            xs = slice(11 - nx, 11) if dx > 0 else slice(7, 7 + nx)
            xd = slice(xs.start - 4 * dx, xs.stop - 4 * dx)
            ys = slice(0, 8) if dy > 0 else slice(0, ny)
            yd = slice(16, 24) if dy > 0 else slice(-8 * dy, ny - 8 * dy)
            copies.append(copy(group, ref.at[xs, ys], ref.at[xd, yd], dx, dy))
        return copies

    in_k1 = halo1("h1k", k1, 7)

    def to_level2(get):
        parts = []
        for c in range(len(get) // 2):
            pair = get[2 * c] + get[2 * c + 1]
            if len(pair) == 8:
                t1[c, 4:12] = pair
            else:
                t1[c] = roll(pair, 4, 0)
        for c in range(len(get) // 2):
            parts.append(row_pairs(t1, c, 0, 8))
        return dot01(jnp.concatenate(parts, axis=0), s["r12"][...]) * 0.125

    def to_level3(pair, row0):
        t2[0] = dot01(pair, s["r23"][...]) * 0.125
        return row_pairs(t2, 0, row0, 2)

    low = to_level2([tile[8 * c : 8 * c + 8] for c in range(4)])
    for c in range(2):
        x2k[6 + c, 2] = low[8 * c + 2 : 8 * c + 6]
    base = to_level3(low[0:8] + low[8:16], 2)

    def ring_x(group, ref, tile_ref, value):
        tile_ref[...] = value
        ref[me_x] = value
        return [copy(group, tile_ref, ref.at[me_x], d, 0) for d in range(1, N)]

    def window_x(group, ref):
        return [
            copy(group, ref.at[6:8, 2], ref.at[6 - 2 * d : 8 - 2 * d, 2], d, 0) for d in (1, -1, 2, -2, 3, -3)
        ]

    def slab(ref):
        lane = iota((2, 128), 1)
        out_parts = []
        for k in range(4):
            v = ref[12 + k]
            for h in (2, 1, 0):
                v = jnp.where(lane % 4 == h, ref[4 * h + k], v)
            out_parts.append(v)
        return out_parts

    def ring_y(group, ref, slab_ref, parts):
        for k in range(4):
            slab_ref[k] = parts[k]
            ref[k, me_y] = parts[k]
        return [copy(group, slab_ref, ref.at[:, me_y], 0, d) for d in range(1, N)]

    def window_y(group, ref):
        return [copy(group, ref.at[:, 2], ref.at[:, 2 - d], 0, d) for d in (1, -1, 2, -2)]

    def window(ref, dest):
        for x in range(14):
            dest[x] = ref[x].reshape(20, 128)[2:18]

    in_ka = ring_x("ka", s["ka"], s["kt"], base)
    in_k2a = window_x("k2a", x2k)

    arrive(in_k0)
    merge0("hk", k0, 3)
    make_ops(k0, ops0, 1.0, 14, 3)
    arrive(in_va)
    arrive(in_src)
    merge0("hv", s["va"], 3)
    merge0("hs", s["src"], 2)
    va, vb, vc, vd, ve, src, g0 = [s[name] for name in ("va", "vb", "vc", "vd", "ve", "src", "g0")]

    def force(x):
        g0[x] = RATE * va[x] + src[x]

    each(1, 13, 3, force)
    sweep(va, vb, g0, ops0, 1, 13, 3)
    sweep(vb, vc, g0, ops0, 2, 12, 2)

    def down0(c):
        put0(c, res_at(vc, g0, ops0, 2 * c + 3) + res_at(vc, g0, ops0, 2 * c + 4))

    each(0, 4, 1, down0)
    tile = take0()
    f1 = s["f1"]
    for c in range(4):
        f1[7 + c, 0:8] = tile[8 * c : 8 * c + 8]
    in_f1 = halo1("h1f", f1, 6)

    arrive(in_ka)
    in_kb = ring_y("kb", s["kb"], s["ks"], slab(s["ka"]))
    arrive(in_k2a)
    in_k2b = window_y("k2b", x2k)
    stay = pltpu.make_async_copy(vc.at[tile0], vd.at[tile0], s["load"].at[0])
    stay.start()
    in_vd = halo0("hd", vc, vd, 2, 1)

    arrive(in_k1)
    make_ops(k1, ops1, 0.25, 18, 4)
    arrive(in_f1)

    v1a, v1b = s["v1a"], s["v1b"]

    def start1(x):
        v1a[x] = ops1[3][x] * f1[x]

    each(1, 17, 4, start1)
    sweep(v1a, v1b, f1, ops1, 2, 16, 7)
    low = to_level2([res_at(v1b, f1, ops1, x) for x in range(3, 15)])
    f2l = s["f2l"]
    f2 = s["f2"]
    for c in range(6):
        f2l[c] = low[8 * c : 8 * c + 8]
    for c in range(2):
        x2f[6 + c, 2] = low[8 * c + 18 : 8 * c + 22]

    arrive(in_k2b)
    window(x2k, k2)
    make_ops(k2, ops2, 0.0625, 14, 13)
    v2a, v2b = s["v2a"], s["v2b"]
    near = [[ref[x, 4:12] for x in range(4, 10)] for ref in ops2]
    fl = [f2l[c] for c in range(6)]
    vl = [near[3][c] * fl[c] for c in range(6)]

    def res_near(v, c):
        return residual(v[c], v[c - 1], v[c + 1], fl[c], near[0][c], near[0][c - 1], near[1][c], near[2][c])

    ul = [None] + [vl[c] + near[3][c] * res_near(vl, c) for c in range(1, 5)]
    base = to_level3(res_near(ul + [None], 2) + res_near(ul + [None], 3), 2)
    in_fa = ring_x("fa", s["fa"], s["ft"], base)
    in_f2a = window_x("f2a", x2f)

    arrive(in_kb)
    kap3 = [s["kb"][k].reshape(32, 128) for k in range(4)]
    kap4 = low_restrict(kap3, 1)
    kap5 = low_restrict(kap4, 2)
    kap6 = low_restrict(kap5, 4)[0]
    for level, kap, spread in ((3, kap3, 1), (4, kap4, 2), (5, kap5, 4)):
        made = low_couple(kap, spread, 1.0 / 4.0**level)
        for number in range(4):
            for k in range(len(kap)):
                s[f"low{level}"][number, k] = made[number][k]

    krow = dot01(pack_six(kap6), s["sel"][...])[0:1]
    q, p = iota((32, 128), 0), iota((32, 128), 1)
    kcol = jnp.sum(jnp.where(q == p, krow, 0.0), axis=1, keepdims=True)
    dy, dz, same_x = (q // 8 - p // 8 + 4) % 4, ((q % 8) // 2 - (p % 8) // 2 + 4) % 4, q % 2 == p % 2
    links = jnp.where(same_x & (dz == 0) & (dy % 2 == 1), 1.0, 0.0) + jnp.where(same_x & (dy == 0) & (dz % 2 == 1), 1.0, 0.0)
    links = links + jnp.where((dz == 0) & (dy == 0) & (q % 2 != p % 2), 2.0, 0.0)
    links = jnp.where(p < 32, links, 0.0)
    off = (0.5 / 4096.0) * links * (krow + kcol)
    diag = RATE + jnp.sum(off, axis=1, keepdims=True)
    m_ref = s["m6"]
    m_ref[...] = jnp.where(q == p, diag, jnp.where(p == q + 32, 1.0, -off))

    def eliminate(k, carry):
        m = m_ref[...]
        pivot_row = m_ref[pl.ds(k, 1), :]
        column = jnp.sum(jnp.where(p == k, m, 0.0), axis=1, keepdims=True)
        pivot = jnp.sum(jnp.where(iota((1, 128), 1) == k, pivot_row, 0.0), axis=1, keepdims=True)
        scaled = pivot_row / pivot
        m_ref[...] = jnp.where(q == k, scaled, m - column * scaled)
        return carry

    lax.fori_loop(0, 16, eliminate, 0)

    arrive(in_fa)
    in_fb = ring_y("fb", s["fb"], s["fs"], slab(s["fa"]))
    arrive(in_f2a)
    in_f2b = window_y("f2b", x2f)
    lax.fori_loop(16, 32, eliminate, 0)
    inverse = roll(m_ref[...], -32, 1)
    inverse = jnp.concatenate([jnp.where(p < 32, inverse, 0.0), jnp.zeros((96, 128), F32)], axis=0)
    s["inv"][...] = inverse

    def low_ops(level, count):
        return [[s[f"low{level}"][number, k] for k in range(count)] for number in range(4)]

    arrive(in_fb)
    g3 = [s["fb"][k].reshape(32, 128) for k in range(4)]
    o3, o4, o5 = low_ops(3, 4), low_ops(4, 2), low_ops(5, 1)

    def down(g, o, spread):
        v = low_sweep([w * f for w, f in zip(o[3], g)], g, o, spread)
        return v, low_restrict(low_res(v, g, o, spread), spread)

    v3, g4 = down(g3, o3, 1)
    v4, g5 = down(g4, o4, 2)
    v5, g6 = down(g5, o5, 4)
    x6 = dot01(pack_six(g6[0]), s["sel"][...])
    x6 = jnp.dot(x6, s["inv"][...], precision=lax.Precision.HIGHEST, preferred_element_type=F32)
    x6 = dot01(x6, s["spr"][...])
    x6 = jnp.concatenate([x6[:, 128 * k : 128 * k + 128] for k in range(4)], axis=0)

    def up(v, e, g, o, spread):
        v = [u + e[k * len(e) // len(v)] for k, u in enumerate(v)]
        return low_sweep(low_sweep(v, g, o, spread), g, o, spread)

    v5 = up(v5, [x6], g5, o5, 4)
    v4 = up(v4, v5, g4, o4, 2)
    v3 = up(v3, v4, g3, o3, 1)

    e3, e2, e1 = s["e3"], s["e2"], s["e1"]
    turn = lax.rem(2 * N - 2 * me_y + 3, 2 * N)
    for k in range(4):
        e3[k] = pltpu.roll(v3[k], turn, 0)[0:8]
    picks = []
    lane8 = iota((8, 128), 1)
    for d in range(-2, 3):
        x = lax.rem(me_x + (d + N), N)
        picks.append(jnp.where(lane8 % 4 == x // 4, e3[lax.rem(x, 4)], 0.0))
    spread3 = dot01(jnp.concatenate(picks, axis=0), s["p32"][...])
    for c in range(5):
        e2[c + 1, pl.ds(0, 8, stride=2), :] = spread3[8 * c : 8 * c + 8]
        e2[c + 1, pl.ds(1, 8, stride=2), :] = spread3[8 * c : 8 * c + 8]

    arrive(in_f2b)
    window(x2f, f2)
    for x in range(1, 13):
        v2a[x] = ops2[3][x] * f2[x]
    sweep(v2a, v2b, f2, ops2, 2, 12, 10)
    for x in range(2, 12):
        v2b[x] = v2b[x] + e2[x // 2]
    sweep(v2b, v2a, f2, ops2, 3, 11, 8)
    sweep(v2a, v2b, f2, ops2, 4, 10, 6)

    spread2 = dot01(jnp.concatenate([v2b[x] for x in range(4, 10)], axis=0), s["p21"][...])
    for c in range(6):
        e1[c, pl.ds(0, 16, stride=2), :] = spread2[16 * c : 16 * c + 16]
        e1[c, pl.ds(1, 16, stride=2), :] = spread2[16 * c : 16 * c + 16]
    for x in range(4, 14):
        c = (x + 5) // 2 - 4
        v1b[x] = v1b[x] + jnp.concatenate([e1[c, 12:28], e1[c, 4:12]], axis=0)
    sweep(v1b, v1a, f1, ops1, 5, 13, 8)
    sweep(v1a, v1b, f1, ops1, 6, 12, 6)

    e0 = s["e0"]
    for c in range(6):
        e0[c, pl.ds(0, 24, stride=2), :] = v1b[6 + c]
        e0[c, pl.ds(1, 24, stride=2), :] = v1b[6 + c]
    row8 = iota((8, 128), 0)
    parts = []
    for c in range(6):
        parts += [e0[c, 0:16], jnp.where(row8 < 4, e0[c, 16:24], e0[c, 40:48])]
    spread1 = dot01(jnp.concatenate(parts, axis=0), s["p10"][...])
    stay.wait()
    arrive(in_vd)
    merge0("hd", vd, 2)
    for x in range(1, 13):
        c = (x + 11) // 2 - 6
        ve[x] = vd[x] + spread1[24 * c : 24 * c + 24]
    sweep(ve, vb, g0, ops0, 2, 12, 2)

    def last(x):
        v = vb[x + 3] + ops0[3][x + 3] * res_at(vb, g0, ops0, x + 3)
        out[x] = v[0:16]

    each(0, 8, 2, last)
    for c in sent:
        c.wait_send()


def scratch_list():
    def vmem(*shape, kind=F32):
        return pltpu.VMEM(shape, kind)

    made = [("mat", vmem(8, 16, 256, kind=jnp.int32))]
    for name in ("k0", "va", "vb", "vc", "vd", "ve", "src", "g0", "cx0", "cy0", "cz0", "w0"):
        made.append((name, vmem(14, 24, 256)))
    for name in ("k1", "f1", "v1a", "v1b", "cx1", "cy1", "cz1", "w1"):
        made.append((name, vmem(18, 24, 128)))
    for name in ("k2", "f2", "v2a", "v2b", "cx2", "cy2", "cz2", "w2"):
        made.append((name, vmem(14, 16, 128)))
    for name in ("x2k", "x2f"):
        made.append((name, vmem(14, 5, 4, 128)))
    for name in ("hk", "hv", "hs", "hd"):
        made.append((name + "_e", vmem(8, 8, 256)))
        made.append((name + "_b", vmem(14, 8, 256)))
    made.append(("f2l", vmem(6, 8, 128)))
    for name in ("ka", "fa"):
        made.append((name, vmem(N, 2, 128)))
    for name in ("kb", "fb"):
        made.append((name, vmem(4, N, 2, 128)))
    for name in ("kt", "ft"):
        made.append((name, vmem(2, 128)))
    for name in ("ks", "fs"):
        made.append((name, vmem(4, 2, 128)))
    made.append(("t0", vmem(4, 2, 16, 128)))
    made.append(("t1", vmem(6, 24, 128)))
    made.append(("t2", vmem(1, 8, 128)))
    made.append(("e3", vmem(4, 8, 128)))
    made.append(("e2", vmem(7, 16, 128)))
    made.append(("e1", vmem(6, 32, 128)))
    made.append(("e0", vmem(6, 48, 128)))
    made.append(("low3", vmem(4, 4, 32, 128)))
    made.append(("low4", vmem(4, 2, 32, 128)))
    made.append(("low5", vmem(4, 1, 32, 128)))
    made.append(("m6", vmem(32, 128)))
    made.append(("inv", vmem(128, 128)))
    for name, shape in (("r01", (256, 128)), ("r12", (128, 128)), ("r23", (128, 128)), ("p32", (128, 128)), ("p21", (128, 128)), ("p10", (128, 256)), ("sel", (128, 128)), ("spr", (128, 512))):
        made.append((name, vmem(*shape, kind=BF16)))
    made.append(("load", pltpu.SemaphoreType.DMA((3,))))
    groups = {"hk": 8, "hv": 8, "hs": 8, "hd": 8, "h1k": 14, "h1f": 14, "ka": 15, "kb": 15, "fa": 15, "fb": 15, "k2a": 6, "f2a": 6, "k2b": 4, "f2b": 4}
    for name, count in groups.items():
        made.append((name + "_s", pltpu.SemaphoreType.DMA((count,))))
        made.append((name + "_r", pltpu.SemaphoreType.DMA((count,))))
    return made


SCRATCH = scratch_list()


def shards(concentration, source, material):
    return pl.pallas_call(
        kernel,
        out_shape=jax.ShapeDtypeStruct(concentration.shape, F32),
        in_specs=[pl.BlockSpec(memory_space=pltpu.HBM)] * 3,
        out_specs=pl.BlockSpec(memory_space=pltpu.VMEM),
        scratch_shapes=[shape for _, shape in SCRATCH],
        compiler_params=pltpu.CompilerParams(collective_id=0, has_side_effects=True, vmem_limit_bytes=48 << 20),
        cost_estimate=pl.CostEstimate(flops=20_000_000, bytes_accessed=1_000_000, transcendentals=0),
        name="vcycle",
    )(concentration, source, material)


def solution(mesh):
    placed = P("tx", "ty", None)
    return jax.shard_map(shards, mesh=mesh, in_specs=(placed,) * 3, out_specs=placed, check_vma=False)
```

```python
import jax
import jax.numpy as jnp
from jax import lax
from jax.experimental import pallas as pl
from jax.experimental.pallas import tpu as pltpu
from jax.sharding import PartitionSpec as P

MESH = pl.DeviceIdType.MESH
F32 = jnp.float32
BF16 = jnp.bfloat16
RATE = 0.001
RELAX = 0.8
TABLE = (0.15, 0.3, 0.5, 0.8, 1.2, 2.0, 3.2, 5.0)
N = 16


def iota(shape, axis):
    return lax.broadcasted_iota(jnp.int32, shape, axis)


def roll(v, shift, axis):
    return pltpu.roll(v, shift % v.shape[axis], axis)


def dot01(v, m):
    hi = v.astype(BF16)
    low = (v - hi.astype(F32)).astype(BF16)
    rows = len(v)
    if rows % 16 == 0:
        both = jnp.dot(jnp.concatenate([hi, low], axis=0), m, preferred_element_type=F32)
        return both[:rows] + both[rows:]
    return jnp.dot(hi, m, preferred_element_type=F32) + jnp.dot(low, m, preferred_element_type=F32)


def each(low, high, unroll, body):
    count = high - low
    whole = count // unroll
    if whole > 1:

        def step(i, carry):
            for k in range(unroll):
                body(low + i * unroll + k)
            return carry

        lax.fori_loop(0, whole, step, 0)
        rest = low + whole * unroll
    else:
        rest = low
    for x in range(rest, high):
        body(x)


def make_ops(kappa, ops, scale, layers, unroll):
    cx, cy, cz, w = ops
    half = 0.5 * scale

    def couple(x):
        k = kappa[x]
        cx[x] = half * (k + kappa[x + 1])
        cy[x] = half * (k + roll(k, -1, 0))
        cz[x] = half * (k + roll(k, -1, 1))

    def weigh(x):
        a, b = cy[x], cz[x]
        diag = (RATE + cx[x] + cx[x - 1]) + (a + roll(a, 1, 0)) + (b + roll(b, 1, 1))
        w[x] = RELAX / diag

    each(0, layers - 1, unroll, couple)
    each(1, layers - 1, unroll, weigh)


def residual(v, below, above, g, cx, cxm, cy, cz):
    fy = cy * (roll(v, -1, 0) - v)
    fz = cz * (roll(v, -1, 1) - v)
    r = (g - RATE * v) + (cx * (above - v) - cxm * (v - below))
    return r + (fy - roll(fy, 1, 0)) + (fz - roll(fz, 1, 1))


def res_at(v, g, ops, x):
    cx, cy, cz, _ = ops
    return residual(v[x], v[x - 1], v[x + 1], g[x], cx[x], cx[x - 1], cy[x], cz[x])


def sweep(v, out, g, ops, low, high, unroll):
    def body(x):
        out[x] = v[x] + ops[3][x] * res_at(v, g, ops, x)

    each(low, high, unroll, body)


def x_hi_next(v):
    lane = iota(v.shape, 1)
    return jnp.where(lane % 4 == 3, roll(v, 3, 1), roll(v, -1, 1))


def x_hi_prev(v):
    lane = iota(v.shape, 1)
    return jnp.where(lane % 4 == 0, roll(v, -3, 1), roll(v, 1, 1))


def low_couple(kappa, s, scale):
    half = 0.5 * scale
    nxt = kappa[1:] + [x_hi_next(kappa[0])]
    cx = [half * (k + n) for k, n in zip(kappa, nxt)]
    cy = [half * (k + roll(k, -s, 0)) for k in kappa]
    cz = [half * (k + roll(k, -4 * s, 1)) for k in kappa]
    cxm = [x_hi_prev(cx[-1])] + cx[:-1]
    w = []
    for a, am, b, c in zip(cx, cxm, cy, cz):
        diag = (RATE + a + am) + (b + roll(b, s, 0)) + (c + roll(c, 4 * s, 1))
        w.append(RELAX / diag)
    return cx, cy, cz, w


def low_res(v, g, ops, s):
    cx, cy, cz, _ = ops
    nxt = v[1:] + [x_hi_next(v[0])]
    fx = [c * (n - u) for c, n, u in zip(cx, nxt, v)]
    fxm = [x_hi_prev(fx[-1])] + fx[:-1]
    out = []
    for u, f, a, am, b, c in zip(v, g, fx, fxm, cy, cz):
        fy = b * (roll(u, -s, 0) - u)
        fz = c * (roll(u, -4 * s, 1) - u)
        r = (f - RATE * u) + (a - am)
        out.append(r + (fy - roll(fy, s, 0)) + (fz - roll(fz, 4 * s, 1)))
    return out


def low_sweep(v, g, ops, s):
    return [u + w * r for u, w, r in zip(v, ops[3], low_res(v, g, ops, s))]


def low_restrict(v, s):
    if len(v) > 1:
        v = [v[2 * k] + v[2 * k + 1] for k in range(len(v) // 2)]
    else:
        u = v[0]
        lane = iota(u.shape, 1)
        v = [u + jnp.where(lane % 2 == 0, roll(u, -1, 1), roll(u, 1, 1))]
    out = []
    for u in v:
        row, lane = iota(u.shape, 0), iota(u.shape, 1)
        u = u + jnp.where((row // s) % 2 == 0, roll(u, -s, 0), roll(u, s, 0))
        u = u + jnp.where((lane // (4 * s)) % 2 == 0, roll(u, -4 * s, 1), roll(u, 4 * s, 1))
        out.append(u * 0.125)
    return out


def pack_six(v):
    lane = iota((8, 128), 1)
    y = (lane % 32) // 4
    out = v[24:32]
    for k in (2, 1, 0):
        out = jnp.where(y == k, v[8 * k : 8 * k + 8], out)
    return out


def kernel(conc, source, material, out, *scratch):
    names = [name for name, _ in SCRATCH]
    s = dict(zip(names, scratch))
    ops0, ops1, ops2 = [[s[f"{name}{level}"] for name in ("cx", "cy", "cz", "w")] for level in (0, 1, 2)]
    me_x, me_y = lax.axis_index("tx"), lax.axis_index("ty")

    def device(dx, dy):
        return (lax.rem(me_x + (dx + N), N), lax.rem(me_y + (dy + N), N))

    counter = {}

    def copy(group, src, dst, dx, dy):
        k = counter.get(group, 0)
        counter[group] = k + 1
        c = pltpu.make_async_remote_copy(
            src, dst, s[group + "_s"].at[k], s[group + "_r"].at[k], device_id=device(dx, dy), device_id_type=MESH
        )
        c.start()
        return c

    sent = []

    def arrive(copies):
        for c in copies:
            c.wait_recv()
        sent.extend(copies)

    tile0 = (slice(3, 11), slice(0, 16))
    loads = [
        pltpu.make_async_copy(material, s["mat"], s["load"].at[0]),
        pltpu.make_async_copy(conc, s["va"].at[3:11, 0:16], s["load"].at[1]),
        pltpu.make_async_copy(source, s["src"].at[3:11, 0:16], s["load"].at[2]),
    ]
    for c in loads:
        c.start()
    barrier = pltpu.get_barrier_semaphore()
    peers = [(d, 0) for d in range(1, N)] + [(0, d) for d in range(1, N)]
    peers += [(a, b) for a in (-2, -1, 1, 2) for b in (-1, 1)]
    peers.sort(key=lambda p: -min(p[0] % N, -p[0] % N) - min(p[1] % N, -p[1] % N))
    for p in peers:
        pl.semaphore_signal(barrier, inc=1, device_id=device(*p), device_id_type=MESH)

    def matrix(name, rule):
        shape = s[name].shape
        s[name][...] = jnp.where(rule(iota(shape, 0), iota(shape, 1)), 1.0, 0.0).astype(BF16)

    matrix("r01", lambda i, j: i // 2 == j)
    matrix("r12", lambda i, j: i // 2 == j % 64)
    matrix("r23", lambda i, j: i // 2 == j // 4)
    matrix("p32", lambda i, j: i // 4 == (j % 64) // 2)
    matrix("p21", lambda i, j: i == j // 2)
    matrix("p10", lambda i, j: i == j // 2)
    matrix("sel", lambda i, j: ((i % 32) // 4 < 4) & (i % 2 == 0) & (j == ((i % 32) // 4) * 8 + (i // 32) * 2 + (i % 4) // 2))
    matrix("spr", lambda i, j: i == (j // 128) * 8 + ((j % 128) // 32) * 2 + (j % 4) // 2)

    loads[0].wait()
    k0 = s["k0"]

    def lookup(x):
        m = s["mat"][x]
        result = jnp.zeros(m.shape, F32)
        for slot, value in enumerate(TABLE):
            result = jnp.where(m == slot, F32(value), result)
        k0[x + 3, 0:16] = result

    each(0, 8, 2, lookup)
    loads[1].wait()
    loads[2].wait()
    pl.semaphore_wait(barrier, len(peers))

    def halo0(group, ref, dest, w, c):
        edge, below = s[group + "_e"], s[group + "_b"]
        for x in range(8):
            edge[x] = roll(ref[x + 3, 8:16], w, 0)
        copies = []
        for dx, dy in ((1, 0), (-1, 0), (0, 1), (0, -1), (1, 1), (1, -1), (-1, 1), (-1, -1)):
            n = c if dy else w
            x0, x1 = {0: (3, 11), -1: (3, 3 + n), 1: (11 - n, 11)}[dx]
            y0, y1 = x0 - 8 * dx, x1 - 8 * dx
            if dy == 0:
                copies.append(copy(group, ref.at[x0:x1, 0:16], dest.at[y0:y1, 0:16], dx, dy))
            elif dy < 0:
                copies.append(copy(group, ref.at[x0:x1, 0:w], dest.at[y0:y1, 16 : 16 + w], dx, dy))
            else:
                copies.append(copy(group, edge.at[x0 - 3 : x1 - 3, 0:w], below.at[y0:y1, 0:w], dx, dy))
        return copies

    def merge0(group, dest, w):
        below = s[group + "_b"]
        row = iota((8, 256), 0)
        for x in range(14):
            dest[x, 16:24] = jnp.where(row < 4, dest[x, 16:24], roll(below[x], -w, 0))

    in_k0 = halo0("hk", k0, k0, 3, 2)
    in_va = halo0("hv", s["va"], s["va"], 3, 2)
    in_src = halo0("hs", s["src"], s["src"], 2, 1)

    t0, t1, t2 = s["t0"], s["t1"], s["t2"]

    def put0(c, pair):
        t0[c, 0] = pair[:16, :128]
        t0[c, 1] = pair[:16, 128:]

    def take0():
        rows = []
        for c in range(4):
            halves = [t0[c, h, pl.ds(0, 8, stride=2), :] + t0[c, h, pl.ds(1, 8, stride=2), :] for h in range(2)]
            rows.append(jnp.concatenate(halves, axis=1))
        return dot01(jnp.concatenate(rows, axis=0), s["r01"][...]) * 0.125

    def row_pairs(ref, k, start, count):
        return ref[k, pl.ds(start, count, stride=2), :] + ref[k, pl.ds(start + 1, count, stride=2), :]

    k1, k2, x2k, x2f = s["k1"], s["k2"], s["x2k"], s["x2f"]
    for c in range(4):
        put0(c, k0[3 + 2 * c, 0:16] + k0[4 + 2 * c, 0:16])
    tile = take0()
    for c in range(4):
        k1[7 + c, 0:8] = tile[8 * c : 8 * c + 8]

    def halo1(group, ref, w):
        copies = []
        for dx, dy in ((1, 0), (-1, 0), (0, 1), (0, -1), (2, 0), (-2, 0), (1, 1), (1, -1), (-1, 1), (-1, -1), (2, 1), (2, -1), (-2, 1), (-2, -1)):
            nx = {0: 4, 1: 4, 2: w - 4 if dy == 0 else w - 5}[abs(dx)]
            ny = 8 if dy == 0 else {0: w, 1: w - 1, 2: w - 5}[abs(dx)]
            xs = slice(11 - nx, 11) if dx > 0 else slice(7, 7 + nx)
            xd = slice(xs.start - 4 * dx, xs.stop - 4 * dx)
            ys = slice(0, 8) if dy > 0 else slice(0, ny)
            yd = slice(16, 24) if dy > 0 else slice(-8 * dy, ny - 8 * dy)
            copies.append(copy(group, ref.at[xs, ys], ref.at[xd, yd], dx, dy))
        return copies

    def to_level2(get):
        parts = []
        for c in range(len(get) // 2):
            pair = get[2 * c] + get[2 * c + 1]
            if len(pair) == 8:
                t1[c, 4:12] = pair
            else:
                t1[c] = roll(pair, 4, 0)
        for c in range(len(get) // 2):
            parts.append(row_pairs(t1, c, 0, 8))
        return dot01(jnp.concatenate(parts, axis=0), s["r12"][...]) * 0.125

    def to_level3(pair, row0):
        t2[0] = dot01(pair, s["r23"][...]) * 0.125
        return row_pairs(t2, 0, row0, 2)

    low = to_level2([tile[8 * c : 8 * c + 8] for c in range(4)])
    for c in range(2):
        x2k[6 + c, 2] = low[8 * c + 2 : 8 * c + 6]
    base = to_level3(low[0:8] + low[8:16], 2)

    def ring_x(group, ref, tile_ref, value):
        tile_ref[...] = value
        ref[me_x] = value
        return [copy(group, tile_ref, ref.at[me_x], d, 0) for d in range(1, N)]

    def window_x(group, ref):
        return [
            copy(group, ref.at[6:8, 2], ref.at[6 - 2 * d : 8 - 2 * d, 2], d, 0) for d in (1, -1, 2, -2, 3, -3)
        ]

    def slab(ref):
        lane = iota((2, 128), 1)
        out_parts = []
        for k in range(4):
            v = ref[12 + k]
            for h in (2, 1, 0):
                v = jnp.where(lane % 4 == h, ref[4 * h + k], v)
            out_parts.append(v)
        return out_parts

    def ring_y(group, ref, slab_ref, parts):
        for k in range(4):
            slab_ref[k] = parts[k]
            ref[k, me_y] = parts[k]
        return [copy(group, slab_ref, ref.at[:, me_y], 0, d) for d in range(1, N)]

    def window_y(group, ref):
        return [copy(group, ref.at[:, 2], ref.at[:, 2 - d], 0, d) for d in (1, -1, 2, -2)]

    def window(ref, dest):
        for x in range(14):
            dest[x] = ref[x].reshape(20, 128)[2:18]

    in_k1 = halo1("h1k", k1, 7)
    in_ka = ring_x("ka", s["ka"], s["kt"], base)
    in_k2a = window_x("k2a", x2k)
    arrive(in_k0)
    merge0("hk", k0, 3)
    make_ops(k0, ops0, 1.0, 14, 3)
    arrive(in_va)
    arrive(in_src)
    merge0("hv", s["va"], 3)
    merge0("hs", s["src"], 2)
    va, vb, vc, vd, ve, src, g0 = [s[name] for name in ("va", "vb", "vc", "vd", "ve", "src", "g0")]

    def force(x):
        g0[x] = RATE * va[x] + src[x]

    each(1, 13, 3, force)
    sweep(va, vb, g0, ops0, 1, 13, 3)
    sweep(vb, vc, g0, ops0, 2, 12, 2)

    def down0(c):
        put0(c, res_at(vc, g0, ops0, 2 * c + 3) + res_at(vc, g0, ops0, 2 * c + 4))

    each(0, 4, 1, down0)
    tile = take0()
    f1 = s["f1"]
    for c in range(4):
        f1[7 + c, 0:8] = tile[8 * c : 8 * c + 8]
    in_f1 = halo1("h1f", f1, 6)

    arrive(in_ka)
    in_kb = ring_y("kb", s["kb"], s["ks"], slab(s["ka"]))
    arrive(in_k2a)
    in_k2b = window_y("k2b", x2k)
    stay = pltpu.make_async_copy(vc.at[tile0], vd.at[tile0], s["load"].at[0])
    stay.start()
    in_vd = halo0("hd", vc, vd, 2, 1)

    arrive(in_k1)
    make_ops(k1, ops1, 0.25, 18, 4)
    arrive(in_f1)

    v1a, v1b = s["v1a"], s["v1b"]

    def start1(x):
        v1a[x] = ops1[3][x] * f1[x]

    each(1, 17, 4, start1)
    sweep(v1a, v1b, f1, ops1, 2, 16, 7)
    low = to_level2([res_at(v1b, f1, ops1, x) for x in range(3, 15)])
    f2l = s["f2l"]
    f2 = s["f2"]
    for c in range(6):
        f2l[c] = low[8 * c : 8 * c + 8]
    for c in range(2):
        x2f[6 + c, 2] = low[8 * c + 18 : 8 * c + 22]

    arrive(in_k2b)
    window(x2k, k2)
    make_ops(k2, ops2, 0.0625, 14, 13)
    v2a, v2b = s["v2a"], s["v2b"]
    near = [[ref[x, 4:12] for x in range(4, 10)] for ref in ops2]
    fl = [f2l[c] for c in range(6)]
    vl = [near[3][c] * fl[c] for c in range(6)]

    def res_near(v, c):
        return residual(v[c], v[c - 1], v[c + 1], fl[c], near[0][c], near[0][c - 1], near[1][c], near[2][c])

    ul = [None] + [vl[c] + near[3][c] * res_near(vl, c) for c in range(1, 5)]
    base = to_level3(res_near(ul + [None], 2) + res_near(ul + [None], 3), 2)
    in_fa = ring_x("fa", s["fa"], s["ft"], base)
    in_f2a = window_x("f2a", x2f)

    arrive(in_kb)
    kap3 = [s["kb"][k].reshape(32, 128) for k in range(4)]
    kap4 = low_restrict(kap3, 1)
    kap5 = low_restrict(kap4, 2)
    kap6 = low_restrict(kap5, 4)[0]
    for level, kap, spread in ((3, kap3, 1), (4, kap4, 2), (5, kap5, 4)):
        made = low_couple(kap, spread, 1.0 / 4.0**level)
        for number in range(4):
            for k in range(len(kap)):
                s[f"low{level}"][number, k] = made[number][k]

    krow = dot01(pack_six(kap6), s["sel"][...])[0:1]
    q, p = iota((32, 128), 0), iota((32, 128), 1)
    kcol = jnp.sum(jnp.where(q == p, krow, 0.0), axis=1, keepdims=True)
    dy, dz, same_x = (q // 8 - p // 8 + 4) % 4, ((q % 8) // 2 - (p % 8) // 2 + 4) % 4, q % 2 == p % 2
    links = jnp.where(same_x & (dz == 0) & (dy % 2 == 1), 1.0, 0.0) + jnp.where(same_x & (dy == 0) & (dz % 2 == 1), 1.0, 0.0)
    links = links + jnp.where((dz == 0) & (dy == 0) & (q % 2 != p % 2), 2.0, 0.0)
    links = jnp.where(p < 32, links, 0.0)
    off = (0.5 / 4096.0) * links * (krow + kcol)
    diag = RATE + jnp.sum(off, axis=1, keepdims=True)
    m_ref = s["m6"]
    m_ref[...] = jnp.where(q == p, diag, jnp.where(p == q + 32, 1.0, -off))

    def eliminate(k, carry):
        m = m_ref[...]
        pivot_row = m_ref[pl.ds(k, 1), :]
        column = jnp.sum(jnp.where(p == k, m, 0.0), axis=1, keepdims=True)
        pivot = jnp.sum(jnp.where(iota((1, 128), 1) == k, pivot_row, 0.0), axis=1, keepdims=True)
        scaled = pivot_row / pivot
        m_ref[...] = jnp.where(q == k, scaled, m - column * scaled)
        return carry

    lax.fori_loop(0, 16, eliminate, 0)

    arrive(in_fa)
    in_fb = ring_y("fb", s["fb"], s["fs"], slab(s["fa"]))
    arrive(in_f2a)
    in_f2b = window_y("f2b", x2f)
    lax.fori_loop(16, 32, eliminate, 0)
    inverse = roll(m_ref[...], -32, 1)
    inverse = jnp.concatenate([jnp.where(p < 32, inverse, 0.0), jnp.zeros((96, 128), F32)], axis=0)
    inverse = dot01(inverse, s["spr"][...])
    hi = inverse.astype(BF16)
    rest = inverse - hi.astype(F32)
    mid = rest.astype(BF16)
    pieces = (hi, mid, (rest - mid.astype(F32)).astype(BF16))
    a, b, c = [jnp.dot(s["sel"][...], piece, preferred_element_type=F32) for piece in pieces]
    s["inv"][...] = a + (b + c)

    def low_ops(level, count):
        return [[s[f"low{level}"][number, k] for k in range(count)] for number in range(4)]

    arrive(in_fb)
    g3 = [s["fb"][k].reshape(32, 128) for k in range(4)]
    o3, o4, o5 = low_ops(3, 4), low_ops(4, 2), low_ops(5, 1)

    def down(g, o, spread):
        v = low_sweep([w * f for w, f in zip(o[3], g)], g, o, spread)
        return v, low_restrict(low_res(v, g, o, spread), spread)

    v3, g4 = down(g3, o3, 1)
    v4, g5 = down(g4, o4, 2)
    v5, g6 = down(g5, o5, 4)
    x6 = jnp.dot(pack_six(g6[0]), s["inv"][...], precision=lax.Precision.HIGHEST, preferred_element_type=F32)
    x6 = jnp.concatenate([x6[:, 128 * k : 128 * k + 128] for k in range(4)], axis=0)

    def up(v, e, g, o, spread):
        v = [u + e[k * len(e) // len(v)] for k, u in enumerate(v)]
        return low_sweep(low_sweep(v, g, o, spread), g, o, spread)

    v5 = up(v5, [x6], g5, o5, 4)
    v4 = up(v4, v5, g4, o4, 2)
    v3 = up(v3, v4, g3, o3, 1)

    e3, e2, e1 = s["e3"], s["e2"], s["e1"]
    turn = lax.rem(2 * N - 2 * me_y + 3, 2 * N)
    for k in range(4):
        e3[k] = pltpu.roll(v3[k], turn, 0)[0:8]
    picks = []
    lane8 = iota((8, 128), 1)
    for d in range(-2, 3):
        x = lax.rem(me_x + (d + N), N)
        picks.append(jnp.where(lane8 % 4 == x // 4, e3[lax.rem(x, 4)], 0.0))
    spread3 = dot01(jnp.concatenate(picks, axis=0), s["p32"][...])
    for c in range(5):
        e2[c + 1, pl.ds(0, 8, stride=2), :] = spread3[8 * c : 8 * c + 8]
        e2[c + 1, pl.ds(1, 8, stride=2), :] = spread3[8 * c : 8 * c + 8]

    arrive(in_f2b)
    window(x2f, f2)
    for x in range(1, 13):
        v2a[x] = ops2[3][x] * f2[x]
    sweep(v2a, v2b, f2, ops2, 2, 12, 10)
    for x in range(2, 12):
        v2b[x] = v2b[x] + e2[x // 2]
    sweep(v2b, v2a, f2, ops2, 3, 11, 8)
    sweep(v2a, v2b, f2, ops2, 4, 10, 6)

    spread2 = dot01(jnp.concatenate([v2b[x] for x in range(4, 10)], axis=0), s["p21"][...])
    for c in range(6):
        e1[c, pl.ds(0, 16, stride=2), :] = spread2[16 * c : 16 * c + 16]
        e1[c, pl.ds(1, 16, stride=2), :] = spread2[16 * c : 16 * c + 16]
    for x in range(4, 14):
        c = (x + 5) // 2 - 4
        v1b[x] = v1b[x] + jnp.concatenate([e1[c, 12:28], e1[c, 4:12]], axis=0)
    sweep(v1b, v1a, f1, ops1, 5, 13, 8)
    sweep(v1a, v1b, f1, ops1, 6, 12, 6)

    e0 = s["e0"]
    for c in range(6):
        e0[c, pl.ds(0, 24, stride=2), :] = v1b[6 + c]
        e0[c, pl.ds(1, 24, stride=2), :] = v1b[6 + c]
    row8 = iota((8, 128), 0)
    parts = []
    for c in range(6):
        parts += [e0[c, 0:16], jnp.where(row8 < 4, e0[c, 16:24], e0[c, 40:48])]
    spread1 = dot01(jnp.concatenate(parts, axis=0), s["p10"][...])
    stay.wait()
    arrive(in_vd)
    merge0("hd", vd, 2)
    for x in range(1, 13):
        c = (x + 11) // 2 - 6
        ve[x] = vd[x] + spread1[24 * c : 24 * c + 24]
    sweep(ve, vb, g0, ops0, 2, 12, 2)

    def last(x):
        v = vb[x + 3] + ops0[3][x + 3] * res_at(vb, g0, ops0, x + 3)
        out[x] = v[0:16]

    each(0, 8, 2, last)
    for c in sent:
        c.wait_send()


def scratch_list():
    def vmem(*shape, kind=F32):
        return pltpu.VMEM(shape, kind)

    made = [("mat", vmem(8, 16, 256, kind=jnp.int32))]
    for name in ("k0", "va", "vb", "vc", "vd", "ve", "src", "g0", "cx0", "cy0", "cz0", "w0"):
        made.append((name, vmem(14, 24, 256)))
    for name in ("k1", "f1", "v1a", "v1b", "cx1", "cy1", "cz1", "w1"):
        made.append((name, vmem(18, 24, 128)))
    for name in ("k2", "f2", "v2a", "v2b", "cx2", "cy2", "cz2", "w2"):
        made.append((name, vmem(14, 16, 128)))
    for name in ("x2k", "x2f"):
        made.append((name, vmem(14, 5, 4, 128)))
    for name in ("hk", "hv", "hs", "hd"):
        made.append((name + "_e", vmem(8, 8, 256)))
        made.append((name + "_b", vmem(14, 8, 256)))
    made.append(("f2l", vmem(6, 8, 128)))
    for name in ("ka", "fa"):
        made.append((name, vmem(N, 2, 128)))
    for name in ("kb", "fb"):
        made.append((name, vmem(4, N, 2, 128)))
    for name in ("kt", "ft"):
        made.append((name, vmem(2, 128)))
    for name in ("ks", "fs"):
        made.append((name, vmem(4, 2, 128)))
    made.append(("t0", vmem(4, 2, 16, 128)))
    made.append(("t1", vmem(6, 24, 128)))
    made.append(("t2", vmem(1, 8, 128)))
    made.append(("e3", vmem(4, 8, 128)))
    made.append(("e2", vmem(7, 16, 128)))
    made.append(("e1", vmem(6, 32, 128)))
    made.append(("e0", vmem(6, 48, 128)))
    made.append(("low3", vmem(4, 4, 32, 128)))
    made.append(("low4", vmem(4, 2, 32, 128)))
    made.append(("low5", vmem(4, 1, 32, 128)))
    made.append(("m6", vmem(32, 128)))
    made.append(("inv", vmem(128, 512)))
    for name, shape in (("r01", (256, 128)), ("r12", (128, 128)), ("r23", (128, 128)), ("p32", (128, 128)), ("p21", (128, 128)), ("p10", (128, 256)), ("sel", (128, 128)), ("spr", (128, 512))):
        made.append((name, vmem(*shape, kind=BF16)))
    made.append(("load", pltpu.SemaphoreType.DMA((3,))))
    groups = {"hk": 8, "hv": 8, "hs": 8, "hd": 8, "h1k": 14, "h1f": 14, "ka": 15, "kb": 15, "fa": 15, "fb": 15, "k2a": 6, "f2a": 6, "k2b": 4, "f2b": 4}
    for name, count in groups.items():
        made.append((name + "_s", pltpu.SemaphoreType.DMA((count,))))
        made.append((name + "_r", pltpu.SemaphoreType.DMA((count,))))
    return made


SCRATCH = scratch_list()


def shards(concentration, source, material):
    return pl.pallas_call(
        kernel,
        out_shape=jax.ShapeDtypeStruct(concentration.shape, F32),
        in_specs=[pl.BlockSpec(memory_space=pltpu.HBM)] * 3,
        out_specs=pl.BlockSpec(memory_space=pltpu.VMEM),
        scratch_shapes=[shape for _, shape in SCRATCH],
        compiler_params=pltpu.CompilerParams(collective_id=0, has_side_effects=True, vmem_limit_bytes=56360960),
        cost_estimate=pl.CostEstimate(flops=20_000_000, bytes_accessed=1_000_000, transcendentals=0),
        name="vcycle",
    )(concentration, source, material)


def solution(mesh):
    placed = P("tx", "ty", None)
    return jax.shard_map(shards, mesh=mesh, in_specs=(placed,) * 3, out_specs=placed, check_vma=False)
```

```python
import jax
import jax.numpy as jnp
from jax import lax
from jax.experimental import pallas as pl
from jax.experimental.pallas import tpu as pltpu
from jax.sharding import PartitionSpec as P

MESH = pl.DeviceIdType.MESH
F32 = jnp.float32
BF16 = jnp.bfloat16
RATE = 0.001
RELAX = 0.8
TABLE = (0.15, 0.3, 0.5, 0.8, 1.2, 2.0, 3.2, 5.0)
N = 16


def iota(shape, axis):
    return lax.broadcasted_iota(jnp.int32, shape, axis)


def roll(v, shift, axis):
    return pltpu.roll(v, shift % v.shape[axis], axis)


def dot01(v, m):
    hi = v.astype(BF16)
    low = (v - hi.astype(F32)).astype(BF16)
    rows = len(v)
    if rows % 16 == 0:
        both = jnp.dot(jnp.concatenate([hi, low], axis=0), m, preferred_element_type=F32)
        return both[:rows] + both[rows:]
    return jnp.dot(hi, m, preferred_element_type=F32) + jnp.dot(low, m, preferred_element_type=F32)


def each(low, high, unroll, body):
    count = high - low
    whole = count // unroll
    if whole > 1:

        def step(i, carry):
            for k in range(unroll):
                body(low + i * unroll + k)
            return carry

        lax.fori_loop(0, whole, step, 0)
        rest = low + whole * unroll
    else:
        rest = low
    for x in range(rest, high):
        body(x)


def make_ops(kappa, ops, scale, layers, unroll):
    cx, cy, cz, w = ops
    half = 0.5 * scale

    def couple(x):
        k = kappa[x]
        cx[x] = half * (k + kappa[x + 1])
        cy[x] = half * (k + roll(k, -1, 0))
        cz[x] = half * (k + roll(k, -1, 1))

    def weigh(x):
        a, b = cy[x], cz[x]
        diag = (RATE + cx[x] + cx[x - 1]) + (a + roll(a, 1, 0)) + (b + roll(b, 1, 1))
        w[x] = RELAX / diag

    each(0, layers - 1, unroll, couple)
    each(1, layers - 1, unroll, weigh)


def residual(v, below, above, g, cx, cxm, cy, cz):
    fy = cy * (roll(v, -1, 0) - v)
    fz = cz * (roll(v, -1, 1) - v)
    r = (g - RATE * v) + (cx * (above - v) - cxm * (v - below))
    return r + (fy - roll(fy, 1, 0)) + (fz - roll(fz, 1, 1))


def res_at(v, g, ops, x):
    cx, cy, cz, _ = ops
    return residual(v[x], v[x - 1], v[x + 1], g[x], cx[x], cx[x - 1], cy[x], cz[x])


def sweep(v, out, g, ops, low, high, unroll):
    def body(x):
        out[x] = v[x] + ops[3][x] * res_at(v, g, ops, x)

    each(low, high, unroll, body)


def x_hi_next(v):
    lane = iota(v.shape, 1)
    return jnp.where(lane % 4 == 3, roll(v, 3, 1), roll(v, -1, 1))


def x_hi_prev(v):
    lane = iota(v.shape, 1)
    return jnp.where(lane % 4 == 0, roll(v, -3, 1), roll(v, 1, 1))


def low_couple(kappa, s, scale):
    half = 0.5 * scale
    nxt = kappa[1:] + [x_hi_next(kappa[0])]
    cx = [half * (k + n) for k, n in zip(kappa, nxt)]
    cy = [half * (k + roll(k, -s, 0)) for k in kappa]
    cz = [half * (k + roll(k, -4 * s, 1)) for k in kappa]
    cxm = [x_hi_prev(cx[-1])] + cx[:-1]
    w = []
    for a, am, b, c in zip(cx, cxm, cy, cz):
        diag = (RATE + a + am) + (b + roll(b, s, 0)) + (c + roll(c, 4 * s, 1))
        w.append(RELAX / diag)
    return cx, cy, cz, w


def low_res(v, g, ops, s):
    cx, cy, cz, _ = ops
    nxt = v[1:] + [x_hi_next(v[0])]
    fx = [c * (n - u) for c, n, u in zip(cx, nxt, v)]
    fxm = [x_hi_prev(fx[-1])] + fx[:-1]
    out = []
    for u, f, a, am, b, c in zip(v, g, fx, fxm, cy, cz):
        fy = b * (roll(u, -s, 0) - u)
        fz = c * (roll(u, -4 * s, 1) - u)
        r = (f - RATE * u) + (a - am)
        out.append(r + (fy - roll(fy, s, 0)) + (fz - roll(fz, 4 * s, 1)))
    return out


def low_sweep(v, g, ops, s):
    return [u + w * r for u, w, r in zip(v, ops[3], low_res(v, g, ops, s))]


def low_restrict(v, s):
    if len(v) > 1:
        v = [v[2 * k] + v[2 * k + 1] for k in range(len(v) // 2)]
    else:
        u = v[0]
        lane = iota(u.shape, 1)
        v = [u + jnp.where(lane % 2 == 0, roll(u, -1, 1), roll(u, 1, 1))]
    out = []
    for u in v:
        row, lane = iota(u.shape, 0), iota(u.shape, 1)
        u = u + jnp.where((row // s) % 2 == 0, roll(u, -s, 0), roll(u, s, 0))
        u = u + jnp.where((lane // (4 * s)) % 2 == 0, roll(u, -4 * s, 1), roll(u, 4 * s, 1))
        out.append(u * 0.125)
    return out


def pack_six(v):
    lane = iota((8, 128), 1)
    y = (lane % 32) // 4
    out = v[24:32]
    for k in (2, 1, 0):
        out = jnp.where(y == k, v[8 * k : 8 * k + 8], out)
    return out


def kernel(conc, source, material, out, *scratch):
    names = [name for name, _ in SCRATCH]
    s = dict(zip(names, scratch))
    ops0, ops1, ops2 = [[s[f"{name}{level}"] for name in ("cx", "cy", "cz", "w")] for level in (0, 1, 2)]
    me_x, me_y = lax.axis_index("tx"), lax.axis_index("ty")

    def device(dx, dy):
        return (lax.rem(me_x + (dx + N), N), lax.rem(me_y + (dy + N), N))

    counter = {}

    def copy(group, src, dst, dx, dy):
        k = counter.get(group, 0)
        counter[group] = k + 1
        c = pltpu.make_async_remote_copy(
            src, dst, s[group + "_s"].at[k], s[group + "_r"].at[k], device_id=device(dx, dy), device_id_type=MESH
        )
        c.start()
        return c

    sent = []

    def arrive(copies):
        for c in copies:
            c.wait_recv()
        sent.extend(copies)

    tile0 = (slice(3, 11), slice(0, 16))
    loads = [
        pltpu.make_async_copy(material, s["mat"], s["load"].at[0]),
        pltpu.make_async_copy(conc, s["va"].at[3:11, 0:16], s["load"].at[1]),
        pltpu.make_async_copy(source, s["src"].at[3:11, 0:16], s["load"].at[2]),
    ]
    for c in loads:
        c.start()
    barrier = pltpu.get_barrier_semaphore()
    peers = [(d, 0) for d in range(1, N)] + [(0, d) for d in range(1, N)]
    peers += [(a, b) for a in (-2, -1, 1, 2) for b in (-1, 1)]
    peers.sort(key=lambda p: -min(p[0] % N, -p[0] % N) - min(p[1] % N, -p[1] % N))
    for p in peers:
        pl.semaphore_signal(barrier, inc=1, device_id=device(*p), device_id_type=MESH)

    def matrix(name, rule):
        shape = s[name].shape
        s[name][...] = jnp.where(rule(iota(shape, 0), iota(shape, 1)), 1.0, 0.0).astype(BF16)

    matrix("r01", lambda i, j: i // 2 == j)
    matrix("r12", lambda i, j: i // 2 == j % 64)
    matrix("r23", lambda i, j: i // 2 == j // 4)
    matrix("p32", lambda i, j: i // 4 == (j % 64) // 2)
    matrix("p21", lambda i, j: i == j // 2)
    matrix("p10", lambda i, j: i == j // 2)
    matrix("sel", lambda i, j: ((i % 32) // 4 < 4) & (i % 2 == 0) & (j == ((i % 32) // 4) * 8 + (i // 32) * 2 + (i % 4) // 2))
    matrix("spr", lambda i, j: i == (j // 128) * 8 + ((j % 128) // 32) * 2 + (j % 4) // 2)

    loads[0].wait()
    k0 = s["k0"]

    def lookup(x):
        m = s["mat"][x]
        result = jnp.zeros(m.shape, F32)
        for slot, value in enumerate(TABLE):
            result = jnp.where(m == slot, F32(value), result)
        k0[x + 3, 0:16] = result

    each(0, 8, 8, lookup)
    loads[1].wait()
    loads[2].wait()
    pl.semaphore_wait(barrier, len(peers))

    def halo0(group, ref, dest, w, c):
        edge, below = s[group + "_e"], s[group + "_b"]
        for x in range(8):
            edge[x] = roll(ref[x + 3, 8:16], w, 0)
        copies = []
        for dx, dy in ((1, 0), (-1, 0), (0, 1), (0, -1), (1, 1), (1, -1), (-1, 1), (-1, -1)):
            n = c if dy else w
            x0, x1 = {0: (3, 11), -1: (3, 3 + n), 1: (11 - n, 11)}[dx]
            y0, y1 = x0 - 8 * dx, x1 - 8 * dx
            if dy == 0:
                copies.append(copy(group, ref.at[x0:x1, 0:16], dest.at[y0:y1, 0:16], dx, dy))
            elif dy < 0:
                copies.append(copy(group, ref.at[x0:x1, 0:w], dest.at[y0:y1, 16 : 16 + w], dx, dy))
            else:
                copies.append(copy(group, edge.at[x0 - 3 : x1 - 3, 0:w], below.at[y0:y1, 0:w], dx, dy))
        return copies

    def merge0(group, dest, w):
        below = s[group + "_b"]
        row = iota((8, 256), 0)
        for x in range(14):
            dest[x, 16:24] = jnp.where(row < 4, dest[x, 16:24], roll(below[x], -w, 0))

    in_k0 = halo0("hk", k0, k0, 3, 2)
    in_va = halo0("hv", s["va"], s["va"], 3, 2)
    in_src = halo0("hs", s["src"], s["src"], 2, 1)

    t0, t1, t2 = s["t0"], s["t1"], s["t2"]

    def put0(c, pair):
        t0[c, 0] = pair[:16, :128]
        t0[c, 1] = pair[:16, 128:]

    def take0():
        rows = []
        for c in range(4):
            halves = [t0[c, h, pl.ds(0, 8, stride=2), :] + t0[c, h, pl.ds(1, 8, stride=2), :] for h in range(2)]
            rows.append(jnp.concatenate(halves, axis=1))
        return dot01(jnp.concatenate(rows, axis=0), s["r01"][...]) * 0.125

    def row_pairs(ref, k, start, count):
        return ref[k, pl.ds(start, count, stride=2), :] + ref[k, pl.ds(start + 1, count, stride=2), :]

    k1, k2, x2k, x2f = s["k1"], s["k2"], s["x2k"], s["x2f"]
    for c in range(4):
        put0(c, k0[3 + 2 * c, 0:16] + k0[4 + 2 * c, 0:16])
    tile = take0()
    for c in range(4):
        k1[7 + c, 0:8] = tile[8 * c : 8 * c + 8]

    def halo1(group, ref, w):
        copies = []
        for dx, dy in ((1, 0), (-1, 0), (0, 1), (0, -1), (2, 0), (-2, 0), (1, 1), (1, -1), (-1, 1), (-1, -1), (2, 1), (2, -1), (-2, 1), (-2, -1)):
            nx = {0: 4, 1: 4, 2: w - 4 if dy == 0 else w - 5}[abs(dx)]
            ny = 8 if dy == 0 else {0: w, 1: w - 1, 2: w - 5}[abs(dx)]
            xs = slice(11 - nx, 11) if dx > 0 else slice(7, 7 + nx)
            xd = slice(xs.start - 4 * dx, xs.stop - 4 * dx)
            ys = slice(0, 8) if dy > 0 else slice(0, ny)
            yd = slice(16, 24) if dy > 0 else slice(-8 * dy, ny - 8 * dy)
            copies.append(copy(group, ref.at[xs, ys], ref.at[xd, yd], dx, dy))
        return copies

    def to_level2(get):
        parts = []
        for c in range(len(get) // 2):
            pair = get[2 * c] + get[2 * c + 1]
            if len(pair) == 8:
                t1[c, 4:12] = pair
            else:
                t1[c] = roll(pair, 4, 0)
        for c in range(len(get) // 2):
            parts.append(row_pairs(t1, c, 0, 8))
        return dot01(jnp.concatenate(parts, axis=0), s["r12"][...]) * 0.125

    def to_level3(pair, row0):
        t2[0] = dot01(pair, s["r23"][...]) * 0.125
        return row_pairs(t2, 0, row0, 2)

    low = to_level2([tile[8 * c : 8 * c + 8] for c in range(4)])
    for c in range(2):
        x2k[6 + c, 2] = low[8 * c + 2 : 8 * c + 6]
    base = to_level3(low[0:8] + low[8:16], 2)

    def ring_x(group, ref, tile_ref, value):
        tile_ref[...] = value
        ref[me_x] = value
        return [copy(group, tile_ref, ref.at[me_x], d, 0) for d in range(1, N)]

    def window_x(group, ref):
        return [
            copy(group, ref.at[6:8, 2], ref.at[6 - 2 * d : 8 - 2 * d, 2], d, 0) for d in (1, -1, 2, -2, 3, -3)
        ]

    def slab(ref):
        lane = iota((2, 128), 1)
        out_parts = []
        for k in range(4):
            v = ref[12 + k]
            for h in (2, 1, 0):
                v = jnp.where(lane % 4 == h, ref[4 * h + k], v)
            out_parts.append(v)
        return out_parts

    def ring_y(group, ref, slab_ref, parts):
        for k in range(4):
            slab_ref[k] = parts[k]
            ref[k, me_y] = parts[k]
        return [copy(group, slab_ref, ref.at[:, me_y], 0, d) for d in range(1, N)]

    def window_y(group, ref):
        return [copy(group, ref.at[:, 2], ref.at[:, 2 - d], 0, d) for d in (1, -1, 2, -2)]

    def window(ref, dest):
        for x in range(14):
            dest[x] = ref[x].reshape(20, 128)[2:18]

    in_k1 = halo1("h1k", k1, 7)
    in_ka = ring_x("ka", s["ka"], s["kt"], base)
    in_k2a = window_x("k2a", x2k)
    arrive(in_k0)
    merge0("hk", k0, 3)
    make_ops(k0, ops0, 1.0, 14, 13)
    arrive(in_va)
    arrive(in_src)
    merge0("hv", s["va"], 3)
    merge0("hs", s["src"], 2)
    va, vb, vc, vd, ve, src, g0 = [s[name] for name in ("va", "vb", "vc", "vd", "ve", "src", "g0")]

    def force(x):
        g0[x] = RATE * va[x] + src[x]

    each(1, 13, 12, force)
    sweep(va, vb, g0, ops0, 1, 13, 12)
    sweep(vb, vc, g0, ops0, 2, 12, 10)

    def down0(c):
        put0(c, res_at(vc, g0, ops0, 2 * c + 3) + res_at(vc, g0, ops0, 2 * c + 4))

    each(0, 4, 4, down0)
    tile = take0()
    f1 = s["f1"]
    for c in range(4):
        f1[7 + c, 0:8] = tile[8 * c : 8 * c + 8]
    in_f1 = halo1("h1f", f1, 6)

    arrive(in_ka)
    in_kb = ring_y("kb", s["kb"], s["ks"], slab(s["ka"]))
    arrive(in_k2a)
    in_k2b = window_y("k2b", x2k)
    stay = pltpu.make_async_copy(vc.at[tile0], vd.at[tile0], s["load"].at[0])
    stay.start()
    in_vd = halo0("hd", vc, vd, 2, 1)

    arrive(in_k1)
    make_ops(k1, ops1, 0.25, 18, 17)
    arrive(in_f1)

    v1a, v1b = s["v1a"], s["v1b"]

    def start1(x):
        v1a[x] = ops1[3][x] * f1[x]

    each(1, 17, 16, start1)
    sweep(v1a, v1b, f1, ops1, 2, 16, 14)
    low = to_level2([res_at(v1b, f1, ops1, x) for x in range(3, 15)])
    f2l = s["f2l"]
    f2 = s["f2"]
    for c in range(6):
        f2l[c] = low[8 * c : 8 * c + 8]
    for c in range(2):
        x2f[6 + c, 2] = low[8 * c + 18 : 8 * c + 22]

    arrive(in_k2b)
    window(x2k, k2)
    make_ops(k2, ops2, 0.0625, 14, 13)
    v2a, v2b = s["v2a"], s["v2b"]
    near = [[ref[x, 4:12] for x in range(4, 10)] for ref in ops2]
    fl = [f2l[c] for c in range(6)]
    vl = [near[3][c] * fl[c] for c in range(6)]

    def res_near(v, c):
        return residual(v[c], v[c - 1], v[c + 1], fl[c], near[0][c], near[0][c - 1], near[1][c], near[2][c])

    ul = [None] + [vl[c] + near[3][c] * res_near(vl, c) for c in range(1, 5)]
    base = to_level3(res_near(ul + [None], 2) + res_near(ul + [None], 3), 2)
    in_fa = ring_x("fa", s["fa"], s["ft"], base)
    in_f2a = window_x("f2a", x2f)

    arrive(in_kb)
    kap3 = [s["kb"][k].reshape(32, 128) for k in range(4)]
    kap4 = low_restrict(kap3, 1)
    kap5 = low_restrict(kap4, 2)
    kap6 = low_restrict(kap5, 4)[0]
    for level, kap, spread in ((3, kap3, 1), (4, kap4, 2), (5, kap5, 4)):
        made = low_couple(kap, spread, 1.0 / 4.0**level)
        for number in range(4):
            for k in range(len(kap)):
                s[f"low{level}"][number, k] = made[number][k]

    krow = dot01(pack_six(kap6), s["sel"][...])[0:1]
    q, p = iota((32, 128), 0), iota((32, 128), 1)
    kcol = jnp.sum(jnp.where(q == p, krow, 0.0), axis=1, keepdims=True)
    dy, dz, same_x = (q // 8 - p // 8 + 4) % 4, ((q % 8) // 2 - (p % 8) // 2 + 4) % 4, q % 2 == p % 2
    links = jnp.where(same_x & (dz == 0) & (dy % 2 == 1), 1.0, 0.0) + jnp.where(same_x & (dy == 0) & (dz % 2 == 1), 1.0, 0.0)
    links = links + jnp.where((dz == 0) & (dy == 0) & (q % 2 != p % 2), 2.0, 0.0)
    links = jnp.where(p < 32, links, 0.0)
    off = (0.5 / 4096.0) * links * (krow + kcol)
    diag = RATE + jnp.sum(off, axis=1, keepdims=True)
    m_ref = s["m6"]
    m_ref[...] = jnp.where(q == p, diag, jnp.where(p == q + 32, 1.0, -off))

    def eliminate(k, carry):
        m = m_ref[...]
        pivot_row = m_ref[pl.ds(k, 1), :]
        column = jnp.sum(jnp.where(p == k, m, 0.0), axis=1, keepdims=True)
        pivot = jnp.sum(jnp.where(iota((1, 128), 1) == k, pivot_row, 0.0), axis=1, keepdims=True)
        scaled = pivot_row / pivot
        m_ref[...] = jnp.where(q == k, scaled, m - column * scaled)
        return carry

    lax.fori_loop(0, 16, eliminate, 0)

    arrive(in_fa)
    in_fb = ring_y("fb", s["fb"], s["fs"], slab(s["fa"]))
    arrive(in_f2a)
    in_f2b = window_y("f2b", x2f)
    lax.fori_loop(16, 32, eliminate, 0)
    inverse = roll(m_ref[...], -32, 1)
    inverse = jnp.concatenate([jnp.where(p < 32, inverse, 0.0), jnp.zeros((96, 128), F32)], axis=0)
    inverse = dot01(inverse, s["spr"][...])
    hi = inverse.astype(BF16)
    rest = inverse - hi.astype(F32)
    mid = rest.astype(BF16)
    pieces = (hi, mid, (rest - mid.astype(F32)).astype(BF16))
    a, b, c = [jnp.dot(s["sel"][...], piece, preferred_element_type=F32) for piece in pieces]
    s["inv"][...] = a + (b + c)

    def low_ops(level, count):
        return [[s[f"low{level}"][number, k] for k in range(count)] for number in range(4)]

    arrive(in_fb)
    g3 = [s["fb"][k].reshape(32, 128) for k in range(4)]
    o3, o4, o5 = low_ops(3, 4), low_ops(4, 2), low_ops(5, 1)

    def down(g, o, spread):
        v = low_sweep([w * f for w, f in zip(o[3], g)], g, o, spread)
        return v, low_restrict(low_res(v, g, o, spread), spread)

    v3, g4 = down(g3, o3, 1)
    v4, g5 = down(g4, o4, 2)
    v5, g6 = down(g5, o5, 4)
    x6 = jnp.dot(pack_six(g6[0]), s["inv"][...], precision=lax.Precision.HIGHEST, preferred_element_type=F32)
    x6 = jnp.concatenate([x6[:, 128 * k : 128 * k + 128] for k in range(4)], axis=0)

    def up(v, e, g, o, spread):
        v = [u + e[k * len(e) // len(v)] for k, u in enumerate(v)]
        return low_sweep(low_sweep(v, g, o, spread), g, o, spread)

    v5 = up(v5, [x6], g5, o5, 4)
    v4 = up(v4, v5, g4, o4, 2)
    v3 = up(v3, v4, g3, o3, 1)

    e3, e2, e1 = s["e3"], s["e2"], s["e1"]
    turn = lax.rem(2 * N - 2 * me_y + 3, 2 * N)
    for k in range(4):
        e3[k] = pltpu.roll(v3[k], turn, 0)[0:8]
    picks = []
    lane8 = iota((8, 128), 1)
    for d in range(-2, 3):
        x = lax.rem(me_x + (d + N), N)
        picks.append(jnp.where(lane8 % 4 == x // 4, e3[lax.rem(x, 4)], 0.0))
    spread3 = dot01(jnp.concatenate(picks, axis=0), s["p32"][...])
    for c in range(5):
        e2[c + 1, pl.ds(0, 8, stride=2), :] = spread3[8 * c : 8 * c + 8]
        e2[c + 1, pl.ds(1, 8, stride=2), :] = spread3[8 * c : 8 * c + 8]

    arrive(in_f2b)
    window(x2f, f2)
    for x in range(1, 13):
        v2a[x] = ops2[3][x] * f2[x]
    sweep(v2a, v2b, f2, ops2, 2, 12, 10)
    for x in range(2, 12):
        v2b[x] = v2b[x] + e2[x // 2]
    sweep(v2b, v2a, f2, ops2, 3, 11, 8)
    sweep(v2a, v2b, f2, ops2, 4, 10, 6)

    spread2 = dot01(jnp.concatenate([v2b[x] for x in range(4, 10)], axis=0), s["p21"][...])
    for c in range(6):
        e1[c, pl.ds(0, 16, stride=2), :] = spread2[16 * c : 16 * c + 16]
        e1[c, pl.ds(1, 16, stride=2), :] = spread2[16 * c : 16 * c + 16]
    for x in range(4, 14):
        c = (x + 5) // 2 - 4
        v1b[x] = v1b[x] + jnp.concatenate([e1[c, 12:28], e1[c, 4:12]], axis=0)
    sweep(v1b, v1a, f1, ops1, 5, 13, 8)
    sweep(v1a, v1b, f1, ops1, 6, 12, 6)

    e0 = s["e0"]
    for c in range(6):
        e0[c, pl.ds(0, 24, stride=2), :] = v1b[6 + c]
        e0[c, pl.ds(1, 24, stride=2), :] = v1b[6 + c]
    row8 = iota((8, 128), 0)
    parts = []
    for c in range(6):
        parts += [e0[c, 0:16], jnp.where(row8 < 4, e0[c, 16:24], e0[c, 40:48])]
    spread1 = dot01(jnp.concatenate(parts, axis=0), s["p10"][...])
    stay.wait()
    arrive(in_vd)
    merge0("hd", vd, 2)
    for x in range(1, 13):
        c = (x + 11) // 2 - 6
        ve[x] = vd[x] + spread1[24 * c : 24 * c + 24]
    sweep(ve, vb, g0, ops0, 2, 12, 10)

    def last(x):
        v = vb[x + 3] + ops0[3][x + 3] * res_at(vb, g0, ops0, x + 3)
        out[x] = v[0:16]

    each(0, 8, 8, last)
    for c in sent:
        c.wait_send()


def scratch_list():
    def vmem(*shape, kind=F32):
        return pltpu.VMEM(shape, kind)

    made = [("mat", vmem(8, 16, 256, kind=jnp.int32))]
    for name in ("k0", "va", "vb", "vc", "vd", "ve", "src", "g0", "cx0", "cy0", "cz0", "w0"):
        made.append((name, vmem(14, 24, 256)))
    for name in ("k1", "f1", "v1a", "v1b", "cx1", "cy1", "cz1", "w1"):
        made.append((name, vmem(18, 24, 128)))
    for name in ("k2", "f2", "v2a", "v2b", "cx2", "cy2", "cz2", "w2"):
        made.append((name, vmem(14, 16, 128)))
    for name in ("x2k", "x2f"):
        made.append((name, vmem(14, 5, 4, 128)))
    for name in ("hk", "hv", "hs", "hd"):
        made.append((name + "_e", vmem(8, 8, 256)))
        made.append((name + "_b", vmem(14, 8, 256)))
    made.append(("f2l", vmem(6, 8, 128)))
    for name in ("ka", "fa"):
        made.append((name, vmem(N, 2, 128)))
    for name in ("kb", "fb"):
        made.append((name, vmem(4, N, 2, 128)))
    for name in ("kt", "ft"):
        made.append((name, vmem(2, 128)))
    for name in ("ks", "fs"):
        made.append((name, vmem(4, 2, 128)))
    made.append(("t0", vmem(4, 2, 16, 128)))
    made.append(("t1", vmem(6, 24, 128)))
    made.append(("t2", vmem(1, 8, 128)))
    made.append(("e3", vmem(4, 8, 128)))
    made.append(("e2", vmem(7, 16, 128)))
    made.append(("e1", vmem(6, 32, 128)))
    made.append(("e0", vmem(6, 48, 128)))
    made.append(("low3", vmem(4, 4, 32, 128)))
    made.append(("low4", vmem(4, 2, 32, 128)))
    made.append(("low5", vmem(4, 1, 32, 128)))
    made.append(("m6", vmem(32, 128)))
    made.append(("inv", vmem(128, 512)))
    for name, shape in (("r01", (256, 128)), ("r12", (128, 128)), ("r23", (128, 128)), ("p32", (128, 128)), ("p21", (128, 128)), ("p10", (128, 256)), ("sel", (128, 128)), ("spr", (128, 512))):
        made.append((name, vmem(*shape, kind=BF16)))
    made.append(("load", pltpu.SemaphoreType.DMA((3,))))
    groups = {"hk": 8, "hv": 8, "hs": 8, "hd": 8, "h1k": 14, "h1f": 14, "ka": 15, "kb": 15, "fa": 15, "fb": 15, "k2a": 6, "f2a": 6, "k2b": 4, "f2b": 4}
    for name, count in groups.items():
        made.append((name + "_s", pltpu.SemaphoreType.DMA((count,))))
        made.append((name + "_r", pltpu.SemaphoreType.DMA((count,))))
    return made


SCRATCH = scratch_list()


def shards(concentration, source, material):
    return pl.pallas_call(
        kernel,
        out_shape=jax.ShapeDtypeStruct(concentration.shape, F32),
        in_specs=[pl.BlockSpec(memory_space=pltpu.HBM)] * 3,
        out_specs=pl.BlockSpec(memory_space=pltpu.VMEM),
        scratch_shapes=[shape for _, shape in SCRATCH],
        compiler_params=pltpu.CompilerParams(collective_id=0, has_side_effects=True, vmem_limit_bytes=56360960),
        cost_estimate=pl.CostEstimate(flops=20_000_000, bytes_accessed=1_000_000, transcendentals=0),
        name="vcycle",
    )(concentration, source, material)


def solution(mesh):
    placed = P("tx", "ty", None)
    return jax.shard_map(shards, mesh=mesh, in_specs=(placed,) * 3, out_specs=placed, check_vma=False)
```

```python
import jax
import jax.numpy as jnp
from jax import lax
from jax.experimental import pallas as pl
from jax.experimental.pallas import tpu as pltpu
from jax.sharding import PartitionSpec as P

MESH = pl.DeviceIdType.MESH
F32 = jnp.float32
BF16 = jnp.bfloat16
RATE = 0.001
RELAX = 0.8
TABLE = (0.15, 0.3, 0.5, 0.8, 1.2, 2.0, 3.2, 5.0)
N = 16


def iota(shape, axis):
    return lax.broadcasted_iota(jnp.int32, shape, axis)


def roll(v, shift, axis):
    return pltpu.roll(v, shift % v.shape[axis], axis)


def dot01(v, m):
    hi = v.astype(BF16)
    low = (v - hi.astype(F32)).astype(BF16)
    rows = len(v)
    if rows % 16 == 0:
        both = jnp.dot(jnp.concatenate([hi, low], axis=0), m, preferred_element_type=F32)
        return both[:rows] + both[rows:]
    return jnp.dot(hi, m, preferred_element_type=F32) + jnp.dot(low, m, preferred_element_type=F32)


def each(low, high, unroll, body):
    count = high - low
    whole = count // unroll
    if whole > 1:

        def step(i, carry):
            for k in range(unroll):
                body(low + i * unroll + k)
            return carry

        lax.fori_loop(0, whole, step, 0)
        rest = low + whole * unroll
    else:
        rest = low
    for x in range(rest, high):
        body(x)


def make_ops(kappa, ops, scale, layers, unroll):
    cx, cy, cz, w = ops
    half = 0.5 * scale

    def couple(x):
        k = kappa[x]
        cx[x] = half * (k + kappa[x + 1])
        cy[x] = half * (k + roll(k, -1, 0))
        cz[x] = half * (k + roll(k, -1, 1))

    def weigh(x):
        a, b = cy[x], cz[x]
        diag = (RATE + cx[x] + cx[x - 1]) + (a + roll(a, 1, 0)) + (b + roll(b, 1, 1))
        w[x] = RELAX / diag

    each(0, layers - 1, unroll, couple)
    each(1, layers - 1, unroll, weigh)


def residual(v, below, above, g, cx, cxm, cy, cz):
    fy = cy * (roll(v, -1, 0) - v)
    fz = cz * (roll(v, -1, 1) - v)
    r = (g - RATE * v) + (cx * (above - v) - cxm * (v - below))
    return r + (fy - roll(fy, 1, 0)) + (fz - roll(fz, 1, 1))


def res_at(v, g, ops, x):
    cx, cy, cz, _ = ops
    return residual(v[x], v[x - 1], v[x + 1], g[x], cx[x], cx[x - 1], cy[x], cz[x])


def sweep(v, out, g, ops, low, high, unroll):
    def body(x):
        out[x] = v[x] + ops[3][x] * res_at(v, g, ops, x)

    each(low, high, unroll, body)


def x_hi_next(v):
    lane = iota(v.shape, 1)
    return jnp.where(lane % 4 == 3, roll(v, 3, 1), roll(v, -1, 1))


def x_hi_prev(v):
    lane = iota(v.shape, 1)
    return jnp.where(lane % 4 == 0, roll(v, -3, 1), roll(v, 1, 1))


def low_couple(kappa, s, scale):
    half = 0.5 * scale
    nxt = kappa[1:] + [x_hi_next(kappa[0])]
    cx = [half * (k + n) for k, n in zip(kappa, nxt)]
    cxm = [x_hi_prev(cx[-1])] + cx[:-1]
    made = []
    for k, a, am in zip(kappa, cx, cxm):
        b, c = half * (k + roll(k, -s, 0)), half * (k + roll(k, -4 * s, 1))
        bm, cm = roll(b, s, 0), roll(c, 4 * s, 1)
        diag = (RATE + a + am) + (b + bm) + (c + cm)
        w = RELAX / diag
        made.append([w * a, w * am, w * b, w * bm, w * c, w * cm, w, diag * (1.0 / RELAX)])
    return made


def low_step(v, wg, ops, s):
    nxt = v[1:] + [x_hi_next(v[0])]
    prv = [x_hi_prev(v[-1])] + v[:-1]
    out = []
    for u, n, p, f, o in zip(v, nxt, prv, wg, ops):
        along_x = o[0] * n + o[1] * p
        along_y = o[2] * roll(u, -s, 0) + o[3] * roll(u, s, 0)
        along_z = o[4] * roll(u, -4 * s, 1) + o[5] * roll(u, 4 * s, 1)
        out.append((along_x + along_y) + (along_z + (f - RELAX * u)))
    return out


def low_sweep(v, wg, ops, s):
    return [u + d for u, d in zip(v, low_step(v, wg, ops, s))]


def low_restrict(v, s):
    if len(v) > 1:
        v = [v[2 * k] + v[2 * k + 1] for k in range(len(v) // 2)]
    else:
        u = v[0]
        lane = iota(u.shape, 1)
        v = [u + jnp.where(lane % 2 == 0, roll(u, -1, 1), roll(u, 1, 1))]
    out = []
    for u in v:
        row, lane = iota(u.shape, 0), iota(u.shape, 1)
        u = u + jnp.where((row // s) % 2 == 0, roll(u, -s, 0), roll(u, s, 0))
        u = u + jnp.where((lane // (4 * s)) % 2 == 0, roll(u, -4 * s, 1), roll(u, 4 * s, 1))
        out.append(u * 0.125)
    return out


def pack_six(v):
    lane = iota((8, 128), 1)
    y = (lane % 32) // 4
    out = v[24:32]
    for k in (2, 1, 0):
        out = jnp.where(y == k, v[8 * k : 8 * k + 8], out)
    return out


def kernel(conc, source, material, out, *scratch):
    names = [name for name, _ in SCRATCH]
    s = dict(zip(names, scratch))
    ops0, ops1, ops2 = [[s[f"{name}{level}"] for name in ("cx", "cy", "cz", "w")] for level in (0, 1, 2)]
    me_x, me_y = lax.axis_index("tx"), lax.axis_index("ty")

    def device(dx, dy):
        return (lax.rem(me_x + (dx + N), N), lax.rem(me_y + (dy + N), N))

    counter = {}

    def copy(group, src, dst, dx, dy):
        k = counter.get(group, 0)
        counter[group] = k + 1
        c = pltpu.make_async_remote_copy(
            src, dst, s[group + "_s"].at[k], s[group + "_r"].at[k], device_id=device(dx, dy), device_id_type=MESH
        )
        c.start()
        return c

    sent = []

    def arrive(copies):
        for c in copies:
            c.wait_recv()
        sent.extend(copies)

    def drain():
        for c in sent:
            c.wait_send()
        sent.clear()

    tile0 = (slice(3, 11), slice(0, 16))
    loads = [
        pltpu.make_async_copy(material, s["mat"], s["load"].at[0]),
        pltpu.make_async_copy(conc, s["va"].at[3:11, 0:16], s["load"].at[1]),
        pltpu.make_async_copy(source, s["src"].at[3:11, 0:16], s["load"].at[2]),
    ]
    for c in loads:
        c.start()
    barrier = pltpu.get_barrier_semaphore()
    peers = [(d, 0) for d in range(1, N)] + [(0, d) for d in range(1, N)]
    peers += [(a, b) for a in (-2, -1, 1, 2) for b in (-1, 1)]
    peers.sort(key=lambda p: -min(p[0] % N, -p[0] % N) - min(p[1] % N, -p[1] % N))
    for p in peers:
        pl.semaphore_signal(barrier, inc=1, device_id=device(*p), device_id_type=MESH)

    loads[0].wait()
    k0 = s["k0"]

    def lookup(x):
        m = s["mat"][x]
        result = jnp.zeros(m.shape, F32)
        for slot, value in enumerate(TABLE):
            result = jnp.where(m == slot, F32(value), result)
        k0[x + 3, 0:16] = result

    each(0, 8, 8, lookup)
    loads[1].wait()
    loads[2].wait()
    def halo0(group, ref, dest, w, c):
        edge, below = s[group + "_e"], s[group + "_b"]
        copies = []
        for dx, dy in ((1, 0), (-1, 0), (0, 1), (0, -1), (1, 1), (1, -1), (-1, 1), (-1, -1)):
            n = c if dy else w
            x0, x1 = {0: (3, 11), -1: (3, 3 + n), 1: (11 - n, 11)}[dx]
            y0, y1 = x0 - 8 * dx, x1 - 8 * dx
            if dy == 0:
                copies.append(copy(group, ref.at[x0:x1, 0:16], dest.at[y0:y1, 0:16], dx, dy))
            elif dy < 0:
                copies.append(copy(group, ref.at[x0:x1, 0:w], dest.at[y0:y1, 16 : 16 + w], dx, dy))
            else:
                copies.append(copy(group, edge.at[x0 - 3 : x1 - 3, 0:w], below.at[y0:y1, 0:w], dx, dy))
        return copies

    def edges0(group, ref, w):
        for x in range(8):
            s[group + "_e"][x] = roll(ref[x + 3, 8:16], w, 0)

    edges0("hk", k0, 3)
    edges0("hv", s["va"], 3)
    edges0("hs", s["src"], 2)
    pl.semaphore_wait(barrier, len(peers))

    def merge0(group, dest, w):
        below = s[group + "_b"]
        row = iota((8, 256), 0)
        for x in range(14):
            dest[x, 16:24] = jnp.where(row < 4, dest[x, 16:24], roll(below[x], -w, 0))

    in_k0 = halo0("hk", k0, k0, 3, 2)
    in_va = halo0("hv", s["va"], s["va"], 3, 2)
    in_src = halo0("hs", s["src"], s["src"], 2, 1)

    def matrix(name, rule):
        shape = s[name].shape
        s[name][...] = jnp.where(rule(iota(shape, 0), iota(shape, 1)), 1.0, 0.0).astype(BF16)

    matrix("r01", lambda i, j: i // 2 == j)
    matrix("r12", lambda i, j: i // 2 == j % 64)
    matrix("r23", lambda i, j: i // 2 == j // 4)
    matrix("p32", lambda i, j: i // 4 == (j % 64) // 2)
    matrix("p21", lambda i, j: i == j // 2)
    matrix("p10", lambda i, j: i == j // 2)
    matrix("sel", lambda i, j: ((i % 32) // 4 < 4) & (i % 2 == 0) & (j == ((i % 32) // 4) * 8 + (i // 32) * 2 + (i % 4) // 2))
    matrix("spr", lambda i, j: i == (j // 128) * 8 + ((j % 128) // 32) * 2 + (j % 4) // 2)

    t0, t1, t2 = s["t0"], s["t1"], s["t2"]

    def put0(c, pair):
        t0[c, 0] = pair[:16, :128]
        t0[c, 1] = pair[:16, 128:]

    def take0():
        rows = []
        for c in range(4):
            halves = [t0[c, h, pl.ds(0, 8, stride=2), :] + t0[c, h, pl.ds(1, 8, stride=2), :] for h in range(2)]
            rows.append(jnp.concatenate(halves, axis=1))
        return dot01(jnp.concatenate(rows, axis=0), s["r01"][...]) * 0.125

    def row_pairs(ref, k, start, count):
        return ref[k, pl.ds(start, count, stride=2), :] + ref[k, pl.ds(start + 1, count, stride=2), :]

    k1, k2, x2k, x2f = s["k1"], s["k2"], s["x2k"], s["x2f"]
    for c in range(4):
        put0(c, k0[3 + 2 * c, 0:16] + k0[4 + 2 * c, 0:16])
    tile = take0()
    for c in range(4):
        k1[7 + c, 0:8] = tile[8 * c : 8 * c + 8]

    def halo1(group, ref, w):
        copies = []
        for dx, dy in ((2, 1), (2, -1), (-2, 1), (-2, -1), (1, 1), (1, -1), (-1, 1), (-1, -1), (0, 1), (0, -1), (2, 0), (-2, 0), (1, 0), (-1, 0)):
            nx = {0: 4, 1: 4, 2: w - 4 if dy == 0 else w - 5}[abs(dx)]
            ny = 8 if dy == 0 else {0: w, 1: w - 1, 2: w - 5}[abs(dx)]
            xs = slice(11 - nx, 11) if dx > 0 else slice(7, 7 + nx)
            xd = slice(xs.start - 4 * dx, xs.stop - 4 * dx)
            ys = slice(0, 8) if dy > 0 else slice(0, ny)
            yd = slice(16, 24) if dy > 0 else slice(-8 * dy, ny - 8 * dy)
            copies.append(copy(group, ref.at[xs, ys], ref.at[xd, yd], dx, dy))
        return copies

    def to_level2(get):
        parts = []
        for c in range(len(get) // 2):
            pair = get[2 * c] + get[2 * c + 1]
            if len(pair) == 8:
                t1[c, 4:12] = pair
            else:
                t1[c] = roll(pair, 4, 0)
        for c in range(len(get) // 2):
            parts.append(row_pairs(t1, c, 0, 8))
        return dot01(jnp.concatenate(parts, axis=0), s["r12"][...]) * 0.125

    def to_level3(pair, row0):
        t2[0] = dot01(pair, s["r23"][...]) * 0.125
        return row_pairs(t2, 0, row0, 2)

    low = to_level2([tile[8 * c : 8 * c + 8] for c in range(4)])
    for c in range(2):
        x2k[6 + c, 2] = low[8 * c + 2 : 8 * c + 6]
    base = to_level3(low[0:8] + low[8:16], 2)

    def ring_x(group, ref, tile_ref, value):
        tile_ref[...] = value
        ref[me_x] = value
        return [copy(group, tile_ref, ref.at[me_x], d, 0) for d in range(1, N)]

    def window_x(group, ref):
        return [
            copy(group, ref.at[6:8, 2], ref.at[6 - 2 * d : 8 - 2 * d, 2], d, 0) for d in (1, -1, 2, -2, 3, -3)
        ]

    def slab(ref):
        lane = iota((2, 128), 1)
        out_parts = []
        for k in range(4):
            v = ref[12 + k]
            for h in (2, 1, 0):
                v = jnp.where(lane % 4 == h, ref[4 * h + k], v)
            out_parts.append(v)
        return out_parts

    def ring_y(group, ref, slab_ref, parts):
        for k in range(4):
            slab_ref[k] = parts[k]
            ref[k, me_y] = parts[k]
        return [copy(group, slab_ref, ref.at[:, me_y], 0, d) for d in range(1, N)]

    def window_y(group, ref):
        return [copy(group, ref.at[:, 2], ref.at[:, 2 - d], 0, d) for d in (1, -1, 2, -2)]

    def window(ref, dest):
        for x in range(14):
            dest[x] = ref[x].reshape(20, 128)[2:18]

    in_k1 = halo1("h1k", k1, 7)
    in_ka = ring_x("ka", s["ka"], s["kt"], base)
    in_k2a = window_x("k2a", x2k)
    arrive(in_k0)
    merge0("hk", k0, 3)
    make_ops(k0, ops0, 1.0, 14, 13)
    arrive(in_va)
    arrive(in_src)
    merge0("hv", s["va"], 3)
    merge0("hs", s["src"], 2)
    va, vb, vc, vd, ve, src, g0 = [s[name] for name in ("va", "vb", "vc", "vd", "ve", "src", "g0")]

    def force(x):
        g0[x] = RATE * va[x] + src[x]

    each(1, 13, 12, force)
    sweep(va, vb, g0, ops0, 1, 13, 12)
    sweep(vb, vc, g0, ops0, 2, 12, 10)

    def down0(c):
        put0(c, res_at(vc, g0, ops0, 2 * c + 3) + res_at(vc, g0, ops0, 2 * c + 4))

    each(0, 4, 4, down0)
    tile = take0()
    f1 = s["f1"]
    for c in range(4):
        f1[7 + c, 0:8] = tile[8 * c : 8 * c + 8]
    in_f1 = halo1("h1f", f1, 6)

    arrive(in_k2a)
    in_k2b = window_y("k2b", x2k)
    arrive(in_ka)
    in_kb = ring_y("kb", s["kb"], s["ks"], slab(s["ka"]))
    stay = pltpu.make_async_copy(vc.at[tile0], vd.at[tile0], s["load"].at[0])
    stay.start()
    edges0("hd", vc, 2)
    in_vd = halo0("hd", vc, vd, 2, 1)

    arrive(in_k1)
    make_ops(k1, ops1, 0.25, 18, 17)
    arrive(in_f1)

    v1a, v1b = s["v1a"], s["v1b"]

    def start1(x):
        v1a[x] = ops1[3][x] * f1[x]

    each(1, 17, 16, start1)
    sweep(v1a, v1b, f1, ops1, 2, 16, 14)
    low = to_level2([res_at(v1b, f1, ops1, x) for x in range(3, 15)])
    f2l = s["f2l"]
    f2 = s["f2"]
    for c in range(6):
        f2l[c] = low[8 * c : 8 * c + 8]
    for c in range(2):
        x2f[6 + c, 2] = low[8 * c + 18 : 8 * c + 22]

    arrive(in_k2b)
    window(x2k, k2)
    make_ops(k2, ops2, 0.0625, 14, 13)
    v2a, v2b = s["v2a"], s["v2b"]
    near = [[ref[x, 4:12] for x in range(4, 10)] for ref in ops2]
    fl = [f2l[c] for c in range(6)]
    vl = [near[3][c] * fl[c] for c in range(6)]

    def res_near(v, c):
        return residual(v[c], v[c - 1], v[c + 1], fl[c], near[0][c], near[0][c - 1], near[1][c], near[2][c])

    ul = [None] + [vl[c] + near[3][c] * res_near(vl, c) for c in range(1, 5)]
    base = to_level3(res_near(ul + [None], 2) + res_near(ul + [None], 3), 2)
    in_fa = ring_x("fa", s["fa"], s["ft"], base)
    in_f2a = window_x("f2a", x2f)

    arrive(in_kb)
    kap3 = [s["kb"][k].reshape(32, 128) for k in range(4)]
    kap4 = low_restrict(kap3, 1)
    kap5 = low_restrict(kap4, 2)
    kap6 = low_restrict(kap5, 4)[0]
    for level, kap, spread in ((3, kap3, 1), (4, kap4, 2), (5, kap5, 4)):
        made = low_couple(kap, spread, 1.0 / 4.0**level)
        for k in range(len(kap)):
            for number in range(8):
                s[f"low{level}"][k, number] = made[k][number]

    krow = dot01(pack_six(kap6), s["sel"][...])[0:1]
    q, p = iota((32, 128), 0), iota((32, 128), 1)
    kcol = jnp.sum(jnp.where(q == p, krow, 0.0), axis=1, keepdims=True)
    dy, dz, same_x = (q // 8 - p // 8 + 4) % 4, ((q % 8) // 2 - (p % 8) // 2 + 4) % 4, q % 2 == p % 2
    links = jnp.where(same_x & (dz == 0) & (dy % 2 == 1), 1.0, 0.0) + jnp.where(same_x & (dy == 0) & (dz % 2 == 1), 1.0, 0.0)
    links = links + jnp.where((dz == 0) & (dy == 0) & (q % 2 != p % 2), 2.0, 0.0)
    links = jnp.where(p < 32, links, 0.0)
    off = (0.5 / 4096.0) * links * (krow + kcol)
    diag = RATE + jnp.sum(off, axis=1, keepdims=True)
    m_ref = s["m6"]
    m_ref[...] = jnp.where(q == p, diag, jnp.where(p == q + 32, 1.0, -off))

    def eliminate(k, carry):
        m = m_ref[...]
        pivot_row = m_ref[pl.ds(k, 1), :]
        column = jnp.sum(jnp.where(p == k, m, 0.0), axis=1, keepdims=True)
        pivot = jnp.sum(jnp.where(iota((1, 128), 1) == k, pivot_row, 0.0), axis=1, keepdims=True)
        scaled = pivot_row / pivot
        m_ref[...] = jnp.where(q == k, scaled, m - column * scaled)
        return carry

    lax.fori_loop(0, 16, eliminate, 0)

    arrive(in_fa)
    in_fb = ring_y("fb", s["fb"], s["fs"], slab(s["fa"]))
    arrive(in_f2a)
    in_f2b = window_y("f2b", x2f)
    lax.fori_loop(16, 32, eliminate, 0)
    inverse = roll(m_ref[...], -32, 1)
    inverse = jnp.concatenate([jnp.where(p < 32, inverse, 0.0), jnp.zeros((96, 128), F32)], axis=0)
    inverse = dot01(inverse, s["spr"][...])
    hi = inverse.astype(BF16)
    rest = inverse - hi.astype(F32)
    mid = rest.astype(BF16)
    pieces = (hi, mid, (rest - mid.astype(F32)).astype(BF16))
    a, b, c = [jnp.dot(s["sel"][...], piece, preferred_element_type=F32) for piece in pieces]
    inverse = a + (b + c)
    hi = inverse.astype(BF16)
    s["inv"][0] = hi
    s["inv"][1] = (inverse - hi.astype(F32)).astype(BF16)

    drain()

    def low_ops(level, count):
        return [[s[f"low{level}"][k, number] for number in range(8)] for k in range(count)]

    arrive(in_fb)
    g3 = [s["fb"][k].reshape(32, 128) for k in range(4)]
    o3, o4, o5 = low_ops(3, 4), low_ops(4, 2), low_ops(5, 1)

    def down(g, o, spread):
        wg = [q[6] * f for q, f in zip(o, g)]
        v = low_sweep(wg, wg, o, spread)
        step = low_step(v, wg, o, spread)
        return v, wg, low_restrict([q[7] * d for q, d in zip(o, step)], spread)

    v3, wg3, g4 = down(g3, o3, 1)
    v4, wg4, g5 = down(g4, o4, 2)
    v5, wg5, g6 = down(g5, o5, 4)
    x6 = pack_six(g6[0])
    hi = x6.astype(BF16).astype(F32)
    both = jnp.concatenate([hi, x6 - hi], axis=0).astype(BF16)
    large = jnp.dot(both, s["inv"][0], preferred_element_type=F32)
    x6 = large[:8] + (large[8:] + jnp.dot(both, s["inv"][1], preferred_element_type=F32)[:8])
    x6 = jnp.concatenate([x6[:, 128 * k : 128 * k + 128] for k in range(4)], axis=0)

    def up(v, e, wg, o, spread):
        v = [u + e[k * len(e) // len(v)] for k, u in enumerate(v)]
        return low_sweep(low_sweep(v, wg, o, spread), wg, o, spread)

    v5 = up(v5, [x6], wg5, o5, 4)
    v4 = up(v4, v5, wg4, o4, 2)
    v3 = up(v3, v4, wg3, o3, 1)

    e3, e2, e1 = s["e3"], s["e2"], s["e1"]
    turn = lax.rem(2 * N - 2 * me_y + 3, 2 * N)
    for k in range(4):
        e3[k] = pltpu.roll(v3[k], turn, 0)[0:8]
    picks = []
    lane8 = iota((8, 128), 1)
    for d in range(-2, 3):
        x = lax.rem(me_x + (d + N), N)
        picks.append(jnp.where(lane8 % 4 == x // 4, e3[lax.rem(x, 4)], 0.0))
    spread3 = dot01(jnp.concatenate(picks, axis=0), s["p32"][...])
    for c in range(5):
        e2[c + 1, pl.ds(0, 8, stride=2), :] = spread3[8 * c : 8 * c + 8]
        e2[c + 1, pl.ds(1, 8, stride=2), :] = spread3[8 * c : 8 * c + 8]

    arrive(in_f2b)
    window(x2f, f2)
    for x in range(1, 13):
        v2a[x] = ops2[3][x] * f2[x]
    sweep(v2a, v2b, f2, ops2, 2, 12, 10)
    for x in range(2, 12):
        v2b[x] = v2b[x] + e2[x // 2]
    sweep(v2b, v2a, f2, ops2, 3, 11, 8)
    sweep(v2a, v2b, f2, ops2, 4, 10, 6)

    spread2 = dot01(jnp.concatenate([v2b[x] for x in range(4, 10)], axis=0), s["p21"][...])
    for c in range(6):
        e1[c, pl.ds(0, 16, stride=2), :] = spread2[16 * c : 16 * c + 16]
        e1[c, pl.ds(1, 16, stride=2), :] = spread2[16 * c : 16 * c + 16]
    for x in range(4, 14):
        c = (x + 5) // 2 - 4
        v1b[x] = v1b[x] + jnp.concatenate([e1[c, 12:28], e1[c, 4:12]], axis=0)
    sweep(v1b, v1a, f1, ops1, 5, 13, 8)
    sweep(v1a, v1b, f1, ops1, 6, 12, 6)

    e0 = s["e0"]
    for c in range(6):
        e0[c, pl.ds(0, 24, stride=2), :] = v1b[6 + c]
        e0[c, pl.ds(1, 24, stride=2), :] = v1b[6 + c]
    row8 = iota((8, 128), 0)
    parts = []
    for c in range(6):
        parts += [e0[c, 0:16], jnp.where(row8 < 4, e0[c, 16:24], e0[c, 40:48])]
    spread1 = dot01(jnp.concatenate(parts, axis=0), s["p10"][...])
    stay.wait()
    arrive(in_vd)
    merge0("hd", vd, 2)
    for x in range(1, 13):
        c = (x + 11) // 2 - 6
        ve[x] = vd[x] + spread1[24 * c : 24 * c + 24]
    sweep(ve, vb, g0, ops0, 2, 12, 10)

    def last(x):
        v = vb[x + 3] + ops0[3][x + 3] * res_at(vb, g0, ops0, x + 3)
        out[x] = v[0:16]

    each(0, 8, 8, last)
    drain()


def scratch_list():
    def vmem(*shape, kind=F32):
        return pltpu.VMEM(shape, kind)

    made = [("mat", vmem(8, 16, 256, kind=jnp.int32))]
    for name in ("k0", "va", "vb", "vc", "vd", "ve", "src", "g0", "cx0", "cy0", "cz0", "w0"):
        made.append((name, vmem(14, 24, 256)))
    for name in ("k1", "f1", "v1a", "v1b", "cx1", "cy1", "cz1", "w1"):
        made.append((name, vmem(18, 24, 128)))
    for name in ("k2", "f2", "v2a", "v2b", "cx2", "cy2", "cz2", "w2"):
        made.append((name, vmem(14, 16, 128)))
    for name in ("x2k", "x2f"):
        made.append((name, vmem(14, 5, 4, 128)))
    for name in ("hk", "hv", "hs", "hd"):
        made.append((name + "_e", vmem(8, 8, 256)))
        made.append((name + "_b", vmem(14, 8, 256)))
    made.append(("f2l", vmem(6, 8, 128)))
    for name in ("ka", "fa"):
        made.append((name, vmem(N, 2, 128)))
    for name in ("kb", "fb"):
        made.append((name, vmem(4, N, 2, 128)))
    for name in ("kt", "ft"):
        made.append((name, vmem(2, 128)))
    for name in ("ks", "fs"):
        made.append((name, vmem(4, 2, 128)))
    made.append(("t0", vmem(4, 2, 16, 128)))
    made.append(("t1", vmem(6, 24, 128)))
    made.append(("t2", vmem(1, 8, 128)))
    made.append(("e3", vmem(4, 8, 128)))
    made.append(("e2", vmem(7, 16, 128)))
    made.append(("e1", vmem(6, 32, 128)))
    made.append(("e0", vmem(6, 48, 128)))
    made.append(("low3", vmem(4, 8, 32, 128)))
    made.append(("low4", vmem(2, 8, 32, 128)))
    made.append(("low5", vmem(1, 8, 32, 128)))
    made.append(("m6", vmem(32, 128)))
    made.append(("inv", vmem(2, 128, 512, kind=BF16)))
    for name, shape in (("r01", (256, 128)), ("r12", (128, 128)), ("r23", (128, 128)), ("p32", (128, 128)), ("p21", (128, 128)), ("p10", (128, 256)), ("sel", (128, 128)), ("spr", (128, 512))):
        made.append((name, vmem(*shape, kind=BF16)))
    made.append(("load", pltpu.SemaphoreType.DMA((3,))))
    groups = {"hk": 8, "hv": 8, "hs": 8, "hd": 8, "h1k": 14, "h1f": 14, "ka": 15, "kb": 15, "fa": 15, "fb": 15, "k2a": 6, "f2a": 6, "k2b": 4, "f2b": 4}
    for name, count in groups.items():
        made.append((name + "_s", pltpu.SemaphoreType.DMA((count,))))
        made.append((name + "_r", pltpu.SemaphoreType.DMA((count,))))
    return made


SCRATCH = scratch_list()


def shards(concentration, source, material):
    return pl.pallas_call(
        kernel,
        out_shape=jax.ShapeDtypeStruct(concentration.shape, F32),
        in_specs=[pl.BlockSpec(memory_space=pltpu.HBM)] * 3,
        out_specs=pl.BlockSpec(memory_space=pltpu.VMEM),
        scratch_shapes=[shape for _, shape in SCRATCH],
        compiler_params=pltpu.CompilerParams(collective_id=0, has_side_effects=True, vmem_limit_bytes=56360960),
        cost_estimate=pl.CostEstimate(flops=20_000_000, bytes_accessed=1_000_000, transcendentals=0),
        name="vcycle",
    )(concentration, source, material)


def solution(mesh):
    placed = P("tx", "ty", None)
    return jax.shard_map(shards, mesh=mesh, in_specs=(placed,) * 3, out_specs=placed, check_vma=False)
```

```python
import jax
import jax.numpy as jnp
from jax import lax
from jax.experimental import pallas as pl
from jax.experimental.pallas import tpu as pltpu
from jax.sharding import PartitionSpec as P

MESH = pl.DeviceIdType.MESH
F32 = jnp.float32
BF16 = jnp.bfloat16
RATE = 0.001
RELAX = 0.8
TABLE = (0.15, 0.3, 0.5, 0.8, 1.2, 2.0, 3.2, 5.0)
N = 16


def iota(shape, axis):
    return lax.broadcasted_iota(jnp.int32, shape, axis)


def roll(v, shift, axis):
    return pltpu.roll(v, shift % v.shape[axis], axis)


def dot01(v, m):
    hi = v.astype(BF16)
    low = (v - hi.astype(F32)).astype(BF16)
    rows = len(v)
    if rows % 16 == 0:
        both = jnp.dot(jnp.concatenate([hi, low], axis=0), m, preferred_element_type=F32)
        return both[:rows] + both[rows:]
    return jnp.dot(hi, m, preferred_element_type=F32) + jnp.dot(low, m, preferred_element_type=F32)


def each(low, high, unroll, body):
    count = high - low
    whole = count // unroll
    if whole > 1:

        def step(i, carry):
            for k in range(unroll):
                body(low + i * unroll + k)
            return carry

        lax.fori_loop(0, whole, step, 0)
        rest = low + whole * unroll
    else:
        rest = low
    for x in range(rest, high):
        body(x)


def make_ops(kappa, ops, scale, layers, unroll):
    cx, cy, cz, w = ops
    half = 0.5 * scale

    def couple(x):
        k = kappa[x]
        cx[x] = half * (k + kappa[x + 1])
        cy[x] = half * (k + roll(k, -1, 0))
        cz[x] = half * (k + roll(k, -1, 1))

    def weigh(x):
        a, b = cy[x], cz[x]
        diag = (RATE + cx[x] + cx[x - 1]) + (a + roll(a, 1, 0)) + (b + roll(b, 1, 1))
        w[x] = RELAX / diag

    each(0, layers - 1, unroll, couple)
    each(1, layers - 1, unroll, weigh)


def residual(v, below, above, g, cx, cxm, cy, cz):
    fy = cy * (roll(v, -1, 0) - v)
    fz = cz * (roll(v, -1, 1) - v)
    r = (g - RATE * v) + (cx * (above - v) - cxm * (v - below))
    return r + (fy - roll(fy, 1, 0)) + (fz - roll(fz, 1, 1))


def res_at(v, g, ops, x):
    cx, cy, cz, _ = ops
    return residual(v[x], v[x - 1], v[x + 1], g[x], cx[x], cx[x - 1], cy[x], cz[x])


def sweep(v, out, g, ops, low, high, unroll):
    def body(x):
        out[x] = v[x] + ops[3][x] * res_at(v, g, ops, x)

    each(low, high, unroll, body)


def x_hi_next(v):
    lane = iota(v.shape, 1)
    return jnp.where(lane % 4 == 3, roll(v, 3, 1), roll(v, -1, 1))


def x_hi_prev(v):
    lane = iota(v.shape, 1)
    return jnp.where(lane % 4 == 0, roll(v, -3, 1), roll(v, 1, 1))


def low_couple(kappa, s, scale):
    half = 0.5 * scale
    nxt = kappa[1:] + [x_hi_next(kappa[0])]
    cx = [half * (k + n) for k, n in zip(kappa, nxt)]
    cxm = [x_hi_prev(cx[-1])] + cx[:-1]
    made = []
    for k, a, am in zip(kappa, cx, cxm):
        b, c = half * (k + roll(k, -s, 0)), half * (k + roll(k, -4 * s, 1))
        bm, cm = roll(b, s, 0), roll(c, 4 * s, 1)
        diag = (RATE + a + am) + (b + bm) + (c + cm)
        w = RELAX / diag
        made.append([w * a, w * am, w * b, w * bm, w * c, w * cm, w, diag * (1.0 / RELAX)])
    return made


def low_step(v, wg, ops, s):
    nxt = v[1:] + [x_hi_next(v[0])]
    prv = [x_hi_prev(v[-1])] + v[:-1]
    out = []
    for u, n, p, f, o in zip(v, nxt, prv, wg, ops):
        along_x = o[0] * n + o[1] * p
        along_y = o[2] * roll(u, -s, 0) + o[3] * roll(u, s, 0)
        along_z = o[4] * roll(u, -4 * s, 1) + o[5] * roll(u, 4 * s, 1)
        out.append((along_x + along_y) + (along_z + (f - RELAX * u)))
    return out


def low_sweep(v, wg, ops, s):
    return [u + d for u, d in zip(v, low_step(v, wg, ops, s))]


def low_restrict(v, s):
    if len(v) > 1:
        v = [v[2 * k] + v[2 * k + 1] for k in range(len(v) // 2)]
    else:
        u = v[0]
        lane = iota(u.shape, 1)
        v = [u + jnp.where(lane % 2 == 0, roll(u, -1, 1), roll(u, 1, 1))]
    out = []
    for u in v:
        row, lane = iota(u.shape, 0), iota(u.shape, 1)
        u = u + jnp.where((row // s) % 2 == 0, roll(u, -s, 0), roll(u, s, 0))
        u = u + jnp.where((lane // (4 * s)) % 2 == 0, roll(u, -4 * s, 1), roll(u, 4 * s, 1))
        out.append(u * 0.125)
    return out


def pack_six(v):
    lane = iota((8, 128), 1)
    y = (lane % 32) // 4
    out = v[24:32]
    for k in (2, 1, 0):
        out = jnp.where(y == k, v[8 * k : 8 * k + 8], out)
    return out


def kernel(conc, source, material, out, *scratch):
    names = [name for name, _ in SCRATCH]
    s = dict(zip(names, scratch))
    ops0, ops1, ops2 = [[s[f"{name}{level}"] for name in ("cx", "cy", "cz", "w")] for level in (0, 1, 2)]
    me_x, me_y = lax.axis_index("tx"), lax.axis_index("ty")

    def device(dx, dy):
        return (lax.rem(me_x + (dx + N), N), lax.rem(me_y + (dy + N), N))

    counter = {}

    def copy(group, src, dst, dx, dy):
        k = counter.get(group, 0)
        counter[group] = k + 1
        c = pltpu.make_async_remote_copy(
            src, dst, s[group + "_s"].at[k], s[group + "_r"].at[k], device_id=device(dx, dy), device_id_type=MESH
        )
        c.start()
        return c

    sent = []

    def arrive(copies):
        for c in copies:
            c.wait_recv()
        sent.extend(copies)

    def drain():
        for c in sent:
            c.wait_send()
        sent.clear()

    tile0 = (slice(3, 11), slice(0, 16))
    loads = [
        pltpu.make_async_copy(material, s["mat"], s["load"].at[0]),
        pltpu.make_async_copy(conc, s["va"].at[3:11, 0:16], s["load"].at[1]),
        pltpu.make_async_copy(source, s["src"].at[3:11, 0:16], s["load"].at[2]),
    ]
    barrier = pltpu.get_barrier_semaphore()
    peers = [(d, 0) for d in range(1, N)] + [(0, d) for d in range(1, N)]
    peers += [(a, b) for a in (-2, -1, 1, 2) for b in (-1, 1)]
    peers.sort(key=lambda p: -min(p[0] % N, -p[0] % N) - min(p[1] % N, -p[1] % N))
    for p in peers:
        pl.semaphore_signal(barrier, inc=1, device_id=device(*p), device_id_type=MESH)
    for c in loads:
        c.start()

    loads[0].wait()
    k0 = s["k0"]

    def lookup(x):
        m = s["mat"][x]
        result = jnp.zeros(m.shape, F32)
        for slot, value in enumerate(TABLE):
            result = jnp.where(m == slot, F32(value), result)
        k0[x + 3, 0:16] = result

    each(0, 8, 8, lookup)
    loads[1].wait()
    loads[2].wait()
    def halo0(group, ref, dest, w, c):
        edge, below = s[group + "_e"], s[group + "_b"]
        copies = []
        for dx, dy in ((1, 0), (-1, 0), (0, 1), (0, -1), (1, 1), (1, -1), (-1, 1), (-1, -1)):
            n = c if dy else w
            x0, x1 = {0: (3, 11), -1: (3, 3 + n), 1: (11 - n, 11)}[dx]
            y0, y1 = x0 - 8 * dx, x1 - 8 * dx
            if dy == 0:
                copies.append(copy(group, ref.at[x0:x1, 0:16], dest.at[y0:y1, 0:16], dx, dy))
            elif dy < 0:
                copies.append(copy(group, ref.at[x0:x1, 0:w], dest.at[y0:y1, 16 : 16 + w], dx, dy))
            else:
                copies.append(copy(group, edge.at[x0 - 3 : x1 - 3, 0:w], below.at[y0:y1, 0:w], dx, dy))
        return copies

    def edges0(group, ref, w):
        for x in range(8):
            s[group + "_e"][x] = roll(ref[x + 3, 8:16], w, 0)

    edges0("hk", k0, 3)
    edges0("hv", s["va"], 3)
    edges0("hs", s["src"], 2)
    pl.semaphore_wait(barrier, len(peers))

    def merge0(group, dest, w, layers=range(14)):
        below = s[group + "_b"]
        row = iota((8, 256), 0)
        for x in layers:
            dest[x, 16:24] = jnp.where(row < 4, dest[x, 16:24], roll(below[x], -w, 0))

    in_k0 = halo0("hk", k0, k0, 3, 2)
    in_va = halo0("hv", s["va"], s["va"], 3, 2)
    in_src = halo0("hs", s["src"], s["src"], 2, 1)

    def matrix(name, rule):
        shape = s[name].shape
        s[name][...] = jnp.where(rule(iota(shape, 0), iota(shape, 1)), 1.0, 0.0).astype(BF16)

    matrix("r01", lambda i, j: i // 2 == j)
    matrix("r12", lambda i, j: i // 2 == j % 64)
    matrix("r23", lambda i, j: i // 2 == j // 4)
    matrix("p32", lambda i, j: i // 4 == (j % 64) // 2)
    matrix("p21", lambda i, j: i == j // 2)
    matrix("p10", lambda i, j: i == j // 2)
    matrix("sel", lambda i, j: ((i % 32) // 4 < 4) & (i % 2 == 0) & (j == ((i % 32) // 4) * 8 + (i // 32) * 2 + (i % 4) // 2))
    matrix("spr", lambda i, j: i == (j // 128) * 8 + ((j % 128) // 32) * 2 + (j % 4) // 2)

    t0, t1, t2 = s["t0"], s["t1"], s["t2"]

    def put0(c, pair):
        t0[c, 0] = pair[:16, :128]
        t0[c, 1] = pair[:16, 128:]

    def take0():
        rows = []
        for c in range(4):
            halves = [t0[c, h, pl.ds(0, 8, stride=2), :] + t0[c, h, pl.ds(1, 8, stride=2), :] for h in range(2)]
            rows.append(jnp.concatenate(halves, axis=1))
        return dot01(jnp.concatenate(rows, axis=0), s["r01"][...]) * 0.125

    def row_pairs(ref, k, start, count):
        return ref[k, pl.ds(start, count, stride=2), :] + ref[k, pl.ds(start + 1, count, stride=2), :]

    k1, k2, x2k, x2f = s["k1"], s["k2"], s["x2k"], s["x2f"]
    for c in range(4):
        put0(c, k0[3 + 2 * c, 0:16] + k0[4 + 2 * c, 0:16])
    tile = take0()
    for c in range(4):
        k1[7 + c, 0:8] = tile[8 * c : 8 * c + 8]

    def halo1(group, ref, w):
        copies = []
        for dx, dy in ((2, 1), (2, -1), (-2, 1), (-2, -1), (1, 1), (1, -1), (-1, 1), (-1, -1), (0, 1), (0, -1), (2, 0), (-2, 0), (1, 0), (-1, 0)):
            nx = {0: 4, 1: 4, 2: w - 4 if dy == 0 else w - 5}[abs(dx)]
            ny = 8 if dy == 0 else {0: w, 1: w - 1, 2: w - 5}[abs(dx)]
            xs = slice(11 - nx, 11) if dx > 0 else slice(7, 7 + nx)
            xd = slice(xs.start - 4 * dx, xs.stop - 4 * dx)
            ys = slice(0, 8) if dy > 0 else slice(0, ny)
            yd = slice(16, 24) if dy > 0 else slice(-8 * dy, ny - 8 * dy)
            copies.append(copy(group, ref.at[xs, ys], ref.at[xd, yd], dx, dy))
        return copies

    def to_level2(get):
        parts = []
        for c in range(len(get) // 2):
            pair = get[2 * c] + get[2 * c + 1]
            if len(pair) == 8:
                t1[c, 4:12] = pair
            else:
                t1[c] = roll(pair, 4, 0)
        for c in range(len(get) // 2):
            parts.append(row_pairs(t1, c, 0, 8))
        return dot01(jnp.concatenate(parts, axis=0), s["r12"][...]) * 0.125

    def to_level3(pair, row0):
        t2[0] = dot01(pair, s["r23"][...]) * 0.125
        return row_pairs(t2, 0, row0, 2)

    low = to_level2([tile[8 * c : 8 * c + 8] for c in range(4)])
    for c in range(2):
        x2k[6 + c, 2] = low[8 * c + 2 : 8 * c + 6]
    base = to_level3(low[0:8] + low[8:16], 2)

    def ring_x(group, ref, tile_ref, value):
        tile_ref[...] = value
        ref[me_x] = value
        return [copy(group, tile_ref, ref.at[me_x], d, 0) for d in range(1, N)]

    def window_x(group, ref):
        return [
            copy(group, ref.at[6:8, 2], ref.at[6 - 2 * d : 8 - 2 * d, 2], d, 0) for d in (1, -1, 2, -2, 3, -3)
        ]

    def slab(ref):
        lane = iota((2, 128), 1)
        out_parts = []
        for k in range(4):
            v = ref[12 + k]
            for h in (2, 1, 0):
                v = jnp.where(lane % 4 == h, ref[4 * h + k], v)
            out_parts.append(v)
        return out_parts

    def ring_y(group, ref, slab_ref, parts):
        for k in range(4):
            slab_ref[k] = parts[k]
            ref[k, me_y] = parts[k]
        return [copy(group, slab_ref, ref.at[:, me_y], 0, d) for d in range(1, N)]

    def window_y(group, ref):
        return [copy(group, ref.at[:, 2], ref.at[:, 2 - d], 0, d) for d in (1, -1, 2, -2)]

    def window(ref, dest):
        for x in range(14):
            dest[x] = ref[x].reshape(20, 128)[2:18]

    in_ka = ring_x("ka", s["ka"], s["kt"], base)
    in_k2a = window_x("k2a", x2k)
    arrive(in_k0)
    merge0("hk", k0, 3)
    make_ops(k0, ops0, 1.0, 14, 13)
    in_k1 = halo1("h1k", k1, 7)
    arrive(in_va[2:4])
    arrive(in_src[2:4])
    merge0("hv", s["va"], 3, range(3, 11))
    merge0("hs", s["src"], 2, range(3, 11))
    va, vb, vc, vd, ve, src, g0 = [s[name] for name in ("va", "vb", "vc", "vd", "ve", "src", "g0")]

    def force(x):
        g0[x] = RATE * va[x] + src[x]

    each(3, 11, 8, force)
    sweep(va, vb, g0, ops0, 4, 10, 6)
    arrive(in_va[:2] + in_va[4:])
    arrive(in_src[:2] + in_src[4:])
    merge0("hv", va, 3, (0, 1, 2, 11, 12, 13))
    merge0("hs", src, 2, (1, 2, 11, 12))
    for x in (1, 2, 11, 12):
        force(x)
    sweep(va, vb, g0, ops0, 1, 4, 3)
    sweep(va, vb, g0, ops0, 10, 13, 3)
    sweep(vb, vc, g0, ops0, 2, 12, 10)

    def down0(c):
        put0(c, res_at(vc, g0, ops0, 2 * c + 3) + res_at(vc, g0, ops0, 2 * c + 4))

    each(0, 4, 4, down0)
    tile = take0()
    f1 = s["f1"]
    for c in range(4):
        f1[7 + c, 0:8] = tile[8 * c : 8 * c + 8]
    in_f1 = halo1("h1f", f1, 6)

    arrive(in_k2a)
    in_k2b = window_y("k2b", x2k)
    arrive(in_ka)
    in_kb = ring_y("kb", s["kb"], s["ks"], slab(s["ka"]))
    stay = pltpu.make_async_copy(vc.at[tile0], vd.at[tile0], s["load"].at[0])
    stay.start()
    edges0("hd", vc, 2)
    in_vd = halo0("hd", vc, vd, 2, 1)

    arrive(in_k1)
    make_ops(k1, ops1, 0.25, 18, 17)
    arrive(in_k2b)
    window(x2k, k2)
    make_ops(k2, ops2, 0.0625, 14, 13)
    arrive(in_f1)

    v1a, v1b = s["v1a"], s["v1b"]

    def start1(x):
        v1a[x] = ops1[3][x] * f1[x]

    each(1, 17, 16, start1)
    sweep(v1a, v1b, f1, ops1, 2, 16, 14)
    low = to_level2([res_at(v1b, f1, ops1, x) for x in range(3, 15)])
    f2l = s["f2l"]
    f2 = s["f2"]
    for c in range(6):
        f2l[c] = low[8 * c : 8 * c + 8]
    for c in range(2):
        x2f[6 + c, 2] = low[8 * c + 18 : 8 * c + 22]

    v2a, v2b = s["v2a"], s["v2b"]
    near = [[ref[x, 4:12] for x in range(4, 10)] for ref in ops2]
    fl = [f2l[c] for c in range(6)]
    vl = [near[3][c] * fl[c] for c in range(6)]

    def res_near(v, c):
        return residual(v[c], v[c - 1], v[c + 1], fl[c], near[0][c], near[0][c - 1], near[1][c], near[2][c])

    ul = [None] + [vl[c] + near[3][c] * res_near(vl, c) for c in range(1, 5)]
    base = to_level3(res_near(ul + [None], 2) + res_near(ul + [None], 3), 2)
    in_fa = ring_x("fa", s["fa"], s["ft"], base)
    in_f2a = window_x("f2a", x2f)

    arrive(in_kb)
    kap3 = [s["kb"][k].reshape(32, 128) for k in range(4)]
    kap4 = low_restrict(kap3, 1)
    kap5 = low_restrict(kap4, 2)
    kap6 = low_restrict(kap5, 4)[0]
    for level, kap, spread in ((3, kap3, 1), (4, kap4, 2), (5, kap5, 4)):
        made = low_couple(kap, spread, 1.0 / 4.0**level)
        for k in range(len(kap)):
            for number in range(8):
                s[f"low{level}"][k, number] = made[k][number]

    krow = dot01(pack_six(kap6), s["sel"][...])[0:1]
    q, p = iota((32, 128), 0), iota((32, 128), 1)
    kcol = jnp.sum(jnp.where(q == p, krow, 0.0), axis=1, keepdims=True)
    dy, dz, same_x = (q // 8 - p // 8 + 4) % 4, ((q % 8) // 2 - (p % 8) // 2 + 4) % 4, q % 2 == p % 2
    links = jnp.where(same_x & (dz == 0) & (dy % 2 == 1), 1.0, 0.0) + jnp.where(same_x & (dy == 0) & (dz % 2 == 1), 1.0, 0.0)
    links = links + jnp.where((dz == 0) & (dy == 0) & (q % 2 != p % 2), 2.0, 0.0)
    links = jnp.where(p < 32, links, 0.0)
    off = (0.5 / 4096.0) * links * (krow + kcol)
    diag = RATE + jnp.sum(off, axis=1, keepdims=True)
    m_ref = s["m6"]
    m_ref[...] = jnp.where(q == p, diag, jnp.where(p == q + 32, 1.0, -off))

    def eliminate(k, carry):
        m = m_ref[...]
        pivot_row = m_ref[pl.ds(k, 1), :]
        column = jnp.sum(jnp.where(p == k, m, 0.0), axis=1, keepdims=True)
        pivot = jnp.sum(jnp.where(iota((1, 128), 1) == k, pivot_row, 0.0), axis=1, keepdims=True)
        scaled = pivot_row / pivot
        m_ref[...] = jnp.where(q == k, scaled, m - column * scaled)
        return carry

    lax.fori_loop(0, 16, eliminate, 0)

    arrive(in_fa)
    in_fb = ring_y("fb", s["fb"], s["fs"], slab(s["fa"]))
    arrive(in_f2a)
    in_f2b = window_y("f2b", x2f)
    lax.fori_loop(16, 32, eliminate, 0)
    inverse = roll(m_ref[...], -32, 1)
    inverse = jnp.concatenate([jnp.where(p < 32, inverse, 0.0), jnp.zeros((96, 128), F32)], axis=0)
    inverse = dot01(inverse, s["spr"][...])
    hi = inverse.astype(BF16)
    rest = inverse - hi.astype(F32)
    mid = rest.astype(BF16)
    pieces = (hi, mid, (rest - mid.astype(F32)).astype(BF16))
    a, b, c = [jnp.dot(s["sel"][...], piece, preferred_element_type=F32) for piece in pieces]
    inverse = a + (b + c)
    hi = inverse.astype(BF16)
    s["inv"][0] = hi
    s["inv"][1] = (inverse - hi.astype(F32)).astype(BF16)

    drain()

    def low_ops(level, count):
        return [[s[f"low{level}"][k, number] for number in range(8)] for k in range(count)]

    arrive(in_fb)
    g3 = [s["fb"][k].reshape(32, 128) for k in range(4)]
    o3, o4, o5 = low_ops(3, 4), low_ops(4, 2), low_ops(5, 1)

    def down(g, o, spread):
        wg = [q[6] * f for q, f in zip(o, g)]
        v = low_sweep(wg, wg, o, spread)
        step = low_step(v, wg, o, spread)
        return v, wg, low_restrict([q[7] * d for q, d in zip(o, step)], spread)

    v3, wg3, g4 = down(g3, o3, 1)
    v4, wg4, g5 = down(g4, o4, 2)
    v5, wg5, g6 = down(g5, o5, 4)
    x6 = pack_six(g6[0])
    hi = x6.astype(BF16).astype(F32)
    both = jnp.concatenate([hi, x6 - hi], axis=0).astype(BF16)
    large = jnp.dot(both, s["inv"][0], preferred_element_type=F32)
    x6 = large[:8] + (large[8:] + jnp.dot(both, s["inv"][1], preferred_element_type=F32)[:8])
    x6 = jnp.concatenate([x6[:, 128 * k : 128 * k + 128] for k in range(4)], axis=0)

    def up(v, e, wg, o, spread):
        v = [u + e[k * len(e) // len(v)] for k, u in enumerate(v)]
        return low_sweep(low_sweep(v, wg, o, spread), wg, o, spread)

    v5 = up(v5, [x6], wg5, o5, 4)
    v4 = up(v4, v5, wg4, o4, 2)
    v3 = up(v3, v4, wg3, o3, 1)

    e3, e2, e1 = s["e3"], s["e2"], s["e1"]
    turn = lax.rem(2 * N - 2 * me_y + 3, 2 * N)
    for k in range(4):
        e3[k] = pltpu.roll(v3[k], turn, 0)[0:8]
    picks = []
    lane8 = iota((8, 128), 1)
    for d in range(-2, 3):
        x = lax.rem(me_x + (d + N), N)
        picks.append(jnp.where(lane8 % 4 == x // 4, e3[lax.rem(x, 4)], 0.0))
    spread3 = dot01(jnp.concatenate(picks, axis=0), s["p32"][...])
    for c in range(5):
        e2[c + 1, pl.ds(0, 8, stride=2), :] = spread3[8 * c : 8 * c + 8]
        e2[c + 1, pl.ds(1, 8, stride=2), :] = spread3[8 * c : 8 * c + 8]

    arrive(in_f2b)
    window(x2f, f2)
    for x in range(1, 13):
        v2a[x] = ops2[3][x] * f2[x]
    sweep(v2a, v2b, f2, ops2, 2, 12, 10)
    for x in range(2, 12):
        v2b[x] = v2b[x] + e2[x // 2]
    sweep(v2b, v2a, f2, ops2, 3, 11, 8)
    sweep(v2a, v2b, f2, ops2, 4, 10, 6)

    spread2 = dot01(jnp.concatenate([v2b[x] for x in range(4, 10)], axis=0), s["p21"][...])
    for c in range(6):
        e1[c, pl.ds(0, 16, stride=2), :] = spread2[16 * c : 16 * c + 16]
        e1[c, pl.ds(1, 16, stride=2), :] = spread2[16 * c : 16 * c + 16]
    for x in range(4, 14):
        c = (x + 5) // 2 - 4
        v1b[x] = v1b[x] + jnp.concatenate([e1[c, 12:28], e1[c, 4:12]], axis=0)
    sweep(v1b, v1a, f1, ops1, 5, 13, 8)
    sweep(v1a, v1b, f1, ops1, 6, 12, 6)

    e0 = s["e0"]
    for c in range(6):
        e0[c, pl.ds(0, 24, stride=2), :] = v1b[6 + c]
        e0[c, pl.ds(1, 24, stride=2), :] = v1b[6 + c]
    row8 = iota((8, 128), 0)
    parts = []
    for c in range(6):
        parts += [e0[c, 0:16], jnp.where(row8 < 4, e0[c, 16:24], e0[c, 40:48])]
    spread1 = dot01(jnp.concatenate(parts, axis=0), s["p10"][...])
    stay.wait()
    arrive(in_vd)
    merge0("hd", vd, 2)
    for x in range(1, 13):
        c = (x + 11) // 2 - 6
        ve[x] = vd[x] + spread1[24 * c : 24 * c + 24]
    sweep(ve, vb, g0, ops0, 2, 12, 10)

    def last(x):
        v = vb[x + 3] + ops0[3][x + 3] * res_at(vb, g0, ops0, x + 3)
        out[x] = v[0:16]

    each(0, 8, 8, last)
    drain()


def scratch_list():
    def vmem(*shape, kind=F32):
        return pltpu.VMEM(shape, kind)

    made = [("mat", vmem(8, 16, 256, kind=jnp.int32))]
    for name in ("k0", "va", "vb", "vc", "vd", "ve", "src", "g0", "cx0", "cy0", "cz0", "w0"):
        made.append((name, vmem(14, 24, 256)))
    for name in ("k1", "f1", "v1a", "v1b", "cx1", "cy1", "cz1", "w1"):
        made.append((name, vmem(18, 24, 128)))
    for name in ("k2", "f2", "v2a", "v2b", "cx2", "cy2", "cz2", "w2"):
        made.append((name, vmem(14, 16, 128)))
    for name in ("x2k", "x2f"):
        made.append((name, vmem(14, 5, 4, 128)))
    for name in ("hk", "hv", "hs", "hd"):
        made.append((name + "_e", vmem(8, 8, 256)))
        made.append((name + "_b", vmem(14, 8, 256)))
    made.append(("f2l", vmem(6, 8, 128)))
    for name in ("ka", "fa"):
        made.append((name, vmem(N, 2, 128)))
    for name in ("kb", "fb"):
        made.append((name, vmem(4, N, 2, 128)))
    for name in ("kt", "ft"):
        made.append((name, vmem(2, 128)))
    for name in ("ks", "fs"):
        made.append((name, vmem(4, 2, 128)))
    made.append(("t0", vmem(4, 2, 16, 128)))
    made.append(("t1", vmem(6, 24, 128)))
    made.append(("t2", vmem(1, 8, 128)))
    made.append(("e3", vmem(4, 8, 128)))
    made.append(("e2", vmem(7, 16, 128)))
    made.append(("e1", vmem(6, 32, 128)))
    made.append(("e0", vmem(6, 48, 128)))
    made.append(("low3", vmem(4, 8, 32, 128)))
    made.append(("low4", vmem(2, 8, 32, 128)))
    made.append(("low5", vmem(1, 8, 32, 128)))
    made.append(("m6", vmem(32, 128)))
    made.append(("inv", vmem(2, 128, 512, kind=BF16)))
    for name, shape in (("r01", (256, 128)), ("r12", (128, 128)), ("r23", (128, 128)), ("p32", (128, 128)), ("p21", (128, 128)), ("p10", (128, 256)), ("sel", (128, 128)), ("spr", (128, 512))):
        made.append((name, vmem(*shape, kind=BF16)))
    made.append(("load", pltpu.SemaphoreType.DMA((3,))))
    groups = {"hk": 8, "hv": 8, "hs": 8, "hd": 8, "h1k": 14, "h1f": 14, "ka": 15, "kb": 15, "fa": 15, "fb": 15, "k2a": 6, "f2a": 6, "k2b": 4, "f2b": 4}
    for name, count in groups.items():
        made.append((name + "_s", pltpu.SemaphoreType.DMA((count,))))
        made.append((name + "_r", pltpu.SemaphoreType.DMA((count,))))
    return made


SCRATCH = scratch_list()


def shards(concentration, source, material):
    return pl.pallas_call(
        kernel,
        out_shape=jax.ShapeDtypeStruct(concentration.shape, F32),
        in_specs=[pl.BlockSpec(memory_space=pltpu.HBM)] * 3,
        out_specs=pl.BlockSpec(memory_space=pltpu.VMEM),
        scratch_shapes=[shape for _, shape in SCRATCH],
        compiler_params=pltpu.CompilerParams(collective_id=0, has_side_effects=True, vmem_limit_bytes=56360960),
        cost_estimate=pl.CostEstimate(flops=20_000_000, bytes_accessed=1_000_000, transcendentals=0),
        name="vcycle",
    )(concentration, source, material)


def solution(mesh):
    placed = P("tx", "ty", None)
    return jax.shard_map(shards, mesh=mesh, in_specs=(placed,) * 3, out_specs=placed, check_vma=False)
```

```python
import jax
import jax.numpy as jnp
from jax import lax
from jax.experimental import pallas as pl
from jax.experimental.pallas import tpu as pltpu
from jax.sharding import PartitionSpec as P

MESH = pl.DeviceIdType.MESH
F32 = jnp.float32
BF16 = jnp.bfloat16
RATE = 0.001
RELAX = 0.8
TABLE = (0.15, 0.3, 0.5, 0.8, 1.2, 2.0, 3.2, 5.0)
N = 16


def iota(shape, axis):
    return lax.broadcasted_iota(jnp.int32, shape, axis)


def roll(v, shift, axis):
    return pltpu.roll(v, shift % v.shape[axis], axis)


def dot01(v, m):
    hi = v.astype(BF16)
    low = (v - hi.astype(F32)).astype(BF16)
    rows = len(v)
    if rows % 16 == 0:
        both = jnp.dot(jnp.concatenate([hi, low], axis=0), m, preferred_element_type=F32)
        return both[:rows] + both[rows:]
    return jnp.dot(hi, m, preferred_element_type=F32) + jnp.dot(low, m, preferred_element_type=F32)


def each(low, high, unroll, body):
    count = high - low
    whole = count // unroll
    if whole > 1:

        def step(i, carry):
            for k in range(unroll):
                body(low + i * unroll + k)
            return carry

        lax.fori_loop(0, whole, step, 0)
        rest = low + whole * unroll
    else:
        rest = low
    for x in range(rest, high):
        body(x)


def make_ops(kappa, ops, scale, layers, unroll):
    cx, cy, cz, w = ops
    half = 0.5 * scale

    def couple(x):
        k = kappa[x]
        cx[x] = half * (k + kappa[x + 1])
        cy[x] = half * (k + roll(k, -1, 0))
        cz[x] = half * (k + roll(k, -1, 1))

    def weigh(x):
        a, b = cy[x], cz[x]
        diag = (RATE + cx[x] + cx[x - 1]) + (a + roll(a, 1, 0)) + (b + roll(b, 1, 1))
        w[x] = RELAX / diag

    each(0, layers - 1, unroll, couple)
    each(1, layers - 1, unroll, weigh)


def residual(v, below, above, g, cx, cxm, cy, cz):
    fy = cy * (roll(v, -1, 0) - v)
    fz = cz * (roll(v, -1, 1) - v)
    r = (g - RATE * v) + (cx * (above - v) - cxm * (v - below))
    return r + (fy - roll(fy, 1, 0)) + (fz - roll(fz, 1, 1))


def res_at(v, g, ops, x):
    cx, cy, cz, _ = ops
    return residual(v[x], v[x - 1], v[x + 1], g[x], cx[x], cx[x - 1], cy[x], cz[x])


def sweep(v, out, g, ops, low, high, unroll):
    def body(x):
        out[x] = v[x] + ops[3][x] * res_at(v, g, ops, x)

    each(low, high, unroll, body)


def x_hi_next(v):
    lane = iota(v.shape, 1)
    return jnp.where(lane % 4 == 3, roll(v, 3, 1), roll(v, -1, 1))


def x_hi_prev(v):
    lane = iota(v.shape, 1)
    return jnp.where(lane % 4 == 0, roll(v, -3, 1), roll(v, 1, 1))


def low_couple(kappa, s, scale):
    half = 0.5 * scale
    nxt = kappa[1:] + [x_hi_next(kappa[0])]
    cx = [half * (k + n) for k, n in zip(kappa, nxt)]
    cxm = [x_hi_prev(cx[-1])] + cx[:-1]
    made = []
    for k, a, am in zip(kappa, cx, cxm):
        b, c = half * (k + roll(k, -s, 0)), half * (k + roll(k, -4 * s, 1))
        bm, cm = roll(b, s, 0), roll(c, 4 * s, 1)
        diag = (RATE + a + am) + (b + bm) + (c + cm)
        w = RELAX / diag
        made.append([w * a, w * am, w * b, w * bm, w * c, w * cm, w, diag * (1.0 / RELAX)])
    return made


def low_step(v, wg, ops, s):
    nxt = v[1:] + [x_hi_next(v[0])]
    prv = [x_hi_prev(v[-1])] + v[:-1]
    out = []
    for u, n, p, f, o in zip(v, nxt, prv, wg, ops):
        along_x = o[0] * n + o[1] * p
        along_y = o[2] * roll(u, -s, 0) + o[3] * roll(u, s, 0)
        along_z = o[4] * roll(u, -4 * s, 1) + o[5] * roll(u, 4 * s, 1)
        out.append((along_x + along_y) + (along_z + (f - RELAX * u)))
    return out


def low_sweep(v, wg, ops, s):
    return [u + d for u, d in zip(v, low_step(v, wg, ops, s))]


def low_restrict(v, s):
    if len(v) > 1:
        v = [v[2 * k] + v[2 * k + 1] for k in range(len(v) // 2)]
    else:
        u = v[0]
        lane = iota(u.shape, 1)
        v = [u + jnp.where(lane % 2 == 0, roll(u, -1, 1), roll(u, 1, 1))]
    out = []
    for u in v:
        row, lane = iota(u.shape, 0), iota(u.shape, 1)
        u = u + jnp.where((row // s) % 2 == 0, roll(u, -s, 0), roll(u, s, 0))
        u = u + jnp.where((lane // (4 * s)) % 2 == 0, roll(u, -4 * s, 1), roll(u, 4 * s, 1))
        out.append(u * 0.125)
    return out


def pack_six(v):
    lane = iota((8, 128), 1)
    y = (lane % 32) // 4
    out = v[24:32]
    for k in (2, 1, 0):
        out = jnp.where(y == k, v[8 * k : 8 * k + 8], out)
    return out


def kernel(conc, source, material, out, *scratch):
    names = [name for name, _ in SCRATCH]
    s = dict(zip(names, scratch))
    ops0, ops1, ops2 = [[s[f"{name}{level}"] for name in ("cx", "cy", "cz", "w")] for level in (0, 1, 2)]
    me_x, me_y = lax.axis_index("tx"), lax.axis_index("ty")

    def device(dx, dy):
        return (lax.rem(me_x + (dx + N), N), lax.rem(me_y + (dy + N), N))

    counter = {}

    def copy(group, src, dst, dx, dy):
        k = counter.get(group, 0)
        counter[group] = k + 1
        c = pltpu.make_async_remote_copy(
            src, dst, s[group + "_s"].at[k], s[group + "_r"].at[k], device_id=device(dx, dy), device_id_type=MESH
        )
        c.start()
        return c

    sent = []

    def arrive(copies):
        for c in copies:
            c.wait_recv()
        sent.extend(copies)

    def drain():
        for c in sent:
            c.wait_send()
        sent.clear()

    tile0 = (slice(3, 11), slice(0, 16))
    loads = [
        pltpu.make_async_copy(material, s["mat"], s["load"].at[0]),
        pltpu.make_async_copy(conc, s["va"].at[3:11, 0:16], s["load"].at[1]),
        pltpu.make_async_copy(source, s["src"].at[3:11, 0:16], s["load"].at[2]),
    ]
    barrier = pltpu.get_barrier_semaphore()
    peers = [(d, 0) for d in range(1, N)] + [(0, d) for d in range(1, N)]
    peers += [(a, b) for a in (-2, -1, 1, 2) for b in (-1, 1)]
    peers.sort(key=lambda p: -min(p[0] % N, -p[0] % N) - min(p[1] % N, -p[1] % N))
    for p in peers:
        pl.semaphore_signal(barrier, inc=1, device_id=device(*p), device_id_type=MESH)
    for c in loads:
        c.start()

    loads[0].wait()
    k0 = s["k0"]

    def lookup(x):
        m = s["mat"][x]
        result = jnp.zeros(m.shape, F32)
        for slot, value in enumerate(TABLE):
            result = jnp.where(m == slot, F32(value), result)
        k0[x + 3, 0:16] = result

    each(0, 8, 8, lookup)
    loads[1].wait()
    loads[2].wait()
    def halo0(group, ref, dest, w, c):
        edge, below = s[group + "_e"], s[group + "_b"]
        copies = []
        for dx, dy in ((1, 0), (-1, 0), (0, 1), (0, -1), (1, 1), (1, -1), (-1, 1), (-1, -1)):
            n = c if dy else w
            x0, x1 = {0: (3, 11), -1: (3, 3 + n), 1: (11 - n, 11)}[dx]
            y0, y1 = x0 - 8 * dx, x1 - 8 * dx
            if dy == 0:
                copies.append(copy(group, ref.at[x0:x1, 0:16], dest.at[y0:y1, 0:16], dx, dy))
            elif dy < 0:
                copies.append(copy(group, ref.at[x0:x1, 0:w], dest.at[y0:y1, 16 : 16 + w], dx, dy))
            else:
                copies.append(copy(group, edge.at[x0 - 3 : x1 - 3, 0:w], below.at[y0:y1, 0:w], dx, dy))
        return copies

    def edges0(group, ref, w):
        for x in range(8):
            s[group + "_e"][x] = roll(ref[x + 3, 8:16], w, 0)

    edges0("hk", k0, 3)
    edges0("hv", s["va"], 3)
    edges0("hs", s["src"], 2)
    pl.semaphore_wait(barrier, len(peers))

    def merge0(group, dest, w, layers=range(14)):
        below = s[group + "_b"]
        row = iota((8, 256), 0)
        for x in layers:
            dest[x, 16:24] = jnp.where(row < 4, dest[x, 16:24], roll(below[x], -w, 0))

    in_k0 = halo0("hk", k0, k0, 3, 2)
    in_va = halo0("hv", s["va"], s["va"], 3, 2)
    in_src = halo0("hs", s["src"], s["src"], 2, 1)

    def matrix(name, rule):
        shape = s[name].shape
        s[name][...] = jnp.where(rule(iota(shape, 0), iota(shape, 1)), 1.0, 0.0).astype(BF16)

    matrix("r01", lambda i, j: i // 2 == j)
    matrix("r12", lambda i, j: i // 2 == j % 64)
    matrix("r23", lambda i, j: i // 2 == j // 4)
    matrix("p32", lambda i, j: i // 4 == (j % 64) // 2)
    matrix("p21", lambda i, j: i == j // 2)
    matrix("p10", lambda i, j: i == j // 2)
    matrix("sel", lambda i, j: ((i % 32) // 4 < 4) & (i % 2 == 0) & (j == ((i % 32) // 4) * 8 + (i // 32) * 2 + (i % 4) // 2))
    matrix("spr", lambda i, j: i == (j // 128) * 8 + ((j % 128) // 32) * 2 + (j % 4) // 2)

    t0, t1, t2 = s["t0"], s["t1"], s["t2"]

    def put0(c, pair):
        t0[c, 0] = pair[:16, :128]
        t0[c, 1] = pair[:16, 128:]

    def take0():
        rows = []
        for c in range(4):
            halves = [t0[c, h, pl.ds(0, 8, stride=2), :] + t0[c, h, pl.ds(1, 8, stride=2), :] for h in range(2)]
            rows.append(jnp.concatenate(halves, axis=1))
        return dot01(jnp.concatenate(rows, axis=0), s["r01"][...]) * 0.125

    def row_pairs(ref, k, start, count):
        return ref[k, pl.ds(start, count, stride=2), :] + ref[k, pl.ds(start + 1, count, stride=2), :]

    k1, k2, x2k, x2f = s["k1"], s["k2"], s["x2k"], s["x2f"]
    for c in range(4):
        put0(c, k0[3 + 2 * c, 0:16] + k0[4 + 2 * c, 0:16])
    tile = take0()
    for c in range(4):
        k1[7 + c, 0:8] = tile[8 * c : 8 * c + 8]

    def halo1(group, ref, w):
        copies = []
        for dx, dy in ((2, 1), (2, -1), (-2, 1), (-2, -1), (1, 1), (1, -1), (-1, 1), (-1, -1), (0, 1), (0, -1), (2, 0), (-2, 0), (1, 0), (-1, 0)):
            nx = {0: 4, 1: 4, 2: w - 4 if dy == 0 else w - 5}[abs(dx)]
            ny = 8 if dy == 0 else {0: w, 1: w - 1, 2: w - 5}[abs(dx)]
            xs = slice(11 - nx, 11) if dx > 0 else slice(7, 7 + nx)
            xd = slice(xs.start - 4 * dx, xs.stop - 4 * dx)
            ys = slice(0, 8) if dy > 0 else slice(0, ny)
            yd = slice(16, 24) if dy > 0 else slice(-8 * dy, ny - 8 * dy)
            copies.append(copy(group, ref.at[xs, ys], ref.at[xd, yd], dx, dy))
        return copies

    def to_level2(get):
        parts = []
        for c in range(len(get) // 2):
            pair = get[2 * c] + get[2 * c + 1]
            if len(pair) == 8:
                t1[c, 4:12] = pair
            else:
                t1[c] = roll(pair, 4, 0)
        for c in range(len(get) // 2):
            parts.append(row_pairs(t1, c, 0, 8))
        return dot01(jnp.concatenate(parts, axis=0), s["r12"][...]) * 0.125

    def to_level3(pair, row0):
        t2[0] = dot01(pair, s["r23"][...]) * 0.125
        return row_pairs(t2, 0, row0, 2)

    low = to_level2([tile[8 * c : 8 * c + 8] for c in range(4)])
    for c in range(2):
        x2k[6 + c, 2] = low[8 * c + 2 : 8 * c + 6]
    base = to_level3(low[0:8] + low[8:16], 2)

    def ring_x(group, ref, tile_ref, value):
        tile_ref[...] = value
        ref[me_x] = value
        return [copy(group, tile_ref, ref.at[me_x], d, 0) for d in (4, 12, 3, 5, 11, 13, 2, 6, 10, 14, 8, 7, 9, 1, 15)]

    def window_x(group, ref):
        return [
            copy(group, ref.at[6:8, 2], ref.at[6 - 2 * d : 8 - 2 * d, 2], d, 0) for d in (1, -1, 2, -2, 3, -3)
        ]

    def slab(ref):
        lane = iota((2, 128), 1)
        out_parts = []
        for k in range(4):
            v = ref[12 + k]
            for h in (2, 1, 0):
                v = jnp.where(lane % 4 == h, ref[4 * h + k], v)
            out_parts.append(v)
        return out_parts

    def ring_y(group, ref, slab_ref, parts):
        for k in range(4):
            slab_ref[k] = parts[k]
            ref[k, me_y] = parts[k]
        return [copy(group, slab_ref, ref.at[:, me_y], 0, d) for d in (12, 4, 5, 11, 13, 3, 10, 6, 8, 14, 2, 7, 9, 15, 1)]

    def window_y(group, ref):
        return [copy(group, ref.at[:, 2], ref.at[:, 2 - d], 0, d) for d in (1, -1, 2, -2)]

    def window(ref, dest):
        for x in range(14):
            dest[x] = ref[x].reshape(20, 128)[2:18]

    in_ka = ring_x("ka", s["ka"], s["kt"], base)
    in_k2a = window_x("k2a", x2k)
    arrive(in_k0)
    merge0("hk", k0, 3)
    make_ops(k0, ops0, 1.0, 14, 13)
    in_k1 = halo1("h1k", k1, 7)
    arrive(in_va[2:4])
    arrive(in_src[2:4])
    merge0("hv", s["va"], 3, range(3, 11))
    merge0("hs", s["src"], 2, range(3, 11))
    va, vb, vc, vd, ve, src, g0 = [s[name] for name in ("va", "vb", "vc", "vd", "ve", "src", "g0")]

    def force(x):
        g0[x] = RATE * va[x] + src[x]

    each(3, 11, 8, force)
    sweep(va, vb, g0, ops0, 4, 10, 6)
    arrive(in_va[:2] + in_va[4:])
    arrive(in_src[:2] + in_src[4:])
    merge0("hv", va, 3, (0, 1, 2, 11, 12, 13))
    merge0("hs", src, 2, (1, 2, 11, 12))
    for x in (1, 2, 11, 12):
        force(x)
    sweep(va, vb, g0, ops0, 1, 4, 3)
    sweep(va, vb, g0, ops0, 10, 13, 3)
    sweep(vb, vc, g0, ops0, 2, 12, 10)

    def down0(c):
        put0(c, res_at(vc, g0, ops0, 2 * c + 3) + res_at(vc, g0, ops0, 2 * c + 4))

    each(0, 4, 4, down0)
    tile = take0()
    f1 = s["f1"]
    for c in range(4):
        f1[7 + c, 0:8] = tile[8 * c : 8 * c + 8]
    in_f1 = halo1("h1f", f1, 6)

    arrive(in_k2a)
    in_k2b = window_y("k2b", x2k)
    arrive(in_ka)
    in_kb = ring_y("kb", s["kb"], s["ks"], slab(s["ka"]))
    stay = pltpu.make_async_copy(vc.at[tile0], vd.at[tile0], s["load"].at[0])
    stay.start()
    edges0("hd", vc, 2)
    in_vd = halo0("hd", vc, vd, 2, 1)

    arrive(in_k1)
    make_ops(k1, ops1, 0.25, 18, 17)
    arrive(in_k2b)
    window(x2k, k2)
    make_ops(k2, ops2, 0.0625, 14, 13)
    near = s["near"]
    for c in range(6):
        a, am, b, d, w = [ref[x, 4:12] for ref, x in zip((ops2[0], ops2[0], ops2[1], ops2[2], ops2[3]), (c + 4, c + 3, c + 4, c + 4, c + 4))]
        bm, dm = roll(b, 1, 0), roll(d, 1, 1)
        diag = (RATE + a + am) + (b + bm) + (d + dm)
        for number, value in enumerate((w * a, w * am, w * b, w * bm, w * d, w * dm, w, diag * (1.0 / RELAX))):
            near[c, number] = value
    arrive(in_f1)

    v1a, v1b = s["v1a"], s["v1b"]

    def start1(x):
        v1a[x] = ops1[3][x] * f1[x]

    each(1, 17, 16, start1)
    sweep(v1a, v1b, f1, ops1, 2, 16, 14)
    low = to_level2([res_at(v1b, f1, ops1, x) for x in range(3, 15)])
    f2l = s["f2l"]
    f2 = s["f2"]
    for c in range(6):
        f2l[c] = low[8 * c : 8 * c + 8]
    for c in range(2):
        x2f[6 + c, 2] = low[8 * c + 18 : 8 * c + 22]

    v2a, v2b = s["v2a"], s["v2b"]
    vl = [near[c, 6] * f2l[c] for c in range(6)]

    def step_near(v, c):
        o, u = [near[c, number] for number in range(6)], v[c]
        along_x = o[0] * v[c + 1] + o[1] * v[c - 1]
        along_y = o[2] * roll(u, -1, 0) + o[3] * roll(u, 1, 0)
        along_z = o[4] * roll(u, -1, 1) + o[5] * roll(u, 1, 1)
        return (along_x + along_y) + (along_z + (vl[c] - RELAX * u))

    ul = [None] + [vl[c] + step_near(vl, c) for c in range(1, 5)] + [None]
    base = to_level3(near[2, 7] * step_near(ul, 2) + near[3, 7] * step_near(ul, 3), 2)
    in_fa = ring_x("fa", s["fa"], s["ft"], base)
    in_f2a = window_x("f2a", x2f)

    arrive(in_kb)
    kap3 = [s["kb"][k].reshape(32, 128) for k in range(4)]
    kap4 = low_restrict(kap3, 1)
    kap5 = low_restrict(kap4, 2)
    kap6 = low_restrict(kap5, 4)[0]
    for level, kap, spread in ((3, kap3, 1), (4, kap4, 2), (5, kap5, 4)):
        made = low_couple(kap, spread, 1.0 / 4.0**level)
        for k in range(len(kap)):
            for number in range(8):
                s[f"low{level}"][k, number] = made[k][number]

    krow = dot01(pack_six(kap6), s["sel"][...])[0:1]
    q, p = iota((32, 128), 0), iota((32, 128), 1)
    kcol = jnp.sum(jnp.where(q == p, krow, 0.0), axis=1, keepdims=True)
    dy, dz, same_x = (q // 8 - p // 8 + 4) % 4, ((q % 8) // 2 - (p % 8) // 2 + 4) % 4, q % 2 == p % 2
    links = jnp.where(same_x & (dz == 0) & (dy % 2 == 1), 1.0, 0.0) + jnp.where(same_x & (dy == 0) & (dz % 2 == 1), 1.0, 0.0)
    links = links + jnp.where((dz == 0) & (dy == 0) & (q % 2 != p % 2), 2.0, 0.0)
    links = jnp.where(p < 32, links, 0.0)
    off = (0.5 / 4096.0) * links * (krow + kcol)
    diag = RATE + jnp.sum(off, axis=1, keepdims=True)
    m_ref = s["m6"]
    m_ref[...] = jnp.where(q == p, diag, jnp.where(p == q + 32, 1.0, -off))

    def eliminate(k, carry):
        m = m_ref[...]
        pivot_row = m_ref[pl.ds(k, 1), :]
        column = jnp.sum(jnp.where(p == k, m, 0.0), axis=1, keepdims=True)
        pivot = jnp.sum(jnp.where(iota((1, 128), 1) == k, pivot_row, 0.0), axis=1, keepdims=True)
        scaled = pivot_row / pivot
        m_ref[...] = jnp.where(q == k, scaled, m - column * scaled)
        return carry

    lax.fori_loop(0, 16, eliminate, 0)

    arrive(in_fa)
    in_fb = ring_y("fb", s["fb"], s["fs"], slab(s["fa"]))
    arrive(in_f2a)
    in_f2b = window_y("f2b", x2f)
    lax.fori_loop(16, 32, eliminate, 0)
    inverse = roll(m_ref[...], -32, 1)
    inverse = jnp.concatenate([jnp.where(p < 32, inverse, 0.0), jnp.zeros((96, 128), F32)], axis=0)
    inverse = dot01(inverse, s["spr"][...])
    hi = inverse.astype(BF16)
    rest = inverse - hi.astype(F32)
    mid = rest.astype(BF16)
    pieces = (hi, mid, (rest - mid.astype(F32)).astype(BF16))
    a, b, c = [jnp.dot(s["sel"][...], piece, preferred_element_type=F32) for piece in pieces]
    inverse = a + (b + c)
    hi = inverse.astype(BF16)
    s["inv"][0] = hi
    s["inv"][1] = (inverse - hi.astype(F32)).astype(BF16)

    drain()

    def low_ops(level, count):
        return [[s[f"low{level}"][k, number] for number in range(8)] for k in range(count)]

    arrive(in_fb)
    g3 = [s["fb"][k].reshape(32, 128) for k in range(4)]
    o3, o4, o5 = low_ops(3, 4), low_ops(4, 2), low_ops(5, 1)

    def down(g, o, spread):
        wg = [q[6] * f for q, f in zip(o, g)]
        v = low_sweep(wg, wg, o, spread)
        step = low_step(v, wg, o, spread)
        return v, wg, low_restrict([q[7] * d for q, d in zip(o, step)], spread)

    v3, wg3, g4 = down(g3, o3, 1)
    v4, wg4, g5 = down(g4, o4, 2)
    v5, wg5, g6 = down(g5, o5, 4)
    x6 = pack_six(g6[0])
    hi = x6.astype(BF16).astype(F32)
    both = jnp.concatenate([hi, x6 - hi], axis=0).astype(BF16)
    large = jnp.dot(both, s["inv"][0], preferred_element_type=F32)
    x6 = large[:8] + (large[8:] + jnp.dot(both, s["inv"][1], preferred_element_type=F32)[:8])
    x6 = jnp.concatenate([x6[:, 128 * k : 128 * k + 128] for k in range(4)], axis=0)

    def up(v, e, wg, o, spread):
        v = [u + e[k * len(e) // len(v)] for k, u in enumerate(v)]
        return low_sweep(low_sweep(v, wg, o, spread), wg, o, spread)

    v5 = up(v5, [x6], wg5, o5, 4)
    v4 = up(v4, v5, wg4, o4, 2)
    v3 = up(v3, v4, wg3, o3, 1)

    e3, e2, e1 = s["e3"], s["e2"], s["e1"]
    turn = lax.rem(2 * N - 2 * me_y + 3, 2 * N)
    for k in range(4):
        e3[k] = pltpu.roll(v3[k], turn, 0)[0:8]
    picks = []
    lane8 = iota((8, 128), 1)
    for d in range(-2, 3):
        x = lax.rem(me_x + (d + N), N)
        picks.append(jnp.where(lane8 % 4 == x // 4, e3[lax.rem(x, 4)], 0.0))
    spread3 = dot01(jnp.concatenate(picks, axis=0), s["p32"][...])
    for c in range(5):
        e2[c + 1, pl.ds(0, 8, stride=2), :] = spread3[8 * c : 8 * c + 8]
        e2[c + 1, pl.ds(1, 8, stride=2), :] = spread3[8 * c : 8 * c + 8]

    arrive(in_f2b)
    window(x2f, f2)
    for x in range(1, 13):
        v2a[x] = ops2[3][x] * f2[x]
    sweep(v2a, v2b, f2, ops2, 2, 12, 10)
    for x in range(2, 12):
        v2b[x] = v2b[x] + e2[x // 2]
    sweep(v2b, v2a, f2, ops2, 3, 11, 8)
    sweep(v2a, v2b, f2, ops2, 4, 10, 6)

    spread2 = dot01(jnp.concatenate([v2b[x] for x in range(4, 10)], axis=0), s["p21"][...])
    for c in range(6):
        e1[c, pl.ds(0, 16, stride=2), :] = spread2[16 * c : 16 * c + 16]
        e1[c, pl.ds(1, 16, stride=2), :] = spread2[16 * c : 16 * c + 16]
    for x in range(4, 14):
        c = (x + 5) // 2 - 4
        v1b[x] = v1b[x] + jnp.concatenate([e1[c, 12:28], e1[c, 4:12]], axis=0)
    sweep(v1b, v1a, f1, ops1, 5, 13, 8)
    sweep(v1a, v1b, f1, ops1, 6, 12, 6)

    e0 = s["e0"]
    for c in range(6):
        e0[c, pl.ds(0, 24, stride=2), :] = v1b[6 + c]
        e0[c, pl.ds(1, 24, stride=2), :] = v1b[6 + c]
    row8 = iota((8, 128), 0)
    parts = []
    for c in range(6):
        parts += [e0[c, 0:16], jnp.where(row8 < 4, e0[c, 16:24], e0[c, 40:48])]
    spread1 = dot01(jnp.concatenate(parts, axis=0), s["p10"][...])
    stay.wait()
    arrive(in_vd)
    merge0("hd", vd, 2)
    for x in range(1, 13):
        c = (x + 11) // 2 - 6
        ve[x] = vd[x] + spread1[24 * c : 24 * c + 24]
    sweep(ve, vb, g0, ops0, 2, 12, 10)

    def last(x):
        v = vb[x + 3] + ops0[3][x + 3] * res_at(vb, g0, ops0, x + 3)
        out[x] = v[0:16]

    each(0, 8, 8, last)
    drain()


def scratch_list():
    def vmem(*shape, kind=F32):
        return pltpu.VMEM(shape, kind)

    made = [("mat", vmem(8, 16, 256, kind=jnp.int32))]
    for name in ("k0", "va", "vb", "vc", "vd", "ve", "src", "g0", "cx0", "cy0", "cz0", "w0"):
        made.append((name, vmem(14, 24, 256)))
    for name in ("k1", "f1", "v1a", "v1b", "cx1", "cy1", "cz1", "w1"):
        made.append((name, vmem(18, 24, 128)))
    for name in ("k2", "f2", "v2a", "v2b", "cx2", "cy2", "cz2", "w2"):
        made.append((name, vmem(14, 16, 128)))
    for name in ("x2k", "x2f"):
        made.append((name, vmem(14, 5, 4, 128)))
    for name in ("hk", "hv", "hs", "hd"):
        made.append((name + "_e", vmem(8, 8, 256)))
        made.append((name + "_b", vmem(14, 8, 256)))
    made.append(("f2l", vmem(6, 8, 128)))
    made.append(("near", vmem(6, 8, 8, 128)))
    for name in ("ka", "fa"):
        made.append((name, vmem(N, 2, 128)))
    for name in ("kb", "fb"):
        made.append((name, vmem(4, N, 2, 128)))
    for name in ("kt", "ft"):
        made.append((name, vmem(2, 128)))
    for name in ("ks", "fs"):
        made.append((name, vmem(4, 2, 128)))
    made.append(("t0", vmem(4, 2, 16, 128)))
    made.append(("t1", vmem(6, 24, 128)))
    made.append(("t2", vmem(1, 8, 128)))
    made.append(("e3", vmem(4, 8, 128)))
    made.append(("e2", vmem(7, 16, 128)))
    made.append(("e1", vmem(6, 32, 128)))
    made.append(("e0", vmem(6, 48, 128)))
    made.append(("low3", vmem(4, 8, 32, 128)))
    made.append(("low4", vmem(2, 8, 32, 128)))
    made.append(("low5", vmem(1, 8, 32, 128)))
    made.append(("m6", vmem(32, 128)))
    made.append(("inv", vmem(2, 128, 512, kind=BF16)))
    for name, shape in (("r01", (256, 128)), ("r12", (128, 128)), ("r23", (128, 128)), ("p32", (128, 128)), ("p21", (128, 128)), ("p10", (128, 256)), ("sel", (128, 128)), ("spr", (128, 512))):
        made.append((name, vmem(*shape, kind=BF16)))
    made.append(("load", pltpu.SemaphoreType.DMA((3,))))
    groups = {"hk": 8, "hv": 8, "hs": 8, "hd": 8, "h1k": 14, "h1f": 14, "ka": 15, "kb": 15, "fa": 15, "fb": 15, "k2a": 6, "f2a": 6, "k2b": 4, "f2b": 4}
    for name, count in groups.items():
        made.append((name + "_s", pltpu.SemaphoreType.DMA((count,))))
        made.append((name + "_r", pltpu.SemaphoreType.DMA((count,))))
    return made


SCRATCH = scratch_list()


def shards(concentration, source, material):
    return pl.pallas_call(
        kernel,
        out_shape=jax.ShapeDtypeStruct(concentration.shape, F32),
        in_specs=[pl.BlockSpec(memory_space=pltpu.HBM)] * 3,
        out_specs=pl.BlockSpec(memory_space=pltpu.VMEM),
        scratch_shapes=[shape for _, shape in SCRATCH],
        compiler_params=pltpu.CompilerParams(collective_id=0, has_side_effects=True, vmem_limit_bytes=56360960),
        cost_estimate=pl.CostEstimate(flops=20_000_000, bytes_accessed=1_000_000, transcendentals=0),
        name="vcycle",
    )(concentration, source, material)


def solution(mesh):
    placed = P("tx", "ty", None)
    return jax.shard_map(shards, mesh=mesh, in_specs=(placed,) * 3, out_specs=placed, check_vma=False)
```

```python
import jax
import jax.numpy as jnp
from jax import lax
from jax.experimental import pallas as pl
from jax.experimental.pallas import tpu as pltpu
from jax.sharding import PartitionSpec as P

MESH = pl.DeviceIdType.MESH
F32 = jnp.float32
BF16 = jnp.bfloat16
RATE = 0.001
RELAX = 0.8
TABLE = (0.15, 0.3, 0.5, 0.8, 1.2, 2.0, 3.2, 5.0)
N = 16


def iota(shape, axis):
    return lax.broadcasted_iota(jnp.int32, shape, axis)


def roll(v, shift, axis):
    return pltpu.roll(v, shift % v.shape[axis], axis)


def dot01(v, m):
    hi = v.astype(BF16)
    low = (v - hi.astype(F32)).astype(BF16)
    rows = len(v)
    if rows % 16 == 0:
        both = jnp.dot(jnp.concatenate([hi, low], axis=0), m, preferred_element_type=F32)
        return both[:rows] + both[rows:]
    return jnp.dot(hi, m, preferred_element_type=F32) + jnp.dot(low, m, preferred_element_type=F32)


def each(low, high, unroll, body):
    count = high - low
    whole = count // unroll
    if whole > 1:

        def step(i, carry):
            for k in range(unroll):
                body(low + i * unroll + k)
            return carry

        lax.fori_loop(0, whole, step, 0)
        rest = low + whole * unroll
    else:
        rest = low
    for x in range(rest, high):
        body(x)


def make_ops(kappa, ops, scale, layers, unroll):
    cx, cy, cz, w = ops
    half = 0.5 * scale

    def couple(x):
        k = kappa[x]
        cx[x] = half * (k + kappa[x + 1])
        cy[x] = half * (k + roll(k, -1, 0))
        cz[x] = half * (k + roll(k, -1, 1))

    def weigh(x):
        a, b = cy[x], cz[x]
        diag = (RATE + cx[x] + cx[x - 1]) + (a + roll(a, 1, 0)) + (b + roll(b, 1, 1))
        w[x] = RELAX / diag

    each(0, layers - 1, unroll, couple)
    each(1, layers - 1, unroll, weigh)


def residual(v, below, above, g, cx, cxm, cy, cz):
    fy = cy * (roll(v, -1, 0) - v)
    fz = cz * (roll(v, -1, 1) - v)
    r = (g - RATE * v) + (cx * (above - v) - cxm * (v - below))
    return r + (fy - roll(fy, 1, 0)) + (fz - roll(fz, 1, 1))


def res_at(v, g, ops, x):
    cx, cy, cz, _ = ops
    return residual(v[x], v[x - 1], v[x + 1], g[x], cx[x], cx[x - 1], cy[x], cz[x])


def sweep(v, out, g, ops, low, high, unroll):
    def body(x):
        out[x] = v[x] + ops[3][x] * res_at(v, g, ops, x)

    each(low, high, unroll, body)


def x_hi_next(v):
    lane = iota(v.shape, 1)
    return jnp.where(lane % 4 == 3, roll(v, 3, 1), roll(v, -1, 1))


def x_hi_prev(v):
    lane = iota(v.shape, 1)
    return jnp.where(lane % 4 == 0, roll(v, -3, 1), roll(v, 1, 1))


def low_couple(kappa, s, scale):
    half = 0.5 * scale
    nxt = kappa[1:] + [x_hi_next(kappa[0])]
    cx = [half * (k + n) for k, n in zip(kappa, nxt)]
    cxm = [x_hi_prev(cx[-1])] + cx[:-1]
    made = []
    for k, a, am in zip(kappa, cx, cxm):
        b, c = half * (k + roll(k, -s, 0)), half * (k + roll(k, -4 * s, 1))
        bm, cm = roll(b, s, 0), roll(c, 4 * s, 1)
        diag = (RATE + a + am) + (b + bm) + (c + cm)
        w = RELAX / diag
        made.append([w * a, w * am, w * b, w * bm, w * c, w * cm, w, diag * (1.0 / RELAX)])
    return made


def low_step(v, wg, ops, s):
    nxt = v[1:] + [x_hi_next(v[0])]
    prv = [x_hi_prev(v[-1])] + v[:-1]
    out = []
    for u, n, p, f, o in zip(v, nxt, prv, wg, ops):
        along_x = o[0] * n + o[1] * p
        along_y = o[2] * roll(u, -s, 0) + o[3] * roll(u, s, 0)
        along_z = o[4] * roll(u, -4 * s, 1) + o[5] * roll(u, 4 * s, 1)
        out.append((along_x + along_y) + (along_z + (f - RELAX * u)))
    return out


def low_sweep(v, wg, ops, s):
    return [u + d for u, d in zip(v, low_step(v, wg, ops, s))]


def low_restrict(v, s):
    if len(v) > 1:
        v = [v[2 * k] + v[2 * k + 1] for k in range(len(v) // 2)]
    else:
        u = v[0]
        lane = iota(u.shape, 1)
        v = [u + jnp.where(lane % 2 == 0, roll(u, -1, 1), roll(u, 1, 1))]
    out = []
    for u in v:
        row, lane = iota(u.shape, 0), iota(u.shape, 1)
        u = u + jnp.where((row // s) % 2 == 0, roll(u, -s, 0), roll(u, s, 0))
        u = u + jnp.where((lane // (4 * s)) % 2 == 0, roll(u, -4 * s, 1), roll(u, 4 * s, 1))
        out.append(u * 0.125)
    return out


def pack_six(v):
    lane = iota((8, 128), 1)
    y = (lane % 32) // 4
    out = v[24:32]
    for k in (2, 1, 0):
        out = jnp.where(y == k, v[8 * k : 8 * k + 8], out)
    return out


def kernel(conc, source, material, out, *scratch):
    names = [name for name, _ in SCRATCH]
    s = dict(zip(names, scratch))
    ops0, ops1, ops2 = [[s[f"{name}{level}"] for name in ("cx", "cy", "cz", "w")] for level in (0, 1, 2)]
    me_x, me_y = lax.axis_index("tx"), lax.axis_index("ty")

    def device(dx, dy):
        return (lax.rem(me_x + (dx + N), N), lax.rem(me_y + (dy + N), N))

    counter = {}

    def copy(group, src, dst, dx, dy):
        k = counter.get(group, 0)
        counter[group] = k + 1
        c = pltpu.make_async_remote_copy(
            src, dst, s[group + "_s"].at[k], s[group + "_r"].at[k], device_id=device(dx, dy), device_id_type=MESH
        )
        c.start()
        return c

    sent = []

    def arrive(copies):
        for c in copies:
            c.wait_recv()
        sent.extend(copies)

    def drain():
        for c in sent:
            c.wait_send()
        sent.clear()

    tile0 = (slice(3, 11), slice(0, 16))
    loads = [
        pltpu.make_async_copy(material, s["mat"], s["load"].at[0]),
        pltpu.make_async_copy(conc, s["va"].at[3:11, 0:16], s["load"].at[1]),
        pltpu.make_async_copy(source, s["src"].at[3:11, 0:16], s["load"].at[2]),
    ]
    barrier = pltpu.get_barrier_semaphore()
    peers = [(d, 0) for d in range(1, N)] + [(0, d) for d in range(1, N)]
    peers += [(a, b) for a in (-2, -1, 1, 2) for b in (-1, 1)]
    peers.sort(key=lambda p: -min(p[0] % N, -p[0] % N) - min(p[1] % N, -p[1] % N))
    for p in peers:
        pl.semaphore_signal(barrier, inc=1, device_id=device(*p), device_id_type=MESH)
    for c in loads:
        c.start()

    loads[0].wait()
    k0 = s["k0"]

    def lookup(x):
        m = s["mat"][x]
        result = jnp.zeros(m.shape, F32)
        for slot, value in enumerate(TABLE):
            result = jnp.where(m == slot, F32(value), result)
        k0[x + 3, 0:16] = result

    each(0, 8, 8, lookup)
    loads[1].wait()
    loads[2].wait()
    def halo0(group, ref, dest, w, c):
        edge, below = s[group + "_e"], s[group + "_b"]
        copies = []
        for dx, dy in ((1, 0), (-1, 0), (0, 1), (0, -1), (1, 1), (1, -1), (-1, 1), (-1, -1)):
            n = c if dy else w
            x0, x1 = {0: (3, 11), -1: (3, 3 + n), 1: (11 - n, 11)}[dx]
            y0, y1 = x0 - 8 * dx, x1 - 8 * dx
            if dy == 0:
                copies.append(copy(group, ref.at[x0:x1, 0:16], dest.at[y0:y1, 0:16], dx, dy))
            elif dy < 0:
                copies.append(copy(group, ref.at[x0:x1, 0:w], dest.at[y0:y1, 16 : 16 + w], dx, dy))
            else:
                copies.append(copy(group, edge.at[x0 - 3 : x1 - 3, 0:w], below.at[y0:y1, 0:w], dx, dy))
        return copies

    def edges0(group, ref, w):
        for x in range(8):
            s[group + "_e"][x] = roll(ref[x + 3, 8:16], w, 0)

    edges0("hk", k0, 3)
    edges0("hv", s["va"], 3)
    edges0("hs", s["src"], 2)
    pl.semaphore_wait(barrier, len(peers))

    def merge0(group, dest, w, layers=range(14)):
        below = s[group + "_b"]
        row = iota((8, 256), 0)
        for x in layers:
            dest[x, 16:24] = jnp.where(row < 4, dest[x, 16:24], roll(below[x], -w, 0))

    in_k0 = halo0("hk", k0, k0, 3, 2)
    in_va = halo0("hv", s["va"], s["va"], 3, 2)
    in_src = halo0("hs", s["src"], s["src"], 2, 1)

    def matrix(name, rule):
        shape = s[name].shape
        s[name][...] = jnp.where(rule(iota(shape, 0), iota(shape, 1)), 1.0, 0.0).astype(BF16)

    matrix("r01", lambda i, j: i // 2 == j)
    matrix("r12", lambda i, j: i // 2 == j % 64)
    matrix("r23", lambda i, j: i // 2 == j // 4)

    t0, t1, t2 = s["t0"], s["t1"], s["t2"]

    def put0(c, pair):
        t0[c, 0] = pair[:16, :128]
        t0[c, 1] = pair[:16, 128:]

    def take0():
        rows = []
        for c in range(4):
            halves = [t0[c, h, pl.ds(0, 8, stride=2), :] + t0[c, h, pl.ds(1, 8, stride=2), :] for h in range(2)]
            rows.append(jnp.concatenate(halves, axis=1))
        return dot01(jnp.concatenate(rows, axis=0), s["r01"][...]) * 0.125

    def row_pairs(ref, k, start, count):
        return ref[k, pl.ds(start, count, stride=2), :] + ref[k, pl.ds(start + 1, count, stride=2), :]

    k1, k2, x2k, x2f = s["k1"], s["k2"], s["x2k"], s["x2f"]
    for c in range(4):
        put0(c, k0[3 + 2 * c, 0:16] + k0[4 + 2 * c, 0:16])
    tile = take0()
    for c in range(4):
        k1[7 + c, 0:8] = tile[8 * c : 8 * c + 8]

    def halo1(group, ref, w):
        copies = []
        for dx, dy in ((2, 1), (2, -1), (-2, 1), (-2, -1), (1, 1), (1, -1), (-1, 1), (-1, -1), (0, 1), (0, -1), (2, 0), (-2, 0), (1, 0), (-1, 0)):
            nx = {0: 4, 1: 4, 2: w - 4 if dy == 0 else w - 5}[abs(dx)]
            ny = 8 if dy == 0 else {0: w, 1: w - 1, 2: w - 5}[abs(dx)]
            xs = slice(11 - nx, 11) if dx > 0 else slice(7, 7 + nx)
            xd = slice(xs.start - 4 * dx, xs.stop - 4 * dx)
            ys = slice(0, 8) if dy > 0 else slice(0, ny)
            yd = slice(16, 24) if dy > 0 else slice(-8 * dy, ny - 8 * dy)
            copies.append(copy(group, ref.at[xs, ys], ref.at[xd, yd], dx, dy))
        return copies

    def to_level2(get):
        parts = []
        for c in range(len(get) // 2):
            pair = get[2 * c] + get[2 * c + 1]
            if len(pair) == 8:
                t1[c, 4:12] = pair
            else:
                t1[c] = roll(pair, 4, 0)
        for c in range(len(get) // 2):
            parts.append(row_pairs(t1, c, 0, 8))
        return dot01(jnp.concatenate(parts, axis=0), s["r12"][...]) * 0.125

    def to_level3(pair, row0):
        t2[0] = dot01(pair, s["r23"][...]) * 0.125
        return row_pairs(t2, 0, row0, 2)

    low = to_level2([tile[8 * c : 8 * c + 8] for c in range(4)])
    for c in range(2):
        x2k[6 + c, 2] = low[8 * c + 2 : 8 * c + 6]
    base = to_level3(low[0:8] + low[8:16], 2)

    def ring_x(group, ref, tile_ref, value):
        tile_ref[...] = value
        ref[me_x] = value
        return [copy(group, tile_ref, ref.at[me_x], d, 0) for d in (4, 12, 3, 5, 11, 13, 2, 6, 10, 14, 8, 7, 9, 1, 15)]

    def window_x(group, ref):
        return [
            copy(group, ref.at[6:8, 2], ref.at[6 - 2 * d : 8 - 2 * d, 2], d, 0) for d in (1, -1, 2, -2, 3, -3)
        ]

    def slab(ref):
        lane = iota((2, 128), 1)
        out_parts = []
        for k in range(4):
            v = ref[12 + k]
            for h in (2, 1, 0):
                v = jnp.where(lane % 4 == h, ref[4 * h + k], v)
            out_parts.append(v)
        return out_parts

    def ring_y(group, ref, slab_ref, parts):
        for k in range(4):
            slab_ref[k] = parts[k]
            ref[k, me_y] = parts[k]
        return [copy(group, slab_ref, ref.at[:, me_y], 0, d) for d in (12, 4, 5, 11, 13, 3, 10, 6, 8, 14, 2, 7, 9, 15, 1)]

    def window_y(group, ref):
        return [copy(group, ref.at[:, 2], ref.at[:, 2 - d], 0, d) for d in (1, -1, 2, -2)]

    def window(ref, dest):
        for x in range(14):
            dest[x] = ref[x].reshape(20, 128)[2:18]

    in_ka = ring_x("ka", s["ka"], s["kt"], base)
    in_k2a = window_x("k2a", x2k)
    matrix("p32", lambda i, j: i // 4 == (j % 64) // 2)
    matrix("p21", lambda i, j: i == j // 2)
    matrix("p10", lambda i, j: i == j // 2)
    matrix("sel", lambda i, j: ((i % 32) // 4 < 4) & (i % 2 == 0) & (j == ((i % 32) // 4) * 8 + (i // 32) * 2 + (i % 4) // 2))
    matrix("spr", lambda i, j: i == (j // 128) * 8 + ((j % 128) // 32) * 2 + (j % 4) // 2)

    arrive(in_k0)
    merge0("hk", k0, 3)
    make_ops(k0, ops0, 1.0, 14, 13)
    in_k1 = halo1("h1k", k1, 7)
    arrive(in_va[2:4])
    arrive(in_src[2:4])
    merge0("hv", s["va"], 3, range(3, 11))
    merge0("hs", s["src"], 2, range(3, 11))
    va, vb, vc, vd, ve, src, g0 = [s[name] for name in ("va", "vb", "vc", "vd", "ve", "src", "g0")]

    def force(x):
        g0[x] = RATE * va[x] + src[x]

    each(3, 11, 8, force)
    sweep(va, vb, g0, ops0, 4, 10, 6)
    arrive(in_va[:2] + in_va[4:])
    arrive(in_src[:2] + in_src[4:])
    merge0("hv", va, 3, (0, 1, 2, 11, 12, 13))
    merge0("hs", src, 2, (1, 2, 11, 12))
    for x in (1, 2, 11, 12):
        force(x)
    sweep(va, vb, g0, ops0, 1, 4, 3)
    sweep(va, vb, g0, ops0, 10, 13, 3)
    sweep(vb, vc, g0, ops0, 2, 12, 10)

    def down0(c):
        put0(c, res_at(vc, g0, ops0, 2 * c + 3) + res_at(vc, g0, ops0, 2 * c + 4))

    each(0, 4, 4, down0)
    tile = take0()
    f1 = s["f1"]
    for c in range(4):
        f1[7 + c, 0:8] = tile[8 * c : 8 * c + 8]
    in_f1 = halo1("h1f", f1, 6)

    arrive(in_k2a)
    in_k2b = window_y("k2b", x2k)
    arrive(in_ka)
    in_kb = ring_y("kb", s["kb"], s["ks"], slab(s["ka"]))
    stay = pltpu.make_async_copy(vc.at[tile0], vd.at[tile0], s["load"].at[0])
    stay.start()
    edges0("hd", vc, 2)
    in_vd = halo0("hd", vc, vd, 2, 1)

    arrive(in_k1)
    make_ops(k1, ops1, 0.25, 18, 17)
    arrive(in_k2b)
    window(x2k, k2)
    make_ops(k2, ops2, 0.0625, 14, 13)
    near = s["near"]
    for c in range(6):
        a, am, b, d, w = [ref[x, 4:12] for ref, x in zip((ops2[0], ops2[0], ops2[1], ops2[2], ops2[3]), (c + 4, c + 3, c + 4, c + 4, c + 4))]
        bm, dm = roll(b, 1, 0), roll(d, 1, 1)
        diag = (RATE + a + am) + (b + bm) + (d + dm)
        for number, value in enumerate((w * a, w * am, w * b, w * bm, w * d, w * dm, w, diag * (1.0 / RELAX))):
            near[c, number] = value
    arrive(in_f1)

    v1a, v1b = s["v1a"], s["v1b"]

    def start1(x):
        v1a[x] = ops1[3][x] * f1[x]

    each(1, 17, 16, start1)
    sweep(v1a, v1b, f1, ops1, 2, 16, 14)
    low = to_level2([res_at(v1b, f1, ops1, x) for x in range(3, 15)])
    f2l = s["f2l"]
    f2 = s["f2"]
    for c in range(6):
        f2l[c] = low[8 * c : 8 * c + 8]
    for c in range(2):
        x2f[6 + c, 2] = low[8 * c + 18 : 8 * c + 22]

    v2a, v2b = s["v2a"], s["v2b"]
    vl = [near[c, 6] * f2l[c] for c in range(6)]

    def step_near(v, c):
        o, u = [near[c, number] for number in range(6)], v[c]
        along_x = o[0] * v[c + 1] + o[1] * v[c - 1]
        along_y = o[2] * roll(u, -1, 0) + o[3] * roll(u, 1, 0)
        along_z = o[4] * roll(u, -1, 1) + o[5] * roll(u, 1, 1)
        return (along_x + along_y) + (along_z + (vl[c] - RELAX * u))

    ul = [None] + [vl[c] + step_near(vl, c) for c in range(1, 5)] + [None]
    base = to_level3(near[2, 7] * step_near(ul, 2) + near[3, 7] * step_near(ul, 3), 2)
    in_fa = ring_x("fa", s["fa"], s["ft"], base)
    in_f2a = window_x("f2a", x2f)

    arrive(in_kb)
    kap3 = [s["kb"][k].reshape(32, 128) for k in range(4)]
    kap4 = low_restrict(kap3, 1)
    kap5 = low_restrict(kap4, 2)
    kap6 = low_restrict(kap5, 4)[0]
    for level, kap, spread in ((3, kap3, 1), (4, kap4, 2), (5, kap5, 4)):
        made = low_couple(kap, spread, 1.0 / 4.0**level)
        for k in range(len(kap)):
            for number in range(8):
                s[f"low{level}"][k, number] = made[k][number]

    krow = dot01(pack_six(kap6), s["sel"][...])[0:1]
    q, p = iota((32, 128), 0), iota((32, 128), 1)
    kcol = jnp.sum(jnp.where(q == p, krow, 0.0), axis=1, keepdims=True)
    dy, dz, same_x = (q // 8 - p // 8 + 4) % 4, ((q % 8) // 2 - (p % 8) // 2 + 4) % 4, q % 2 == p % 2
    links = jnp.where(same_x & (dz == 0) & (dy % 2 == 1), 1.0, 0.0) + jnp.where(same_x & (dy == 0) & (dz % 2 == 1), 1.0, 0.0)
    links = links + jnp.where((dz == 0) & (dy == 0) & (q % 2 != p % 2), 2.0, 0.0)
    links = jnp.where(p < 32, links, 0.0)
    off = (0.5 / 4096.0) * links * (krow + kcol)
    diag = RATE + jnp.sum(off, axis=1, keepdims=True)
    m_ref = s["m6"]
    m_ref[...] = jnp.where(q == p, diag, jnp.where(p == q + 32, 1.0, -off))

    def eliminate(k, carry):
        m = m_ref[...]
        pivot_row = m_ref[pl.ds(k, 1), :]
        column = jnp.sum(jnp.where(p == k, m, 0.0), axis=1, keepdims=True)
        pivot = jnp.sum(jnp.where(iota((1, 128), 1) == k, pivot_row, 0.0), axis=1, keepdims=True)
        scaled = pivot_row / pivot
        m_ref[...] = jnp.where(q == k, scaled, m - column * scaled)
        return carry

    lax.fori_loop(0, 16, eliminate, 0)

    arrive(in_fa)
    in_fb = ring_y("fb", s["fb"], s["fs"], slab(s["fa"]))
    arrive(in_f2a)
    in_f2b = window_y("f2b", x2f)
    lax.fori_loop(16, 32, eliminate, 0)
    inverse = roll(m_ref[...], -32, 1)
    inverse = jnp.concatenate([jnp.where(p < 32, inverse, 0.0), jnp.zeros((96, 128), F32)], axis=0)
    inverse = dot01(inverse, s["spr"][...])
    hi = inverse.astype(BF16)
    rest = inverse - hi.astype(F32)
    mid = rest.astype(BF16)
    pieces = (hi, mid, (rest - mid.astype(F32)).astype(BF16))
    a, b, c = [jnp.dot(s["sel"][...], piece, preferred_element_type=F32) for piece in pieces]
    inverse = a + (b + c)
    hi = inverse.astype(BF16)
    s["inv"][0] = hi
    s["inv"][1] = (inverse - hi.astype(F32)).astype(BF16)

    drain()

    def low_ops(level, count):
        return [[s[f"low{level}"][k, number] for number in range(8)] for k in range(count)]

    arrive(in_fb)
    g3 = [s["fb"][k].reshape(32, 128) for k in range(4)]
    o3, o4, o5 = low_ops(3, 4), low_ops(4, 2), low_ops(5, 1)

    def down(g, o, spread):
        wg = [q[6] * f for q, f in zip(o, g)]
        v = low_sweep(wg, wg, o, spread)
        step = low_step(v, wg, o, spread)
        return v, wg, low_restrict([q[7] * d for q, d in zip(o, step)], spread)

    v3, wg3, g4 = down(g3, o3, 1)
    v4, wg4, g5 = down(g4, o4, 2)
    v5, wg5, g6 = down(g5, o5, 4)
    x6 = pack_six(g6[0])
    hi = x6.astype(BF16).astype(F32)
    both = jnp.concatenate([hi, x6 - hi], axis=0).astype(BF16)
    large = jnp.dot(both, s["inv"][0], preferred_element_type=F32)
    x6 = large[:8] + (large[8:] + jnp.dot(both, s["inv"][1], preferred_element_type=F32)[:8])
    x6 = jnp.concatenate([x6[:, 128 * k : 128 * k + 128] for k in range(4)], axis=0)

    def up(v, e, wg, o, spread):
        v = [u + e[k * len(e) // len(v)] for k, u in enumerate(v)]
        return low_sweep(low_sweep(v, wg, o, spread), wg, o, spread)

    v5 = up(v5, [x6], wg5, o5, 4)
    v4 = up(v4, v5, wg4, o4, 2)
    v3 = up(v3, v4, wg3, o3, 1)

    e3, e2, e1 = s["e3"], s["e2"], s["e1"]
    turn = lax.rem(2 * N - 2 * me_y + 3, 2 * N)
    for k in range(4):
        e3[k] = pltpu.roll(v3[k], turn, 0)[0:8]
    picks = []
    lane8 = iota((8, 128), 1)
    for d in range(-2, 3):
        x = lax.rem(me_x + (d + N), N)
        picks.append(jnp.where(lane8 % 4 == x // 4, e3[lax.rem(x, 4)], 0.0))
    spread3 = dot01(jnp.concatenate(picks, axis=0), s["p32"][...])
    for c in range(5):
        e2[c + 1, pl.ds(0, 8, stride=2), :] = spread3[8 * c : 8 * c + 8]
        e2[c + 1, pl.ds(1, 8, stride=2), :] = spread3[8 * c : 8 * c + 8]

    arrive(in_f2b)
    window(x2f, f2)
    for x in range(1, 13):
        v2a[x] = ops2[3][x] * f2[x]
    sweep(v2a, v2b, f2, ops2, 2, 12, 10)
    for x in range(2, 12):
        v2b[x] = v2b[x] + e2[x // 2]
    sweep(v2b, v2a, f2, ops2, 3, 11, 8)
    sweep(v2a, v2b, f2, ops2, 4, 10, 6)

    spread2 = dot01(jnp.concatenate([v2b[x] for x in range(4, 10)], axis=0), s["p21"][...])
    for c in range(6):
        e1[c, pl.ds(0, 16, stride=2), :] = spread2[16 * c : 16 * c + 16]
        e1[c, pl.ds(1, 16, stride=2), :] = spread2[16 * c : 16 * c + 16]
    for x in range(4, 14):
        c = (x + 5) // 2 - 4
        v1b[x] = v1b[x] + jnp.concatenate([e1[c, 12:28], e1[c, 4:12]], axis=0)
    sweep(v1b, v1a, f1, ops1, 5, 13, 8)
    sweep(v1a, v1b, f1, ops1, 6, 12, 6)

    e0 = s["e0"]
    for c in range(6):
        e0[c, pl.ds(0, 24, stride=2), :] = v1b[6 + c]
        e0[c, pl.ds(1, 24, stride=2), :] = v1b[6 + c]
    row8 = iota((8, 128), 0)
    parts = []
    for c in range(6):
        parts += [e0[c, 0:16], jnp.where(row8 < 4, e0[c, 16:24], e0[c, 40:48])]
    spread1 = dot01(jnp.concatenate(parts, axis=0), s["p10"][...])
    stay.wait()
    arrive(in_vd)
    merge0("hd", vd, 2)
    for x in range(1, 13):
        c = (x + 11) // 2 - 6
        ve[x] = vd[x] + spread1[24 * c : 24 * c + 24]
    sweep(ve, vb, g0, ops0, 2, 12, 10)

    def last(x):
        v = vb[x + 3] + ops0[3][x + 3] * res_at(vb, g0, ops0, x + 3)
        out[x] = v[0:16]

    each(0, 8, 8, last)
    drain()


def scratch_list():
    def vmem(*shape, kind=F32):
        return pltpu.VMEM(shape, kind)

    made = [("mat", vmem(8, 16, 256, kind=jnp.int32))]
    for name in ("k0", "va", "vb", "vc", "vd", "ve", "src", "g0", "cx0", "cy0", "cz0", "w0"):
        made.append((name, vmem(14, 24, 256)))
    for name in ("k1", "f1", "v1a", "v1b", "cx1", "cy1", "cz1", "w1"):
        made.append((name, vmem(18, 24, 128)))
    for name in ("k2", "f2", "v2a", "v2b", "cx2", "cy2", "cz2", "w2"):
        made.append((name, vmem(14, 16, 128)))
    for name in ("x2k", "x2f"):
        made.append((name, vmem(14, 5, 4, 128)))
    for name in ("hk", "hv", "hs", "hd"):
        made.append((name + "_e", vmem(8, 8, 256)))
        made.append((name + "_b", vmem(14, 8, 256)))
    made.append(("f2l", vmem(6, 8, 128)))
    made.append(("near", vmem(6, 8, 8, 128)))
    for name in ("ka", "fa"):
        made.append((name, vmem(N, 2, 128)))
    for name in ("kb", "fb"):
        made.append((name, vmem(4, N, 2, 128)))
    for name in ("kt", "ft"):
        made.append((name, vmem(2, 128)))
    for name in ("ks", "fs"):
        made.append((name, vmem(4, 2, 128)))
    made.append(("t0", vmem(4, 2, 16, 128)))
    made.append(("t1", vmem(6, 24, 128)))
    made.append(("t2", vmem(1, 8, 128)))
    made.append(("e3", vmem(4, 8, 128)))
    made.append(("e2", vmem(7, 16, 128)))
    made.append(("e1", vmem(6, 32, 128)))
    made.append(("e0", vmem(6, 48, 128)))
    made.append(("low3", vmem(4, 8, 32, 128)))
    made.append(("low4", vmem(2, 8, 32, 128)))
    made.append(("low5", vmem(1, 8, 32, 128)))
    made.append(("m6", vmem(32, 128)))
    made.append(("inv", vmem(2, 128, 512, kind=BF16)))
    for name, shape in (("r01", (256, 128)), ("r12", (128, 128)), ("r23", (128, 128)), ("p32", (128, 128)), ("p21", (128, 128)), ("p10", (128, 256)), ("sel", (128, 128)), ("spr", (128, 512))):
        made.append((name, vmem(*shape, kind=BF16)))
    made.append(("load", pltpu.SemaphoreType.DMA((3,))))
    groups = {"hk": 8, "hv": 8, "hs": 8, "hd": 8, "h1k": 14, "h1f": 14, "ka": 15, "kb": 15, "fa": 15, "fb": 15, "k2a": 6, "f2a": 6, "k2b": 4, "f2b": 4}
    for name, count in groups.items():
        made.append((name + "_s", pltpu.SemaphoreType.DMA((count,))))
        made.append((name + "_r", pltpu.SemaphoreType.DMA((count,))))
    return made


SCRATCH = scratch_list()


def shards(concentration, source, material):
    return pl.pallas_call(
        kernel,
        out_shape=jax.ShapeDtypeStruct(concentration.shape, F32),
        in_specs=[pl.BlockSpec(memory_space=pltpu.HBM)] * 3,
        out_specs=pl.BlockSpec(memory_space=pltpu.VMEM),
        scratch_shapes=[shape for _, shape in SCRATCH],
        compiler_params=pltpu.CompilerParams(collective_id=0, has_side_effects=True, vmem_limit_bytes=56360960),
        cost_estimate=pl.CostEstimate(flops=20_000_000, bytes_accessed=1_000_000, transcendentals=0),
        name="vcycle",
    )(concentration, source, material)


def solution(mesh):
    placed = P("tx", "ty", None)
    return jax.shard_map(shards, mesh=mesh, in_specs=(placed,) * 3, out_specs=placed, check_vma=False)
```

```python
import jax
import jax.numpy as jnp
from jax import lax
from jax.experimental import pallas as pl
from jax.experimental.pallas import tpu as pltpu
from jax.sharding import PartitionSpec as P

MESH = pl.DeviceIdType.MESH
F32 = jnp.float32
BF16 = jnp.bfloat16
RATE = 0.001
RELAX = 0.8
TABLE = (0.15, 0.3, 0.5, 0.8, 1.2, 2.0, 3.2, 5.0)
N = 16


def iota(shape, axis):
    return lax.broadcasted_iota(jnp.int32, shape, axis)


def roll(v, shift, axis):
    return pltpu.roll(v, shift % v.shape[axis], axis)


def dot01(v, m):
    hi = v.astype(BF16)
    low = (v - hi.astype(F32)).astype(BF16)
    rows = len(v)
    if rows % 16 == 0:
        both = jnp.dot(jnp.concatenate([hi, low], axis=0), m, preferred_element_type=F32)
        return both[:rows] + both[rows:]
    return jnp.dot(hi, m, preferred_element_type=F32) + jnp.dot(low, m, preferred_element_type=F32)


def each(low, high, unroll, body):
    count = high - low
    whole = count // unroll
    if whole > 1:

        def step(i, carry):
            for k in range(unroll):
                body(low + i * unroll + k)
            return carry

        lax.fori_loop(0, whole, step, 0)
        rest = low + whole * unroll
    else:
        rest = low
    for x in range(rest, high):
        body(x)


def make_ops(kappa, ops, scale, layers, unroll):
    cx, cy, cz, w = ops
    half = 0.5 * scale

    def couple(x):
        k = kappa[x]
        cx[x] = half * (k + kappa[x + 1])
        cy[x] = half * (k + roll(k, -1, 0))
        cz[x] = half * (k + roll(k, -1, 1))

    def weigh(x):
        a, b = cy[x], cz[x]
        diag = (RATE + cx[x] + cx[x - 1]) + (a + roll(a, 1, 0)) + (b + roll(b, 1, 1))
        w[x] = RELAX / diag

    each(0, layers - 1, unroll, couple)
    each(1, layers - 1, unroll, weigh)


def residual(v, below, above, g, cx, cxm, cy, cz):
    fy = cy * (roll(v, -1, 0) - v)
    fz = cz * (roll(v, -1, 1) - v)
    r = (g - RATE * v) + (cx * (above - v) - cxm * (v - below))
    return r + (fy - roll(fy, 1, 0)) + (fz - roll(fz, 1, 1))


def res_at(v, g, ops, x):
    cx, cy, cz, _ = ops
    return residual(v[x], v[x - 1], v[x + 1], g[x], cx[x], cx[x - 1], cy[x], cz[x])


def sweep(v, out, g, ops, low, high, unroll):
    def body(x):
        out[x] = v[x] + ops[3][x] * res_at(v, g, ops, x)

    each(low, high, unroll, body)


def x_hi_next(v):
    lane = iota(v.shape, 1)
    return jnp.where(lane % 4 == 3, roll(v, 3, 1), roll(v, -1, 1))


def x_hi_prev(v):
    lane = iota(v.shape, 1)
    return jnp.where(lane % 4 == 0, roll(v, -3, 1), roll(v, 1, 1))


def low_couple(kappa, s, scale):
    half = 0.5 * scale
    nxt = kappa[1:] + [x_hi_next(kappa[0])]
    cx = [half * (k + n) for k, n in zip(kappa, nxt)]
    cxm = [x_hi_prev(cx[-1])] + cx[:-1]
    made = []
    for k, a, am in zip(kappa, cx, cxm):
        b, c = half * (k + roll(k, -s, 0)), half * (k + roll(k, -4 * s, 1))
        bm, cm = roll(b, s, 0), roll(c, 4 * s, 1)
        diag = (RATE + a + am) + (b + bm) + (c + cm)
        w = RELAX / diag
        made.append([w * a, w * am, w * b, w * bm, w * c, w * cm, w, diag * (1.0 / RELAX)])
    return made


def low_step(v, wg, ops, s):
    nxt = v[1:] + [x_hi_next(v[0])]
    prv = [x_hi_prev(v[-1])] + v[:-1]
    out = []
    for u, n, p, f, o in zip(v, nxt, prv, wg, ops):
        along_x = o[0] * n + o[1] * p
        along_y = o[2] * roll(u, -s, 0) + o[3] * roll(u, s, 0)
        along_z = o[4] * roll(u, -4 * s, 1) + o[5] * roll(u, 4 * s, 1)
        out.append((along_x + along_y) + (along_z + (f - RELAX * u)))
    return out


def low_sweep(v, wg, ops, s):
    return [u + d for u, d in zip(v, low_step(v, wg, ops, s))]


def low_restrict(v, s):
    if len(v) > 1:
        v = [v[2 * k] + v[2 * k + 1] for k in range(len(v) // 2)]
    else:
        u = v[0]
        lane = iota(u.shape, 1)
        v = [u + jnp.where(lane % 2 == 0, roll(u, -1, 1), roll(u, 1, 1))]
    out = []
    for u in v:
        row, lane = iota(u.shape, 0), iota(u.shape, 1)
        u = u + jnp.where((row // s) % 2 == 0, roll(u, -s, 0), roll(u, s, 0))
        u = u + jnp.where((lane // (4 * s)) % 2 == 0, roll(u, -4 * s, 1), roll(u, 4 * s, 1))
        out.append(u * 0.125)
    return out


def pack_six(v):
    lane = iota((8, 128), 1)
    y = (lane % 32) // 4
    out = v[24:32]
    for k in (2, 1, 0):
        out = jnp.where(y == k, v[8 * k : 8 * k + 8], out)
    return out


def kernel(conc, source, material, out, *scratch):
    names = [name for name, _ in SCRATCH]
    s = dict(zip(names, scratch))
    ops0, ops1, ops2 = [[s[f"{name}{level}"] for name in ("cx", "cy", "cz", "w")] for level in (0, 1, 2)]
    me_x, me_y = lax.axis_index("tx"), lax.axis_index("ty")

    def device(dx, dy):
        return (lax.rem(me_x + (dx + N), N), lax.rem(me_y + (dy + N), N))

    counter = {}

    def copy(group, src, dst, dx, dy):
        k = counter.get(group, 0)
        counter[group] = k + 1
        c = pltpu.make_async_remote_copy(
            src, dst, s[group + "_s"].at[k], s[group + "_r"].at[k], device_id=device(dx, dy), device_id_type=MESH
        )
        c.start()
        return c

    sent = []

    def arrive(copies):
        for c in copies:
            c.wait_recv()
        sent.extend(copies)

    def drain():
        for c in sent:
            c.wait_send()
        sent.clear()

    tile0 = (slice(3, 11), slice(0, 16))
    loads = [
        pltpu.make_async_copy(material, s["mat"], s["load"].at[0]),
        pltpu.make_async_copy(conc, s["va"].at[3:11, 0:16], s["load"].at[1]),
        pltpu.make_async_copy(source, s["src"].at[3:11, 0:16], s["load"].at[2]),
    ]
    barrier = pltpu.get_barrier_semaphore()
    peers = [(d, 0) for d in range(1, N)] + [(0, d) for d in range(1, N)]
    peers += [(a, b) for a in (-2, -1, 1, 2) for b in (-1, 1)]
    peers.sort(key=lambda p: -min(p[0] % N, -p[0] % N) - min(p[1] % N, -p[1] % N))
    for p in peers:
        pl.semaphore_signal(barrier, inc=1, device_id=device(*p), device_id_type=MESH)
    for c in loads:
        c.start()

    loads[0].wait()
    k0 = s["k0"]

    def lookup(x):
        m = s["mat"][x]
        result = jnp.zeros(m.shape, F32)
        for slot, value in enumerate(TABLE):
            result = jnp.where(m == slot, F32(value), result)
        k0[x + 3, 0:16] = result

    each(0, 8, 8, lookup)
    loads[1].wait()
    loads[2].wait()
    def halo0(group, ref, dest, w, c):
        edge, below = s[group + "_e"], s[group + "_b"]
        copies = []
        for dx, dy in ((1, 0), (-1, 0), (0, 1), (0, -1), (1, 1), (1, -1), (-1, 1), (-1, -1)):
            n = c if dy else w
            x0, x1 = {0: (3, 11), -1: (3, 3 + n), 1: (11 - n, 11)}[dx]
            y0, y1 = x0 - 8 * dx, x1 - 8 * dx
            if dy == 0:
                copies.append(copy(group, ref.at[x0:x1, 0:16], dest.at[y0:y1, 0:16], dx, dy))
            elif dy < 0:
                copies.append(copy(group, ref.at[x0:x1, 0:w], dest.at[y0:y1, 16 : 16 + w], dx, dy))
            else:
                copies.append(copy(group, edge.at[x0 - 3 : x1 - 3, 0:w], below.at[y0:y1, 0:w], dx, dy))
        return copies

    def edges0(group, ref, w):
        for x in range(8):
            s[group + "_e"][x] = roll(ref[x + 3, 8:16], w, 0)

    edges0("hk", k0, 3)
    edges0("hv", s["va"], 3)
    edges0("hs", s["src"], 2)
    pl.semaphore_wait(barrier, len(peers))

    def merge0(group, dest, w, layers=range(14)):
        below = s[group + "_b"]
        row = iota((8, 256), 0)
        for x in layers:
            dest[x, 16:24] = jnp.where(row < 4, dest[x, 16:24], roll(below[x], -w, 0))

    in_k0 = halo0("hk", k0, k0, 3, 2)
    in_va = halo0("hv", s["va"], s["va"], 3, 2)
    in_src = halo0("hs", s["src"], s["src"], 2, 1)

    def matrix(name, rule):
        shape = s[name].shape
        s[name][...] = jnp.where(rule(iota(shape, 0), iota(shape, 1)), 1.0, 0.0).astype(BF16)

    matrix("r01", lambda i, j: i // 2 == j)
    matrix("r12", lambda i, j: i // 2 == j % 64)
    matrix("r23", lambda i, j: i // 2 == j // 4)

    t0, t1, t2 = s["t0"], s["t1"], s["t2"]

    def put0(c, pair):
        t0[c, 0] = pair[:16, :128]
        t0[c, 1] = pair[:16, 128:]

    def take0():
        rows = []
        for c in range(4):
            halves = [t0[c, h, pl.ds(0, 8, stride=2), :] + t0[c, h, pl.ds(1, 8, stride=2), :] for h in range(2)]
            rows.append(jnp.concatenate(halves, axis=1))
        return dot01(jnp.concatenate(rows, axis=0), s["r01"][...]) * 0.125

    def row_pairs(ref, k, start, count):
        return ref[k, pl.ds(start, count, stride=2), :] + ref[k, pl.ds(start + 1, count, stride=2), :]

    k1, k2, x2k, x2f = s["k1"], s["k2"], s["x2k"], s["x2f"]
    for c in range(4):
        put0(c, k0[3 + 2 * c, 0:16] + k0[4 + 2 * c, 0:16])
    tile = take0()
    for c in range(4):
        k1[7 + c, 0:8] = tile[8 * c : 8 * c + 8]

    def halo1(group, ref, w):
        copies = []
        for dx, dy in ((2, 1), (2, -1), (-2, 1), (-2, -1), (1, 1), (1, -1), (-1, 1), (-1, -1), (0, 1), (0, -1), (2, 0), (-2, 0), (1, 0), (-1, 0)):
            nx = {0: 4, 1: 4, 2: w - 4 if dy == 0 else w - 5}[abs(dx)]
            ny = 8 if dy == 0 else {0: w, 1: w - 1, 2: w - 5}[abs(dx)]
            xs = slice(11 - nx, 11) if dx > 0 else slice(7, 7 + nx)
            xd = slice(xs.start - 4 * dx, xs.stop - 4 * dx)
            ys = slice(0, 8) if dy > 0 else slice(0, ny)
            yd = slice(16, 24) if dy > 0 else slice(-8 * dy, ny - 8 * dy)
            copies.append(copy(group, ref.at[xs, ys], ref.at[xd, yd], dx, dy))
        return copies

    def to_level2(get):
        parts = []
        for c in range(len(get) // 2):
            pair = get[2 * c] + get[2 * c + 1]
            if len(pair) == 8:
                t1[c, 4:12] = pair
            else:
                t1[c] = roll(pair, 4, 0)
        for c in range(len(get) // 2):
            parts.append(row_pairs(t1, c, 0, 8))
        return dot01(jnp.concatenate(parts, axis=0), s["r12"][...]) * 0.125

    def to_level3(pair, row0):
        t2[0] = dot01(pair, s["r23"][...]) * 0.125
        return row_pairs(t2, 0, row0, 2)

    low = to_level2([tile[8 * c : 8 * c + 8] for c in range(4)])
    for c in range(2):
        x2k[6 + c, 2] = low[8 * c + 2 : 8 * c + 6]
    base = to_level3(low[0:8] + low[8:16], 2)

    def ring_x(group, ref, tile_ref, value):
        tile_ref[...] = value
        ref[me_x] = value
        return [copy(group, tile_ref, ref.at[me_x], d, 0) for d in (4, 12, 3, 5, 11, 13, 2, 6, 10, 14, 8, 7, 9, 1, 15)]

    def window_x(group, ref):
        return [
            copy(group, ref.at[6:8, 2], ref.at[6 - 2 * d : 8 - 2 * d, 2], d, 0) for d in (1, -1, 2, -2, 3, -3)
        ]

    def slab(ref):
        lane = iota((2, 128), 1)
        out_parts = []
        for k in range(4):
            v = ref[12 + k]
            for h in (2, 1, 0):
                v = jnp.where(lane % 4 == h, ref[4 * h + k], v)
            out_parts.append(v)
        return out_parts

    def ring_y(group, ref, slab_ref, parts):
        for k in range(4):
            slab_ref[k] = parts[k]
            ref[k, me_y] = parts[k]
        return [copy(group, slab_ref, ref.at[:, me_y], 0, d) for d in (12, 4, 5, 11, 13, 3, 10, 6, 8, 14, 2, 7, 9, 15, 1)]

    def window_y(group, ref):
        return [copy(group, ref.at[:, 2], ref.at[:, 2 - d], 0, d) for d in (1, -1, 2, -2)]

    def window(ref, dest):
        for x in range(14):
            dest[x] = ref[x].reshape(20, 128)[2:18]

    in_ka = ring_x("ka", s["ka"], s["kt"], base)
    in_k2a = window_x("k2a", x2k)
    matrix("p32", lambda i, j: i // 4 == (j % 64) // 2)
    matrix("p21", lambda i, j: i == j // 2)
    matrix("p10", lambda i, j: i == j // 2)
    matrix("sel", lambda i, j: ((i % 32) // 4 < 4) & (i % 2 == 0) & (j == ((i % 32) // 4) * 8 + (i // 32) * 2 + (i % 4) // 2))
    matrix("spr", lambda i, j: i == (j // 128) * 8 + ((j % 128) // 32) * 2 + (j % 4) // 2)

    arrive(in_k0)
    merge0("hk", k0, 3)
    make_ops(k0, ops0, 1.0, 14, 13)
    in_k1 = halo1("h1k", k1, 7)
    arrive(in_va[2:4])
    arrive(in_src[2:4])
    merge0("hv", s["va"], 3, range(3, 11))
    merge0("hs", s["src"], 2, range(3, 11))
    va, vb, vc, vd, ve, src, g0 = [s[name] for name in ("va", "vb", "vc", "vd", "ve", "src", "g0")]

    def force(x):
        g0[x] = RATE * va[x] + src[x]

    each(3, 11, 8, force)
    sweep(va, vb, g0, ops0, 4, 10, 6)
    arrive(in_va[:2] + in_va[4:])
    arrive(in_src[:2] + in_src[4:])
    merge0("hv", va, 3, (0, 1, 2, 11, 12, 13))
    merge0("hs", src, 2, (1, 2, 11, 12))
    for x in (1, 2, 11, 12):
        force(x)
    sweep(va, vb, g0, ops0, 1, 4, 3)
    sweep(va, vb, g0, ops0, 10, 13, 3)
    sweep(vb, vc, g0, ops0, 2, 12, 10)

    def down0(c):
        put0(c, res_at(vc, g0, ops0, 2 * c + 3) + res_at(vc, g0, ops0, 2 * c + 4))

    each(0, 4, 4, down0)
    tile = take0()
    f1 = s["f1"]
    for c in range(4):
        f1[7 + c, 0:8] = tile[8 * c : 8 * c + 8]
    in_f1 = halo1("h1f", f1, 6)

    arrive(in_k2a)
    in_k2b = window_y("k2b", x2k)
    arrive(in_ka)
    in_kb = ring_y("kb", s["kb"], s["ks"], slab(s["ka"]))

    arrive(in_k1)
    make_ops(k1, ops1, 0.25, 18, 17)
    arrive(in_k2b)
    window(x2k, k2)
    make_ops(k2, ops2, 0.0625, 14, 13)
    near = s["near"]
    for c in range(6):
        a, am, b, d, w = [ref[x, 4:12] for ref, x in zip((ops2[0], ops2[0], ops2[1], ops2[2], ops2[3]), (c + 4, c + 3, c + 4, c + 4, c + 4))]
        bm, dm = roll(b, 1, 0), roll(d, 1, 1)
        diag = (RATE + a + am) + (b + bm) + (d + dm)
        for number, value in enumerate((w * a, w * am, w * b, w * bm, w * d, w * dm, w, diag * (1.0 / RELAX))):
            near[c, number] = value
    arrive(in_f1)

    v1a, v1b = s["v1a"], s["v1b"]

    def start1(x):
        v1a[x] = ops1[3][x] * f1[x]

    each(1, 17, 16, start1)
    sweep(v1a, v1b, f1, ops1, 2, 16, 14)
    low = to_level2([res_at(v1b, f1, ops1, x) for x in range(3, 15)])
    f2l = s["f2l"]
    f2 = s["f2"]
    for c in range(6):
        f2l[c] = low[8 * c : 8 * c + 8]
    for c in range(2):
        x2f[6 + c, 2] = low[8 * c + 18 : 8 * c + 22]

    v2a, v2b = s["v2a"], s["v2b"]
    vl = [near[c, 6] * f2l[c] for c in range(6)]

    def step_near(v, c):
        o, u = [near[c, number] for number in range(6)], v[c]
        along_x = o[0] * v[c + 1] + o[1] * v[c - 1]
        along_y = o[2] * roll(u, -1, 0) + o[3] * roll(u, 1, 0)
        along_z = o[4] * roll(u, -1, 1) + o[5] * roll(u, 1, 1)
        return (along_x + along_y) + (along_z + (vl[c] - RELAX * u))

    ul = [None] + [vl[c] + step_near(vl, c) for c in range(1, 5)] + [None]
    base = to_level3(near[2, 7] * step_near(ul, 2) + near[3, 7] * step_near(ul, 3), 2)
    in_fa = ring_x("fa", s["fa"], s["ft"], base)
    in_f2a = window_x("f2a", x2f)

    arrive(in_kb)
    kap3 = [s["kb"][k].reshape(32, 128) for k in range(4)]
    kap4 = low_restrict(kap3, 1)
    kap5 = low_restrict(kap4, 2)
    kap6 = low_restrict(kap5, 4)[0]
    for level, kap, spread in ((3, kap3, 1), (4, kap4, 2), (5, kap5, 4)):
        made = low_couple(kap, spread, 1.0 / 4.0**level)
        for k in range(len(kap)):
            for number in range(8):
                s[f"low{level}"][k, number] = made[k][number]

    krow = dot01(pack_six(kap6), s["sel"][...])[0:1]
    q, p = iota((32, 128), 0), iota((32, 128), 1)
    kcol = jnp.sum(jnp.where(q == p, krow, 0.0), axis=1, keepdims=True)
    dy, dz, same_x = (q // 8 - p // 8 + 4) % 4, ((q % 8) // 2 - (p % 8) // 2 + 4) % 4, q % 2 == p % 2
    links = jnp.where(same_x & (dz == 0) & (dy % 2 == 1), 1.0, 0.0) + jnp.where(same_x & (dy == 0) & (dz % 2 == 1), 1.0, 0.0)
    links = links + jnp.where((dz == 0) & (dy == 0) & (q % 2 != p % 2), 2.0, 0.0)
    links = jnp.where(p < 32, links, 0.0)
    off = (0.5 / 4096.0) * links * (krow + kcol)
    diag = RATE + jnp.sum(off, axis=1, keepdims=True)
    m_ref = s["m6"]
    m_ref[...] = jnp.where(q == p, diag, jnp.where(p == q + 32, 1.0, -off))

    def eliminate(k, carry):
        m = m_ref[...]
        pivot_row = m_ref[pl.ds(k, 1), :]
        column = jnp.sum(jnp.where(p == k, m, 0.0), axis=1, keepdims=True)
        pivot = jnp.sum(jnp.where(iota((1, 128), 1) == k, pivot_row, 0.0), axis=1, keepdims=True)
        scaled = pivot_row / pivot
        m_ref[...] = jnp.where(q == k, scaled, m - column * scaled)
        return carry

    lax.fori_loop(0, 16, eliminate, 0)

    arrive(in_fa)
    in_fb = ring_y("fb", s["fb"], s["fs"], slab(s["fa"]))
    arrive(in_f2a)
    in_f2b = window_y("f2b", x2f)
    stay = pltpu.make_async_copy(vc.at[tile0], vd.at[tile0], s["load"].at[0])
    stay.start()
    edges0("hd", vc, 2)
    in_vd = halo0("hd", vc, vd, 2, 1)
    lax.fori_loop(16, 32, eliminate, 0)
    inverse = roll(m_ref[...], -32, 1)
    inverse = jnp.concatenate([jnp.where(p < 32, inverse, 0.0), jnp.zeros((96, 128), F32)], axis=0)
    inverse = dot01(inverse, s["spr"][...])
    hi = inverse.astype(BF16)
    rest = inverse - hi.astype(F32)
    mid = rest.astype(BF16)
    pieces = (hi, mid, (rest - mid.astype(F32)).astype(BF16))
    a, b, c = [jnp.dot(s["sel"][...], piece, preferred_element_type=F32) for piece in pieces]
    inverse = a + (b + c)
    hi = inverse.astype(BF16)
    s["inv"][0] = hi
    s["inv"][1] = (inverse - hi.astype(F32)).astype(BF16)

    drain()

    def low_ops(level, count):
        return [[s[f"low{level}"][k, number] for number in range(8)] for k in range(count)]

    arrive(in_fb)
    g3 = [s["fb"][k].reshape(32, 128) for k in range(4)]
    o3, o4, o5 = low_ops(3, 4), low_ops(4, 2), low_ops(5, 1)

    def down(g, o, spread):
        wg = [q[6] * f for q, f in zip(o, g)]
        v = low_sweep(wg, wg, o, spread)
        step = low_step(v, wg, o, spread)
        return v, wg, low_restrict([q[7] * d for q, d in zip(o, step)], spread)

    v3, wg3, g4 = down(g3, o3, 1)
    v4, wg4, g5 = down(g4, o4, 2)
    v5, wg5, g6 = down(g5, o5, 4)
    x6 = pack_six(g6[0])
    hi = x6.astype(BF16).astype(F32)
    both = jnp.concatenate([hi, x6 - hi], axis=0).astype(BF16)
    large = jnp.dot(both, s["inv"][0], preferred_element_type=F32)
    x6 = large[:8] + (large[8:] + jnp.dot(both, s["inv"][1], preferred_element_type=F32)[:8])
    x6 = jnp.concatenate([x6[:, 128 * k : 128 * k + 128] for k in range(4)], axis=0)

    def up(v, e, wg, o, spread):
        v = [u + e[k * len(e) // len(v)] for k, u in enumerate(v)]
        return low_sweep(low_sweep(v, wg, o, spread), wg, o, spread)

    v5 = up(v5, [x6], wg5, o5, 4)
    v4 = up(v4, v5, wg4, o4, 2)
    v3 = up(v3, v4, wg3, o3, 1)

    e3, e2, e1 = s["e3"], s["e2"], s["e1"]
    turn = lax.rem(2 * N - 2 * me_y + 3, 2 * N)
    for k in range(4):
        e3[k] = pltpu.roll(v3[k], turn, 0)[0:8]
    picks = []
    lane8 = iota((8, 128), 1)
    for d in range(-2, 3):
        x = lax.rem(me_x + (d + N), N)
        picks.append(jnp.where(lane8 % 4 == x // 4, e3[lax.rem(x, 4)], 0.0))
    spread3 = dot01(jnp.concatenate(picks, axis=0), s["p32"][...])
    for c in range(5):
        e2[c + 1, pl.ds(0, 8, stride=2), :] = spread3[8 * c : 8 * c + 8]
        e2[c + 1, pl.ds(1, 8, stride=2), :] = spread3[8 * c : 8 * c + 8]

    arrive(in_f2b)
    window(x2f, f2)
    for x in range(1, 13):
        v2a[x] = ops2[3][x] * f2[x]
    sweep(v2a, v2b, f2, ops2, 2, 12, 10)
    for x in range(2, 12):
        v2b[x] = v2b[x] + e2[x // 2]
    sweep(v2b, v2a, f2, ops2, 3, 11, 8)
    sweep(v2a, v2b, f2, ops2, 4, 10, 6)

    spread2 = dot01(jnp.concatenate([v2b[x] for x in range(4, 10)], axis=0), s["p21"][...])
    for c in range(6):
        e1[c, pl.ds(0, 16, stride=2), :] = spread2[16 * c : 16 * c + 16]
        e1[c, pl.ds(1, 16, stride=2), :] = spread2[16 * c : 16 * c + 16]
    for x in range(4, 14):
        c = (x + 5) // 2 - 4
        v1b[x] = v1b[x] + jnp.concatenate([e1[c, 12:28], e1[c, 4:12]], axis=0)
    sweep(v1b, v1a, f1, ops1, 5, 13, 8)
    sweep(v1a, v1b, f1, ops1, 6, 12, 6)

    e0 = s["e0"]
    for c in range(6):
        e0[c, pl.ds(0, 24, stride=2), :] = v1b[6 + c]
        e0[c, pl.ds(1, 24, stride=2), :] = v1b[6 + c]
    row8 = iota((8, 128), 0)
    parts = []
    for c in range(6):
        parts += [e0[c, 0:16], jnp.where(row8 < 4, e0[c, 16:24], e0[c, 40:48])]
    spread1 = dot01(jnp.concatenate(parts, axis=0), s["p10"][...])
    stay.wait()
    arrive(in_vd)
    merge0("hd", vd, 2)
    for x in range(1, 13):
        c = (x + 11) // 2 - 6
        ve[x] = vd[x] + spread1[24 * c : 24 * c + 24]
    sweep(ve, vb, g0, ops0, 2, 12, 10)

    def last(x):
        v = vb[x + 3] + ops0[3][x + 3] * res_at(vb, g0, ops0, x + 3)
        out[x] = v[0:16]

    each(0, 8, 8, last)
    drain()


def scratch_list():
    def vmem(*shape, kind=F32):
        return pltpu.VMEM(shape, kind)

    made = [("mat", vmem(8, 16, 256, kind=jnp.int32))]
    for name in ("k0", "va", "vb", "vc", "vd", "ve", "src", "g0", "cx0", "cy0", "cz0", "w0"):
        made.append((name, vmem(14, 24, 256)))
    for name in ("k1", "f1", "v1a", "v1b", "cx1", "cy1", "cz1", "w1"):
        made.append((name, vmem(18, 24, 128)))
    for name in ("k2", "f2", "v2a", "v2b", "cx2", "cy2", "cz2", "w2"):
        made.append((name, vmem(14, 16, 128)))
    for name in ("x2k", "x2f"):
        made.append((name, vmem(14, 5, 4, 128)))
    for name in ("hk", "hv", "hs", "hd"):
        made.append((name + "_e", vmem(8, 8, 256)))
        made.append((name + "_b", vmem(14, 8, 256)))
    made.append(("f2l", vmem(6, 8, 128)))
    made.append(("near", vmem(6, 8, 8, 128)))
    for name in ("ka", "fa"):
        made.append((name, vmem(N, 2, 128)))
    for name in ("kb", "fb"):
        made.append((name, vmem(4, N, 2, 128)))
    for name in ("kt", "ft"):
        made.append((name, vmem(2, 128)))
    for name in ("ks", "fs"):
        made.append((name, vmem(4, 2, 128)))
    made.append(("t0", vmem(4, 2, 16, 128)))
    made.append(("t1", vmem(6, 24, 128)))
    made.append(("t2", vmem(1, 8, 128)))
    made.append(("e3", vmem(4, 8, 128)))
    made.append(("e2", vmem(7, 16, 128)))
    made.append(("e1", vmem(6, 32, 128)))
    made.append(("e0", vmem(6, 48, 128)))
    made.append(("low3", vmem(4, 8, 32, 128)))
    made.append(("low4", vmem(2, 8, 32, 128)))
    made.append(("low5", vmem(1, 8, 32, 128)))
    made.append(("m6", vmem(32, 128)))
    made.append(("inv", vmem(2, 128, 512, kind=BF16)))
    for name, shape in (("r01", (256, 128)), ("r12", (128, 128)), ("r23", (128, 128)), ("p32", (128, 128)), ("p21", (128, 128)), ("p10", (128, 256)), ("sel", (128, 128)), ("spr", (128, 512))):
        made.append((name, vmem(*shape, kind=BF16)))
    made.append(("load", pltpu.SemaphoreType.DMA((3,))))
    groups = {"hk": 8, "hv": 8, "hs": 8, "hd": 8, "h1k": 14, "h1f": 14, "ka": 15, "kb": 15, "fa": 15, "fb": 15, "k2a": 6, "f2a": 6, "k2b": 4, "f2b": 4}
    for name, count in groups.items():
        made.append((name + "_s", pltpu.SemaphoreType.DMA((count,))))
        made.append((name + "_r", pltpu.SemaphoreType.DMA((count,))))
    return made


SCRATCH = scratch_list()


def shards(concentration, source, material):
    return pl.pallas_call(
        kernel,
        out_shape=jax.ShapeDtypeStruct(concentration.shape, F32),
        in_specs=[pl.BlockSpec(memory_space=pltpu.HBM)] * 3,
        out_specs=pl.BlockSpec(memory_space=pltpu.VMEM),
        scratch_shapes=[shape for _, shape in SCRATCH],
        compiler_params=pltpu.CompilerParams(collective_id=0, has_side_effects=True, vmem_limit_bytes=56360960),
        cost_estimate=pl.CostEstimate(flops=20_000_000, bytes_accessed=1_000_000, transcendentals=0),
        name="vcycle",
    )(concentration, source, material)


def solution(mesh):
    placed = P("tx", "ty", None)
    return jax.shard_map(shards, mesh=mesh, in_specs=(placed,) * 3, out_specs=placed, check_vma=False)
```
